32 devices in a mesh: depth: 4 (over y, core), lat: 8 (over z, x).
Axes of the slice: x: 2, y: 2, z: 4, core: 2. Of those that a mesh axis runs over, the one named last changes fastest.
Arguments:
- potential: float32 [2, 4, 2, 1024, 2048], P(None, 'depth', None, 'lat'), may hold values from -3 to 3, as said below
- incident: float32 [2, 2, 1024, 1024], P(None, None, 'lat'), may hold values from -6 to 6
- measured: float32 [2, 1024, 1024], P(None, 'lat'), may hold values from 0 to 3
- offsets: int32 [2, 2], replicated, may hold values from 0 to 1024, as said below
- kernel: bfloat16 [2, 9], replicated, may hold values from -1 to 1
Outputs:
- potential_grad: float32 [2, 4, 2, 1024, 2048], P(None, 'depth', None, 'lat')
The draws below stay inside these ranges and needn't reach their ends.
Inputs may be any that keep to these rules, and one draw needn't show every extreme that they name: Row offsets are multiples of 128 from 0 to 1024; column offsets run from 0 to 1024. `potential`: part 0 (phase) lies in -3 to 3; part 1 (absorption) lies in 0.004 to 0.05.
All inputs are finite; a program needn't handle non-finite values.
Results may differ from the reference program's by a relative error of at most 0.038.
Values may be sent and summed in bfloat16 or wider, within the bound.
A program may use at most 64 MiB of HBM per device.

```python
import jax
import jax.numpy as jnp
from jax import lax

WIN = 1024
HALF = 4
PROBES = 2
COL_SCAN = 1024
BAND = 128
SLICES = 4
OBJ_COLS = 2048


def draw_potential(key, part):
    phase_key, absorb_key = jax.random.split(key)
    shape_tail = (SLICES, 2, WIN, OBJ_COLS)
    phase_part = jax.random.uniform(phase_key, shape_tail, jnp.float32, -2.9, 2.9)
    exponent = jax.random.uniform(absorb_key, shape_tail, jnp.float32, -5.29, -3.0)
    absorb = jnp.exp(exponent)
    return jnp.stack([phase_part, absorb]).astype(jnp.float32)


def draw_kernel(key, part):
    angle_key, side_key = jax.random.split(jax.random.fold_in(key, 17))
    theta = jax.random.uniform(angle_key, (), jnp.float32, -3.14159, 3.14159)
    side_angles = jax.random.uniform(side_key, (2 * HALF + 1,), jnp.float32, -3.14159, 3.14159)
    side_size = (0.32 / HALF) ** 0.5
    side_taps = side_size * jnp.stack([jnp.cos(side_angles), jnp.sin(side_angles)])
    centre_mask = (jnp.arange(2 * HALF + 1) == HALF)[None, :]
    centre_vals = 0.6 * jnp.stack([jnp.cos(theta), jnp.sin(theta)])[:, None]
    taps = jnp.where(centre_mask, centre_vals, side_taps)
    return taps.astype(jnp.bfloat16)


def draw_offsets(key, part):
    row_key, col_key, pick_key, inner_key, near_key = jax.random.split(key, 5)
    band_count = WIN // BAND
    probe_ids = jnp.arange(PROBES, dtype=jnp.int32)
    row_bands = jax.random.randint(row_key, (PROBES,), 0, band_count + 1)
    col_start = jax.random.randint(col_key, (PROBES,), 0, COL_SCAN + 1)
    chosen = jax.random.randint(pick_key, (), 0, PROBES)
    partner = (chosen + 1) % PROBES
    if WIN >= COL_SCAN:
        row_bands = jnp.where(probe_ids == chosen, band_count, row_bands)
    else:
        col_start = jnp.where(probe_ids == chosen, COL_SCAN, col_start)
    inner_band = jax.random.randint(inner_key, (), 1, band_count)
    row_bands = jnp.where(probe_ids == partner, inner_band, row_bands)
    chosen_col = jnp.sum(jnp.where(probe_ids == chosen, col_start, 0))
    nearby = jax.random.randint(near_key, (), -(WIN // 2), WIN // 2 + 1)
    partner_col = jnp.clip(chosen_col + nearby, 0, COL_SCAN)
    col_start = jnp.where(probe_ids == partner, partner_col, col_start)
    return jnp.stack([row_bands * BAND, col_start], axis=1).astype(jnp.int32)


def block_levels(own_key, dims, pieces, low, high):
    loudness = 1.0
    for axis_at, blocks in pieces:
        draws = jax.random.uniform(jax.random.fold_in(jax.random.fold_in(own_key, 6), axis_at), (blocks,), jnp.float32, low / len(pieces), high / len(pieces))
        loudness = loudness * jnp.repeat(jnp.exp(draws), dims[axis_at] // blocks).reshape((-1,) + (1,) * (len(dims) - 1 - axis_at))
    return loudness


def centred(key, shape, width, limit, pieces=(), held_as=jnp.bfloat16):
    array = width * jax.random.normal(key, shape, jnp.float32)
    if pieces:
        array = array * block_levels(key, shape, pieces, -0.22, 0.18)
    return jnp.clip(array, -limit, limit).astype(held_as)


def setup_inputs(seed: int = 0) -> dict:
    arg_keys = jax.random.split(jax.random.key(seed), 6)
    return {
        "potential": draw_potential(jax.random.fold_in(arg_keys[5], 71), 0),
        "incident": centred(arg_keys[1], (2, PROBES, WIN, WIN), 1.0, 6.0, ((2, 8),), jnp.float32),
        "measured": jnp.clip(3.0 * jax.random.uniform(arg_keys[2], (PROBES, WIN, WIN), jnp.float32) ** block_levels(arg_keys[2], (PROBES, WIN, WIN), ((1, 8),), -0.2, 0.2), 0.0, 3.0),
        "offsets": draw_offsets(jax.random.fold_in(arg_keys[5], 71), 0),
        "kernel": draw_kernel(jax.random.fold_in(arg_keys[5], 71), 0),
    }


def rounded(field_in):
    return lax.optimization_barrier(field_in.astype(jnp.bfloat16)).astype(jnp.float32)


def complex_conv(field_in, taps_re, taps_im, axis_dim):
    half_width = (taps_re.shape[0] - 1) // 2
    length = field_in.shape[axis_dim]
    widths = [(0, 0), (0, 0), (0, 0)]
    widths[axis_dim] = (half_width, half_width)
    padded = jnp.pad(field_in, widths)
    out_re = jnp.zeros(field_in.shape[1:], jnp.float32)
    out_im = jnp.zeros(field_in.shape[1:], jnp.float32)
    for tap_index in range(2 * half_width + 1):
        shifted = lax.slice_in_dim(padded, tap_index, tap_index + length, axis=axis_dim)
        out_re = out_re + taps_re[tap_index] * shifted[0] - taps_im[tap_index] * shifted[1]
        out_im = out_im + taps_re[tap_index] * shifted[1] + taps_im[tap_index] * shifted[0]
    return jnp.stack([out_re, out_im])


def rotate_rows(field_in, shift_rows, axis_dim):
    doubled = jnp.concatenate([field_in, field_in], axis=axis_dim)
    return lax.dynamic_slice_in_dim(doubled, shift_rows, field_in.shape[axis_dim], axis_dim)


def reference(potential, incident, measured, offsets, kernel):
    taps_re = kernel[0].astype(jnp.float32)
    taps_im = kernel[1].astype(jnp.float32)
    back_re = taps_re[::-1]
    back_im = -taps_im[::-1]
    layered = potential.reshape(2, SLICES, 2 * WIN, OBJ_COLS)
    gradient = jnp.zeros_like(layered)
    for probe_index in range(PROBES):
        row_start = offsets[probe_index, 0].astype(jnp.int32)
        col_start = offsets[probe_index, 1].astype(jnp.int32)
        zero_index = jnp.zeros((), jnp.int32)
        view = lax.dynamic_slice(layered, (zero_index, zero_index, row_start, col_start), (2, SLICES, WIN, WIN))
        damping = jnp.exp(-view[1])
        transmit = jnp.stack([damping * jnp.cos(view[0]), damping * jnp.sin(view[0])])
        shift_rows = (row_start % WIN).astype(jnp.int32)
        wave_now = rounded(rotate_rows(incident[:, probe_index], shift_rows, 1))
        entries = []
        for slice_index in range(SLICES):
            entries.append(wave_now)
            factor = transmit[:, slice_index]
            product = rounded(jnp.stack([factor[0] * wave_now[0] - factor[1] * wave_now[1],
                                         factor[0] * wave_now[1] + factor[1] * wave_now[0]]))
            spread = rounded(complex_conv(product, taps_re, taps_im, 1))
            wave_now = rounded(complex_conv(spread, taps_re, taps_im, 2))
        target = rotate_rows(measured[probe_index], shift_rows, 0)
        residual = wave_now[0] * wave_now[0] + wave_now[1] * wave_now[1] - target
        adjoint = rounded(2.0 * residual[None] * wave_now)
        for slice_index in reversed(range(SLICES)):
            spread = rounded(complex_conv(adjoint, back_re, back_im, 2))
            local_grad = rounded(complex_conv(spread, back_re, back_im, 1))
            factor = transmit[:, slice_index]
            entry_wave = entries[slice_index]
            cross_re = entry_wave[0] * local_grad[0] + entry_wave[1] * local_grad[1]
            cross_im = entry_wave[0] * local_grad[1] - entry_wave[1] * local_grad[0]
            turned_re = factor[0] * cross_re + factor[1] * cross_im
            turned_im = factor[0] * cross_im - factor[1] * cross_re
            corner = (zero_index, zero_index + slice_index, row_start, col_start)
            current = lax.dynamic_slice(gradient, corner, (2, 1, WIN, WIN))
            addition = jnp.stack([turned_im, -turned_re])[:, None]
            gradient = lax.dynamic_update_slice(gradient, current + addition, corner)
            adjoint = rounded(jnp.stack([factor[0] * local_grad[0] + factor[1] * local_grad[1],
                                         factor[0] * local_grad[1] - factor[1] * local_grad[0]]))
    return gradient.reshape(2, SLICES, 2, WIN, OBJ_COLS)
```

```python
import functools

import jax
import jax.numpy as jnp
from jax import lax
from jax.experimental import pallas as pl
from jax.experimental.pallas import tpu as pltpu
from jax.sharding import PartitionSpec as P


def with_halo(cells, sides, width):
    for axis, dim in sides:
        count = lax.axis_size(axis)
        head = lax.slice_in_dim(cells, 0, width, axis=dim)
        tail = lax.slice_in_dim(cells, cells.shape[dim] - width, cells.shape[dim], axis=dim)
        cells = jnp.concatenate(
            [
                lax.ppermute(tail, axis, [(i, (i + 1) % count) for i in range(count)]),
                cells,
                lax.ppermute(head, axis, [((i + 1) % count, i) for i in range(count)]),
            ],
            axis=dim,
        )
    return cells


def from_behind(array, axis, by):
    count = lax.axis_size(axis)
    pairs = [(i, i + by) for i in range(count) if 0 <= i + by < count]
    return lax.ppermute(array, axis, pairs)


def rounded(field_in):
    return lax.optimization_barrier(field_in.astype(jnp.bfloat16)).astype(jnp.float32)


def band_matrix(taps_re, taps_im, row_count, col_count, half_width, transposed):
    row_index = lax.broadcasted_iota(jnp.int32, (row_count, col_count), 0)
    col_index = lax.broadcasted_iota(jnp.int32, (row_count, col_count), 1)
    offset = row_index - col_index if transposed else col_index - row_index
    chooser = (offset[:, :, None] == jnp.arange(2 * half_width + 1, dtype=jnp.int32)).astype(
        jnp.float32
    )
    real_part = jnp.sum(chooser * taps_re, axis=2).astype(jnp.bfloat16)
    imag_part = jnp.sum(chooser * taps_im, axis=2).astype(jnp.bfloat16)
    return (real_part, imag_part)


def along_rows(field_in, real_mat, imag_mat):
    direct = jnp.einsum("rq,xpqc->xprc", real_mat, field_in, preferred_element_type=jnp.float32)
    crossed = jnp.einsum("rq,xpqc->xprc", imag_mat, field_in, preferred_element_type=jnp.float32)
    return jnp.stack([direct[0] - crossed[1], crossed[0] + direct[1]])


def along_cols(field_in, real_slab, imag_slab, half_width):
    columns = field_in.shape[-1]
    blocks = columns // 128
    padded = jnp.pad(field_in, ((0, 0), (0, 0), (0, 0), (half_width, 128 - half_width)))
    main_part = padded[..., :columns].reshape(field_in.shape[:-1] + (blocks, 128))
    extra_part = padded[..., 128 : columns + 128].reshape(field_in.shape[:-1] + (blocks, 128))[
        ..., : 2 * half_width
    ]
    slab_rows = jnp.concatenate([main_part, extra_part], axis=-1)
    direct = jnp.einsum("xprbq,qo->xprbo", slab_rows, real_slab, preferred_element_type=jnp.float32)
    crossed = jnp.einsum(
        "xprbq,qo->xprbo", slab_rows, imag_slab, preferred_element_type=jnp.float32
    )
    joined = jnp.stack([direct[0] - crossed[1], crossed[0] + direct[1]])
    return joined.reshape(field_in.shape)


def local(potential, incident, measured, offsets, kernel):
    lat_count = lax.axis_size("lat")
    depth_count = lax.axis_size("depth")
    lat_index = lax.axis_index("lat")
    depth_index = lax.axis_index("depth")
    band_rows = potential.shape[3]
    window = incident.shape[3]
    probe_count = incident.shape[1]
    half_width = (kernel.shape[1] - 1) // 2
    taps_re = kernel[0].astype(jnp.float32)
    taps_im = kernel[1].astype(jnp.float32)
    back_re = taps_re[::-1]
    back_im = -taps_im[::-1]
    row_pixel = offsets[:, 0]
    col_pixel = offsets[:, 1]
    first_band = row_pixel // band_rows
    place_band = (lat_index - first_band) % lat_count
    layer_pot = potential[:, 0]
    reach_steps = 2
    margin = reach_steps * half_width
    full_rows = band_rows + 2 * margin
    most_out = full_rows - 2 * half_width
    row_forward = band_matrix(taps_re, taps_im, most_out, full_rows, half_width, False)
    row_adjoint = band_matrix(back_re, back_im, most_out, full_rows, half_width, False)
    column_forward = band_matrix(taps_re, taps_im, 128 + 2 * half_width, 128, half_width, True)
    column_adjoint = band_matrix(back_re, back_im, 128 + 2 * half_width, 128, half_width, True)
    local_rows = jnp.arange(full_rows, dtype=jnp.int32) - margin
    window_row = place_band[:, None] * band_rows + local_rows[None, :]
    valid_rows = (window_row >= 0) & (window_row < window)
    keep_mask = valid_rows[None, :, :, None]
    padded_pot = with_halo(layer_pot, (("lat", 2),), margin)
    local_rows = jnp.arange(band_rows + 2 * margin, dtype=jnp.int32) - margin
    side_rows = (local_rows >= band_rows).astype(jnp.int32) - (local_rows < 0).astype(jnp.int32)
    halves = jnp.clip(
        (first_band[:, None] + place_band[:, None] + side_rows[None, :]) // lat_count, 0, 1
    )

    def cut_window(col_start):
        return lax.dynamic_slice_in_dim(padded_pot, col_start, window, 3)

    windows = jax.vmap(cut_window)(col_pixel)
    chosen = jnp.where((halves == 0)[:, None, :, None], windows[:, :, 0], windows[:, :, 1])
    damping = jnp.exp(-chosen[:, 1])
    phase_part = chosen[:, 0]
    transmit = jnp.stack([damping * jnp.cos(phase_part), damping * jnp.sin(phase_part)])

    def forward_segment(wave_ext, extent):
        low_row = margin - extent
        rows_in = band_rows + 2 * extent
        rows_out = rows_in - 2 * half_width
        factor = transmit[:, :, low_row : low_row + rows_in]
        inside = keep_mask[:, :, low_row : low_row + rows_in]
        values = wave_ext.astype(jnp.float32)
        product = jnp.stack(
            [
                factor[0] * values[0] - factor[1] * values[1],
                factor[0] * values[1] + factor[1] * values[0],
            ]
        )
        product = jnp.where(inside, product, 0.0).astype(jnp.bfloat16)
        spread = along_rows(
            product, row_forward[0][:rows_out, :rows_in], row_forward[1][:rows_out, :rows_in]
        ).astype(jnp.bfloat16)
        return along_cols(spread, column_forward[0], column_forward[1], half_width).astype(
            jnp.bfloat16
        )

    def backward_segment(adjoint, extent, entry):
        low_row = margin - extent
        rows_in = band_rows + 2 * extent
        rows_out = rows_in - 2 * half_width
        inside = keep_mask[:, :, low_row : low_row + rows_in]
        masked = jnp.where(inside, adjoint, jnp.zeros_like(adjoint))
        spread = along_cols(masked, column_adjoint[0], column_adjoint[1], half_width).astype(
            jnp.bfloat16
        )
        local_grad = rounded(
            along_rows(
                spread, row_adjoint[0][:rows_out, :rows_in], row_adjoint[1][:rows_out, :rows_in]
            )
        )
        factor = transmit[:, :, low_row + half_width : low_row + half_width + rows_out]
        earlier = jnp.stack(
            [
                factor[0] * local_grad[0] + factor[1] * local_grad[1],
                factor[0] * local_grad[1] - factor[1] * local_grad[0],
            ]
        ).astype(jnp.bfloat16)
        centre = extent - half_width
        own_rows = local_grad[:, :, centre : centre + band_rows]
        own_factor = factor[:, :, centre : centre + band_rows]
        entry_wave = entry.astype(jnp.float32)
        cross_re = entry_wave[0] * own_rows[0] + entry_wave[1] * own_rows[1]
        cross_im = entry_wave[0] * own_rows[1] - entry_wave[1] * own_rows[0]
        turned_re = own_factor[0] * cross_re + own_factor[1] * cross_im
        turned_im = own_factor[0] * cross_im - own_factor[1] * cross_re
        return (earlier, jnp.stack([turned_im, -turned_re]))

    start_wave = incident.astype(jnp.bfloat16)
    zeros_wave = jnp.zeros_like(start_wave)
    blocks = depth_count // reach_steps

    def forward_block(block_index, carry):
        moving, stored, leaving = carry
        entering = jnp.where(depth_index == 0, start_wave, moving)
        wave_ext = with_halo(entering, (("lat", 2),), margin)
        for sub_step in range(reach_steps):
            extent = margin - sub_step * half_width
            result = forward_segment(wave_ext, extent)
            active = depth_index == block_index * reach_steps + sub_step
            stored = jnp.where(active, wave_ext[:, :, extent : extent + band_rows], stored)
            if sub_step == reach_steps - 1:
                leaving = jnp.where(active, result, leaving)
            wave_ext = from_behind(result, "depth", 1)
        return (wave_ext, stored, leaving)

    moving, stored, leaving = lax.fori_loop(
        0, blocks, forward_block, (zeros_wave, zeros_wave, zeros_wave)
    )
    exit_vals = leaving.astype(jnp.float32)
    residual = exit_vals[0] * exit_vals[0] + exit_vals[1] * exit_vals[1] - measured
    seed_wave = (2.0 * residual[None] * exit_vals).astype(jnp.bfloat16)
    zeros_term = jnp.zeros(start_wave.shape, jnp.float32)

    def backward_block(block_index, carry):
        moving_back, collected = carry
        entering = jnp.where(depth_index == depth_count - 1, seed_wave, moving_back)
        adjoint = with_halo(entering, (("lat", 2),), margin)
        for sub_step in range(reach_steps):
            extent = margin - sub_step * half_width
            earlier, grad_term = backward_segment(adjoint, extent, stored)
            active = depth_index == depth_count - 1 - (block_index * reach_steps + sub_step)
            collected = jnp.where(active, grad_term, collected)
            adjoint = from_behind(earlier, "depth", -1)
        return (adjoint, collected)

    moving_back, gathered = lax.fori_loop(0, blocks, backward_block, (zeros_wave, zeros_term))
    own_half = (first_band + place_band) // lat_count
    gradient = jnp.zeros_like(layer_pot)

    def accumulate(probe_index, running):
        portion = lax.dynamic_index_in_dim(gathered, probe_index, 1, keepdims=False)
        zero_index = jnp.zeros((), jnp.int32)
        corner = (zero_index, own_half[probe_index], zero_index, col_pixel[probe_index])
        current = lax.dynamic_slice(running, corner, (2, 1, band_rows, window))
        return lax.dynamic_update_slice(running, current + portion[:, None], corner)

    gradient = lax.fori_loop(0, probe_count, accumulate, gradient)
    return gradient[:, None]


ROW_BLOCK = 32


def fits(mesh, potential_shape, incident_shape, kernel_shape):
    depth_count, lat_count = mesh.shape["depth"], mesh.shape["lat"]
    slices, window, columns = potential_shape[1], incident_shape[3], potential_shape[4]
    half_width = (kernel_shape[1] - 1) // 2
    if incident_shape[1] != 2 or depth_count != 4 or slices != 4:
        return False
    half_band = potential_shape[3] // lat_count // 2
    reach = 2 * slices * half_width
    return (
        half_width <= 8
        and reach <= half_band
        and reach % 16 == 0
        and half_band % ROW_BLOCK == 0
        and (half_band + 2 * reach) % 128 == 0
        and window % 128 == 0
        and columns == 2 * window
    )


def transmission_kernel(scalars, pot_ref, out_ref):
    col = scalars[2 + pl.program_id(0)]
    columns, window = pot_ref.shape[3], out_ref.shape[3]
    shift = lax.rem(columns - col, columns)
    phase = pltpu.roll(pot_ref[0, 0], shift, 1)[:, :window]
    absorb = pltpu.roll(pot_ref[1, 0], shift, 1)[:, :window]
    damping = jnp.exp(-absorb)
    out_ref[0, 0] = (damping * jnp.cos(phase)).astype(out_ref.dtype)
    out_ref[0, 1] = (damping * jnp.sin(phase)).astype(out_ref.dtype)


def transmissions(scalars, layer_pot, window):
    band_rows, columns = layer_pot.shape[2:]
    return pl.pallas_call(
        transmission_kernel,
        out_shape=jax.ShapeDtypeStruct((2, 2, band_rows, window), jnp.bfloat16),
        grid_spec=pltpu.PrefetchScalarGridSpec(
            num_scalar_prefetch=1,
            grid=(2, band_rows // ROW_BLOCK),
            in_specs=[
                pl.BlockSpec((2, 1, ROW_BLOCK, columns), lambda q, r, sc: (0, sc[q], r, 0))
            ],
            out_specs=pl.BlockSpec((1, 2, ROW_BLOCK, window), lambda q, r, sc: (q, 0, r, 0)),
        ),
    )(scalars, layer_pot)


def band(taps, rows, cols, start, half_width):
    offset = (
        lax.broadcasted_iota(jnp.int32, (rows, cols), 0)
        - lax.broadcasted_iota(jnp.int32, (rows, cols), 1)
        - start
        + half_width
    )
    total = jnp.zeros((rows, cols), jnp.float32)
    for tap_index, tap in enumerate(taps):
        total = jnp.where(offset == tap_index, tap, total)
    return total


def main_kernel(sc, taps_ref, keep, recv, wave_ref, meas_ref, out_ref, waves, row_mat, col_mat):
    rows, window = meas_ref.shape
    slices = waves.shape[0]
    tap_count = taps_ref.shape[1]
    half_width = (tap_count - 1) // 2
    reach = 2 * slices * half_width
    base, half, probe = sc[0], sc[1], sc[2]
    blocks = window // 128
    re = [taps_ref[0, i] for i in range(tap_count)]
    im = [taps_ref[1, i] for i in range(tap_count)]
    ways = ((re, im), (re[::-1], [-tap for tap in im[::-1]]))
    for way, (tap_re, tap_im) in enumerate(ways):
        real = band(tap_re[::-1], rows, rows, 0, half_width)
        imag = band(tap_im[::-1], rows, rows, 0, half_width)
        row_mat[way, :rows, :rows] = real.astype(jnp.bfloat16)
        row_mat[way, :rows, rows:] = (-imag).astype(jnp.bfloat16)
        row_mat[way, rows:, :rows] = imag.astype(jnp.bfloat16)
        row_mat[way, rows:, rows:] = real.astype(jnp.bfloat16)
        real = band(tap_re, 384, 128, 128, half_width)
        imag = band(tap_im, 384, 128, 128, half_width)
        col_mat[way, :384, :128] = real.astype(jnp.bfloat16)
        col_mat[way, :384, 128:] = imag.astype(jnp.bfloat16)
        col_mat[way, 384:, :128] = (-imag).astype(jnp.bfloat16)
        col_mat[way, 384:, 128:] = real.astype(jnp.bfloat16)

    def rows_conv(field, way):
        return jnp.dot(row_mat[way], field, preferred_element_type=jnp.float32).astype(
            jnp.bfloat16
        )

    def cols_conv(field, way):
        edge = jnp.zeros((rows, 128), jnp.bfloat16)
        padded = [
            jnp.concatenate([edge, field[k * rows : (k + 1) * rows], edge], axis=1)
            for k in range(2)
        ]
        slabs = jnp.concatenate(
            [
                jnp.concatenate([part[:, 128 * b : 128 * b + 384] for part in padded], axis=1)
                for b in range(blocks)
            ],
            axis=0,
        )
        out = jnp.dot(slabs, col_mat[way], preferred_element_type=jnp.float32)
        out = out.astype(jnp.bfloat16)
        return [
            jnp.concatenate(
                [out[b * rows : (b + 1) * rows, 128 * k : 128 * k + 128] for b in range(blocks)],
                axis=1,
            )
            for k in range(2)
        ]

    def factor(s):
        core, side = lax.rem(s + half, 2), lax.rem(s // 2 + probe, 2)
        return [
            jnp.where(core == 0, keep[side, k], recv[side, k]).astype(jnp.float32)
            for k in range(2)
        ]

    wave = [wave_ref[0], wave_ref[1]]
    for s in range(slices):
        waves[s, 0], waves[s, 1] = wave
        t_re, t_im = factor(s)
        w_re, w_im = [part.astype(jnp.float32) for part in wave]
        product = jnp.concatenate([t_re * w_re - t_im * w_im, t_re * w_im + t_im * w_re], axis=0)
        wave = cols_conv(rows_conv(product.astype(jnp.bfloat16), 0), 0)

    w_re, w_im = [part.astype(jnp.float32) for part in wave]
    window_row = base + lax.broadcasted_iota(jnp.int32, (rows, window), 0)
    inside = (window_row >= 0) & (window_row < window)
    residual = 2.0 * (w_re * w_re + w_im * w_im - meas_ref[...])
    residual = jnp.where(inside, residual, 0.0)
    adjoint = [(residual * w_re).astype(jnp.bfloat16), (residual * w_im).astype(jnp.bfloat16)]
    for s in reversed(range(slices)):
        spread = cols_conv(jnp.concatenate(adjoint, axis=0), 1)
        grad = rows_conv(jnp.concatenate(spread, axis=0), 1).astype(jnp.float32)
        g_re, g_im = grad[:rows], grad[rows:]
        t_re, t_im = factor(s)
        back_re = t_re * g_re + t_im * g_im
        back_im = t_re * g_im - t_im * g_re
        own = slice(reach, rows - reach)
        e_re = waves[s, 0, own].astype(jnp.float32)
        e_im = waves[s, 1, own].astype(jnp.float32)
        core, side = lax.rem(s + half, 2), lax.rem(s // 2 + probe, 2)
        out_ref[core, side, 0] = (e_re * back_im[own] - e_im * back_re[own]).astype(jnp.bfloat16)
        out_ref[core, side, 1] = (-e_re * back_re[own] - e_im * back_im[own]).astype(jnp.bfloat16)
        adjoint = [back_re.astype(jnp.bfloat16), back_im.astype(jnp.bfloat16)]


def section_terms(scalars, taps, keep, recv, wave, meas, half_band):
    slices, rows, window = 4, meas.shape[0], meas.shape[1]
    smem = pl.BlockSpec(memory_space=pltpu.SMEM)
    vmem = pl.BlockSpec(memory_space=pltpu.VMEM)
    return pl.pallas_call(
        main_kernel,
        out_shape=jax.ShapeDtypeStruct((2, 2, 2, half_band, window), jnp.bfloat16),
        in_specs=[smem, smem, vmem, vmem, vmem, vmem],
        out_specs=vmem,
        scratch_shapes=[
            pltpu.VMEM((slices, 2, rows, window), jnp.bfloat16),
            pltpu.VMEM((2, 2 * rows, 2 * rows), jnp.bfloat16),
            pltpu.VMEM((2, 768, 256), jnp.bfloat16),
        ],
        compiler_params=pltpu.CompilerParams(vmem_limit_bytes=48 * 1024 * 1024),
    )(scalars, taps, keep, recv, wave, meas)


def place_kernel(scalars, own_ref, other_ref, out_ref):
    columns, window = out_ref.shape[3], own_ref.shape[3]
    for part in range(2):
        totals = [None, None]
        for q, ref in enumerate((own_ref, other_ref)):
            values = ref[0, part].astype(jnp.float32)
            wide = jnp.concatenate([values, jnp.zeros_like(values)], axis=1)
            wide = pltpu.roll(wide, scalars[2 + q], 1)
            for layer in range(2):
                term = jnp.where(scalars[q] == layer, wide, 0.0)
                totals[layer] = term if q == 0 else totals[layer] + term
        for layer in range(2):
            out_ref[part, layer] = totals[layer]


def placed(scalars, own, other, columns):
    half_band, window = own.shape[2:]
    per_half = half_band // ROW_BLOCK

    def pick(r, sc):
        return (lax.rem(r // per_half + sc[4], 2), 0, lax.rem(r, per_half), 0)

    spec = pl.BlockSpec((1, 2, ROW_BLOCK, window), pick)
    return pl.pallas_call(
        place_kernel,
        out_shape=jax.ShapeDtypeStruct((2, 2, 2 * half_band, columns), jnp.float32),
        grid_spec=pltpu.PrefetchScalarGridSpec(
            num_scalar_prefetch=1,
            grid=(2 * per_half,),
            in_specs=[spec, spec],
            out_specs=pl.BlockSpec((2, 2, ROW_BLOCK, columns), lambda r, sc: (0, 0, r, 0)),
        ),
    )(scalars, own, other)


def local_fast(potential, incident, measured, offsets, kernel):
    lat_count = lax.axis_size("lat")
    lat_index = lax.axis_index("lat")
    depth_index = lax.axis_index("depth")
    band_rows, columns = potential.shape[3:]
    window = incident.shape[3]
    half_width = (kernel.shape[1] - 1) // 2
    half_band = band_rows // 2
    reach = 8 * half_width
    rows = half_band + 2 * reach
    probe, half = depth_index // 2, depth_index % 2
    order = jnp.stack([probe, 1 - probe])
    first_band = offsets[:, 0][order] // band_rows
    place_band = (lat_index - first_band) % lat_count
    own_layer = (first_band + place_band) // lat_count
    scalars = jnp.concatenate([own_layer, offsets[:, 1][order], half[None]]).astype(jnp.int32)

    own_t = transmissions(scalars, potential[:, 0], window)
    up = [(i, (i + 1) % lat_count) for i in range(lat_count)]
    down = [((i + 1) % lat_count, i) for i in range(lat_count)]
    above = lax.ppermute(own_t[:, :, band_rows - reach :], "lat", up)
    below = lax.ppermute(own_t[:, :, :reach], "lat", down)
    none = jnp.zeros((), jnp.bfloat16)
    above = jnp.where((place_band > 0)[:, None, None, None], above, none)
    below = jnp.where((place_band < lat_count - 1)[:, None, None, None], below, none)
    ext_t = jnp.concatenate([above, own_t, below], axis=2)

    across = [(i, i ^ 2) for i in range(4)]
    beside = [(i, i ^ 1) for i in range(4)]
    far_t = lax.ppermute(ext_t[1], "depth", across)
    both_t = jnp.stack([ext_t[0], far_t])
    keep_t = lax.dynamic_slice_in_dim(both_t, half * half_band, rows, 2)
    send_t = lax.dynamic_slice_in_dim(both_t, (1 - half) * half_band, rows, 2)
    recv_t = lax.ppermute(send_t, "depth", beside)

    ring = []
    for d in range(4):
        for i in range(lat_count):
            to = (i + 1) % lat_count if d % 2 == 0 else (i - 1) % lat_count
            ring.append((d * lat_count + i, d * lat_count + to))

    def extended(array):
        axis = array.ndim - 2
        tail = lax.slice_in_dim(array, band_rows - reach, band_rows, axis=axis)
        front = lax.slice_in_dim(array, 0, reach, axis=axis)
        edge = lax.ppermute(jnp.where(half == 0, tail, front), ("depth", "lat"), ring)
        kept = rows - reach
        low = jnp.concatenate([edge, lax.slice_in_dim(array, 0, kept, axis=axis)], axis)
        high = jnp.concatenate(
            [lax.slice_in_dim(array, band_rows - kept, band_rows, axis=axis), edge], axis
        )
        return jnp.where(half == 0, low, high)

    wave = extended(
        lax.dynamic_index_in_dim(incident, probe, 1, keepdims=False).astype(jnp.bfloat16)
    )
    meas = extended(lax.dynamic_index_in_dim(measured, probe, 0, keepdims=False))

    base = place_band[0] * band_rows + half * half_band - reach
    facts = jnp.stack([base, half, probe]).astype(jnp.int32)
    terms = section_terms(
        facts, kernel.astype(jnp.float32), keep_t, recv_t, wave, meas, half_band
    )
    joined = jnp.stack([terms[0], lax.ppermute(terms[1], "depth", beside)], axis=1)
    other = lax.ppermute(joined[1], "depth", across)
    return placed(scalars, joined[0], other, columns)[:, None]


def solution(mesh):
    def run(*args):
        potential, incident, _, _, kernel = args
        body = local_fast if fits(mesh, potential.shape, incident.shape, kernel.shape) else local
        in_specs = (
            P(None, "depth", None, "lat", None),
            P(None, None, "lat", None),
            P(None, "lat", None),
            P(),
            P(),
        )
        out_specs = P(None, "depth", None, "lat", None)
        return jax.shard_map(
            body, mesh=mesh, in_specs=in_specs, out_specs=out_specs, check_vma=False
        )(*args)

    return run
```

```python
import functools

import jax
import jax.numpy as jnp
from jax import lax
from jax.experimental import pallas as pl
from jax.experimental.pallas import tpu as pltpu
from jax.sharding import PartitionSpec as P


def with_halo(cells, sides, width):
    for axis, dim in sides:
        count = lax.axis_size(axis)
        head = lax.slice_in_dim(cells, 0, width, axis=dim)
        tail = lax.slice_in_dim(cells, cells.shape[dim] - width, cells.shape[dim], axis=dim)
        cells = jnp.concatenate(
            [
                lax.ppermute(tail, axis, [(i, (i + 1) % count) for i in range(count)]),
                cells,
                lax.ppermute(head, axis, [((i + 1) % count, i) for i in range(count)]),
            ],
            axis=dim,
        )
    return cells


def from_behind(array, axis, by):
    count = lax.axis_size(axis)
    pairs = [(i, i + by) for i in range(count) if 0 <= i + by < count]
    return lax.ppermute(array, axis, pairs)


def rounded(field_in):
    return lax.optimization_barrier(field_in.astype(jnp.bfloat16)).astype(jnp.float32)


def band_matrix(taps_re, taps_im, row_count, col_count, half_width, transposed):
    row_index = lax.broadcasted_iota(jnp.int32, (row_count, col_count), 0)
    col_index = lax.broadcasted_iota(jnp.int32, (row_count, col_count), 1)
    offset = row_index - col_index if transposed else col_index - row_index
    chooser = (offset[:, :, None] == jnp.arange(2 * half_width + 1, dtype=jnp.int32)).astype(
        jnp.float32
    )
    real_part = jnp.sum(chooser * taps_re, axis=2).astype(jnp.bfloat16)
    imag_part = jnp.sum(chooser * taps_im, axis=2).astype(jnp.bfloat16)
    return (real_part, imag_part)


def along_rows(field_in, real_mat, imag_mat):
    direct = jnp.einsum("rq,xpqc->xprc", real_mat, field_in, preferred_element_type=jnp.float32)
    crossed = jnp.einsum("rq,xpqc->xprc", imag_mat, field_in, preferred_element_type=jnp.float32)
    return jnp.stack([direct[0] - crossed[1], crossed[0] + direct[1]])


def along_cols(field_in, real_slab, imag_slab, half_width):
    columns = field_in.shape[-1]
    blocks = columns // 128
    padded = jnp.pad(field_in, ((0, 0), (0, 0), (0, 0), (half_width, 128 - half_width)))
    main_part = padded[..., :columns].reshape(field_in.shape[:-1] + (blocks, 128))
    extra_part = padded[..., 128 : columns + 128].reshape(field_in.shape[:-1] + (blocks, 128))[
        ..., : 2 * half_width
    ]
    slab_rows = jnp.concatenate([main_part, extra_part], axis=-1)
    direct = jnp.einsum("xprbq,qo->xprbo", slab_rows, real_slab, preferred_element_type=jnp.float32)
    crossed = jnp.einsum(
        "xprbq,qo->xprbo", slab_rows, imag_slab, preferred_element_type=jnp.float32
    )
    joined = jnp.stack([direct[0] - crossed[1], crossed[0] + direct[1]])
    return joined.reshape(field_in.shape)


def local(potential, incident, measured, offsets, kernel):
    lat_count = lax.axis_size("lat")
    depth_count = lax.axis_size("depth")
    lat_index = lax.axis_index("lat")
    depth_index = lax.axis_index("depth")
    band_rows = potential.shape[3]
    window = incident.shape[3]
    probe_count = incident.shape[1]
    half_width = (kernel.shape[1] - 1) // 2
    taps_re = kernel[0].astype(jnp.float32)
    taps_im = kernel[1].astype(jnp.float32)
    back_re = taps_re[::-1]
    back_im = -taps_im[::-1]
    row_pixel = offsets[:, 0]
    col_pixel = offsets[:, 1]
    first_band = row_pixel // band_rows
    place_band = (lat_index - first_band) % lat_count
    layer_pot = potential[:, 0]
    reach_steps = 2
    margin = reach_steps * half_width
    full_rows = band_rows + 2 * margin
    most_out = full_rows - 2 * half_width
    row_forward = band_matrix(taps_re, taps_im, most_out, full_rows, half_width, False)
    row_adjoint = band_matrix(back_re, back_im, most_out, full_rows, half_width, False)
    column_forward = band_matrix(taps_re, taps_im, 128 + 2 * half_width, 128, half_width, True)
    column_adjoint = band_matrix(back_re, back_im, 128 + 2 * half_width, 128, half_width, True)
    local_rows = jnp.arange(full_rows, dtype=jnp.int32) - margin
    window_row = place_band[:, None] * band_rows + local_rows[None, :]
    valid_rows = (window_row >= 0) & (window_row < window)
    keep_mask = valid_rows[None, :, :, None]
    padded_pot = with_halo(layer_pot, (("lat", 2),), margin)
    local_rows = jnp.arange(band_rows + 2 * margin, dtype=jnp.int32) - margin
    side_rows = (local_rows >= band_rows).astype(jnp.int32) - (local_rows < 0).astype(jnp.int32)
    halves = jnp.clip(
        (first_band[:, None] + place_band[:, None] + side_rows[None, :]) // lat_count, 0, 1
    )

    def cut_window(col_start):
        return lax.dynamic_slice_in_dim(padded_pot, col_start, window, 3)

    windows = jax.vmap(cut_window)(col_pixel)
    chosen = jnp.where((halves == 0)[:, None, :, None], windows[:, :, 0], windows[:, :, 1])
    damping = jnp.exp(-chosen[:, 1])
    phase_part = chosen[:, 0]
    transmit = jnp.stack([damping * jnp.cos(phase_part), damping * jnp.sin(phase_part)])

    def forward_segment(wave_ext, extent):
        low_row = margin - extent
        rows_in = band_rows + 2 * extent
        rows_out = rows_in - 2 * half_width
        factor = transmit[:, :, low_row : low_row + rows_in]
        inside = keep_mask[:, :, low_row : low_row + rows_in]
        values = wave_ext.astype(jnp.float32)
        product = jnp.stack(
            [
                factor[0] * values[0] - factor[1] * values[1],
                factor[0] * values[1] + factor[1] * values[0],
            ]
        )
        product = jnp.where(inside, product, 0.0).astype(jnp.bfloat16)
        spread = along_rows(
            product, row_forward[0][:rows_out, :rows_in], row_forward[1][:rows_out, :rows_in]
        ).astype(jnp.bfloat16)
        return along_cols(spread, column_forward[0], column_forward[1], half_width).astype(
            jnp.bfloat16
        )

    def backward_segment(adjoint, extent, entry):
        low_row = margin - extent
        rows_in = band_rows + 2 * extent
        rows_out = rows_in - 2 * half_width
        inside = keep_mask[:, :, low_row : low_row + rows_in]
        masked = jnp.where(inside, adjoint, jnp.zeros_like(adjoint))
        spread = along_cols(masked, column_adjoint[0], column_adjoint[1], half_width).astype(
            jnp.bfloat16
        )
        local_grad = rounded(
            along_rows(
                spread, row_adjoint[0][:rows_out, :rows_in], row_adjoint[1][:rows_out, :rows_in]
            )
        )
        factor = transmit[:, :, low_row + half_width : low_row + half_width + rows_out]
        earlier = jnp.stack(
            [
                factor[0] * local_grad[0] + factor[1] * local_grad[1],
                factor[0] * local_grad[1] - factor[1] * local_grad[0],
            ]
        ).astype(jnp.bfloat16)
        centre = extent - half_width
        own_rows = local_grad[:, :, centre : centre + band_rows]
        own_factor = factor[:, :, centre : centre + band_rows]
        entry_wave = entry.astype(jnp.float32)
        cross_re = entry_wave[0] * own_rows[0] + entry_wave[1] * own_rows[1]
        cross_im = entry_wave[0] * own_rows[1] - entry_wave[1] * own_rows[0]
        turned_re = own_factor[0] * cross_re + own_factor[1] * cross_im
        turned_im = own_factor[0] * cross_im - own_factor[1] * cross_re
        return (earlier, jnp.stack([turned_im, -turned_re]))

    start_wave = incident.astype(jnp.bfloat16)
    zeros_wave = jnp.zeros_like(start_wave)
    blocks = depth_count // reach_steps

    def forward_block(block_index, carry):
        moving, stored, leaving = carry
        entering = jnp.where(depth_index == 0, start_wave, moving)
        wave_ext = with_halo(entering, (("lat", 2),), margin)
        for sub_step in range(reach_steps):
            extent = margin - sub_step * half_width
            result = forward_segment(wave_ext, extent)
            active = depth_index == block_index * reach_steps + sub_step
            stored = jnp.where(active, wave_ext[:, :, extent : extent + band_rows], stored)
            if sub_step == reach_steps - 1:
                leaving = jnp.where(active, result, leaving)
            wave_ext = from_behind(result, "depth", 1)
        return (wave_ext, stored, leaving)

    moving, stored, leaving = lax.fori_loop(
        0, blocks, forward_block, (zeros_wave, zeros_wave, zeros_wave)
    )
    exit_vals = leaving.astype(jnp.float32)
    residual = exit_vals[0] * exit_vals[0] + exit_vals[1] * exit_vals[1] - measured
    seed_wave = (2.0 * residual[None] * exit_vals).astype(jnp.bfloat16)
    zeros_term = jnp.zeros(start_wave.shape, jnp.float32)

    def backward_block(block_index, carry):
        moving_back, collected = carry
        entering = jnp.where(depth_index == depth_count - 1, seed_wave, moving_back)
        adjoint = with_halo(entering, (("lat", 2),), margin)
        for sub_step in range(reach_steps):
            extent = margin - sub_step * half_width
            earlier, grad_term = backward_segment(adjoint, extent, stored)
            active = depth_index == depth_count - 1 - (block_index * reach_steps + sub_step)
            collected = jnp.where(active, grad_term, collected)
            adjoint = from_behind(earlier, "depth", -1)
        return (adjoint, collected)

    moving_back, gathered = lax.fori_loop(0, blocks, backward_block, (zeros_wave, zeros_term))
    own_half = (first_band + place_band) // lat_count
    gradient = jnp.zeros_like(layer_pot)

    def accumulate(probe_index, running):
        portion = lax.dynamic_index_in_dim(gathered, probe_index, 1, keepdims=False)
        zero_index = jnp.zeros((), jnp.int32)
        corner = (zero_index, own_half[probe_index], zero_index, col_pixel[probe_index])
        current = lax.dynamic_slice(running, corner, (2, 1, band_rows, window))
        return lax.dynamic_update_slice(running, current + portion[:, None], corner)

    gradient = lax.fori_loop(0, probe_count, accumulate, gradient)
    return gradient[:, None]


ROW_BLOCK = 32


def fits(mesh, potential_shape, incident_shape, kernel_shape):
    depth_count, lat_count = mesh.shape["depth"], mesh.shape["lat"]
    slices, window, columns = potential_shape[1], incident_shape[3], potential_shape[4]
    half_width = (kernel_shape[1] - 1) // 2
    if incident_shape[1] != 2 or depth_count != 4 or slices != 4:
        return False
    half_band = potential_shape[3] // lat_count // 2
    reach = slices * half_width
    return (
        half_width <= 8
        and 2 * reach <= half_band
        and reach % 16 == 0
        and half_band % ROW_BLOCK == 0
        and window % 128 == 0
        and columns == 2 * window
    )


def series(square, divisors):
    total = 1.0 / divisors[-1]
    for divisor in divisors[-2::-1]:
        total = total * square + 1.0 / divisor
    return total


def transmission_kernel(scalars, pot_ref, out_ref):
    col = scalars[2 + pl.program_id(0)]
    columns, window = pot_ref.shape[3], out_ref.shape[3]
    shift = lax.rem(columns - col, columns)
    phase = pltpu.roll(pot_ref[0, 0], shift, 1)[:, :window]
    absorb = pltpu.roll(pot_ref[1, 0], shift, 1)[:, :window]
    damping = jnp.exp(-absorb)
    turn = 0.5 * phase
    square = turn * turn
    sine = turn * series(square, (1, -6, 120, -5040, 362880, -39916800, 6227020800))
    cosine = series(square, (1, -2, 24, -720, 40320, -3628800, 479001600))
    out_ref[0, 0] = (damping * (1.0 - 2.0 * sine * sine)).astype(out_ref.dtype)
    out_ref[0, 1] = (2.0 * damping * sine * cosine).astype(out_ref.dtype)


def transmissions(scalars, layer_pot, window):
    band_rows, columns = layer_pot.shape[2:]
    return pl.pallas_call(
        transmission_kernel,
        out_shape=jax.ShapeDtypeStruct((2, 2, band_rows, window), jnp.bfloat16),
        grid_spec=pltpu.PrefetchScalarGridSpec(
            num_scalar_prefetch=1,
            grid=(2, band_rows // ROW_BLOCK),
            in_specs=[
                pl.BlockSpec((2, 1, ROW_BLOCK, columns), lambda q, r, sc: (0, sc[q], r, 0))
            ],
            out_specs=pl.BlockSpec((1, 2, ROW_BLOCK, window), lambda q, r, sc: (q, 0, r, 0)),
        ),
    )(scalars, layer_pot)


def band(taps, rows, cols, start, half_width):
    offset = (
        lax.broadcasted_iota(jnp.int32, (rows, cols), 0)
        - lax.broadcasted_iota(jnp.int32, (rows, cols), 1)
        - start
        + half_width
    )
    total = jnp.zeros((rows, cols), jnp.float32)
    for tap_index, tap in enumerate(taps):
        total = jnp.where(offset == tap_index, tap, total)
    return total


def main_kernel(
    flags, taps_ref, own_t, incident, measured, out_ref,
    t_all, start, waves, adj, terms, row_mat, col_mat,
    send_sem, far_sem, beside_sem, edge_sem, start_sem, adj_sem, term_sem,
):
    slices, _, rows, window = waves.shape
    tap_count = taps_ref.shape[1]
    half_width = (tap_count - 1) // 2
    band_rows = own_t.shape[2]
    half_band = band_rows // 2
    reach = (rows - half_band) // 2
    blocks = window // 128
    depth, lat = lax.axis_index("depth"), lax.axis_index("lat")
    lat_count = lax.axis_size("lat")
    probe, half = depth // 2, lax.rem(depth, 2)
    other_half = 1 - half
    beside = 2 * probe + other_half
    across = 2 * (1 - probe) + half
    before, after = lax.rem(lat + lat_count - 1, lat_count), lax.rem(lat + 1, lat_count)
    near = lax.rem(lat + 2 * half + lat_count - 1, lat_count)

    def remote(src, dst, send, recv, to):
        return pltpu.make_async_remote_copy(
            src_ref=src,
            dst_ref=dst,
            send_sem=send_sem.at[send],
            recv_sem=recv,
            device_id=to,
            device_id_type=pl.DeviceIdType.MESH,
        )

    barrier = pltpu.get_barrier_semaphore()
    senders = [
        (beside, lat),
        (across, lat),
        (2 * (1 - probe) + other_half, lat),
        (2 * probe, near),
        (2 * probe + 1, near),
    ]
    for to in senders:
        pl.semaphore_signal(
            barrier, inc=1, device_id=to, device_id_type=pl.DeviceIdType.MESH
        )
    pl.semaphore_wait(barrier, len(senders))

    inner = pl.ds(reach, band_rows)
    far = remote(own_t.at[1], t_all.at[0, 1, :, inner], 0, far_sem.at[0], (across, lat))
    far.start()
    t_all[0, 0, :, inner] = own_t[0]
    start[:, inner] = incident[:, probe].astype(jnp.bfloat16)

    shared = pl.ds(pl.multiple_of(reach + (half_band - reach) * other_half, 16), half_band + reach)
    edge_rows = pl.ds(pl.multiple_of((band_rows + reach) * half, 16), reach)
    tail, head = pl.ds(band_rows, reach), pl.ds(reach, reach)
    low, high = pl.ds(0, reach), pl.ds(band_rows + reach, reach)

    def slot_copies(side):
        return [
            remote(
                t_all.at[0, side, :, shared], t_all.at[1, side, :, shared],
                1 + side, beside_sem.at[side], (beside, lat),
            ),
            remote(
                t_all.at[0, side, :, tail], t_all.at[half, side, :, low],
                3 + side, edge_sem.at[half, side], (2 * probe, after),
            ),
            remote(
                t_all.at[0, side, :, head], t_all.at[other_half, side, :, high],
                5 + side, edge_sem.at[other_half, side], (2 * probe + 1, before),
            ),
        ]

    def finish_slot(side):
        slot_copies(side)[0].wait_recv()
        for core in range(2):
            remote(
                t_all.at[0, side, :, tail], t_all.at[core, side, :, edge_rows],
                3, edge_sem.at[core, side], (beside, lat),
            ).wait_recv()
            edge = t_all[core, side, :, edge_rows]
            t_all[core, side, :, edge_rows] = jnp.where(flags[2] != 0, edge, jnp.zeros_like(edge))

    start_rows = pl.ds(pl.multiple_of(reach + (band_rows - reach) * other_half, 16), reach)
    toward = lax.rem(lat + 1 - 2 * half + lat_count, lat_count)
    start_copy = remote(
        start.at[:, start_rows], start.at[:, edge_rows], 7, start_sem.at[0], (depth, toward)
    )
    near_copies = slot_copies(0)
    for copy in [start_copy] + near_copies:
        copy.start()

    re = [taps_ref[0, i] for i in range(tap_count)]
    im = [taps_ref[1, i] for i in range(tap_count)]
    ways = ((re, im), (re[::-1], [-tap for tap in im[::-1]]))
    for way, (tap_re, tap_im) in enumerate(ways):
        real = band(tap_re[::-1], rows, rows, 0, half_width)
        imag = band(tap_im[::-1], rows, rows, 0, half_width)
        row_mat[way] = jnp.concatenate(
            [
                jnp.concatenate([real, -imag], axis=1),
                jnp.concatenate([imag, real], axis=1),
            ],
            axis=0,
        ).astype(jnp.bfloat16)
        real = band(tap_re, 384, 128, 128, half_width)
        imag = band(tap_im, 384, 128, 128, half_width)
        col_mat[way, :384, :128] = real.astype(jnp.bfloat16)
        col_mat[way, :384, 128:] = imag.astype(jnp.bfloat16)
        col_mat[way, 384:, :128] = (-imag).astype(jnp.bfloat16)
        col_mat[way, 384:, 128:] = real.astype(jnp.bfloat16)

    def rows_conv(field, way):
        return jnp.dot(row_mat[way], field, preferred_element_type=jnp.float32).astype(
            jnp.bfloat16
        )

    def cols_conv(field, way):
        edge = jnp.zeros((rows, 128), jnp.bfloat16)
        padded = [
            jnp.concatenate([edge, field[k * rows : (k + 1) * rows], edge], axis=1)
            for k in range(2)
        ]
        slabs = jnp.concatenate(
            [
                jnp.concatenate([part[:, 128 * b : 128 * b + 384] for part in padded], axis=1)
                for b in range(blocks)
            ],
            axis=0,
        )
        out = jnp.dot(slabs, col_mat[way], preferred_element_type=jnp.float32)
        out = out.astype(jnp.bfloat16)
        return [
            jnp.concatenate(
                [out[b * rows : (b + 1) * rows, 128 * k : 128 * k + 128] for b in range(blocks)],
                axis=1,
            )
            for k in range(2)
        ]

    extent = pl.ds(pl.multiple_of(half_band * half, 16), rows)

    def place_of(s):
        return lax.rem(s % 2 + half, 2), lax.rem(s // 2 + probe, 2)

    def factor(s):
        core, side = place_of(s)
        both = t_all[core, side, :, extent].astype(jnp.float32)
        return both[0], both[1]

    def relay():
        far.wait_recv()
        for copy in slot_copies(1):
            copy.start()
        finish_slot(1)

    start_copy.wait_recv()
    finish_slot(0)
    pl.when(probe == 1)(relay)
    waves[0] = start[:, extent]
    wave = None
    for s in range(slices):
        if s == slices // 2:
            pl.when(probe == 0)(relay)
        t_re, t_im = factor(s)
        w_re, w_im = waves[s, 0].astype(jnp.float32), waves[s, 1].astype(jnp.float32)
        product = jnp.concatenate([t_re * w_re - t_im * w_im, t_re * w_im + t_im * w_re], axis=0)
        wave = cols_conv(rows_conv(product.astype(jnp.bfloat16), 0), 0)
        if s + 1 < slices:
            waves[s + 1, 0], waves[s + 1, 1] = wave

    own = slice(reach, rows - reach)
    w_re, w_im = [part[own].astype(jnp.float32) for part in wave]
    own_rows = pl.ds(pl.multiple_of(half_band * half, 16), half_band)
    residual = 2.0 * (w_re * w_re + w_im * w_im - measured[probe, own_rows])
    adj[0, own] = (residual * w_re).astype(jnp.bfloat16)
    adj[1, own] = (residual * w_im).astype(jnp.bfloat16)
    up_lat = lax.rem(lat + half + lat_count - 1, lat_count)
    down_lat = lax.rem(lat + half, lat_count)
    adj_copies = [
        remote(
            adj.at[:, pl.ds(reach, reach)], adj.at[:, pl.ds(rows - reach, reach)],
            8, adj_sem.at[1], (beside, up_lat),
        ),
        remote(
            adj.at[:, pl.ds(rows - 2 * reach, reach)], adj.at[:, pl.ds(0, reach)],
            9, adj_sem.at[0], (beside, down_lat),
        ),
    ]
    for copy in adj_copies:
        copy.start()
    for copy in adj_copies:
        copy.wait_recv()
    adjoint = []
    for k in range(2):
        top, bottom = adj[k, :reach], adj[k, rows - reach :]
        adjoint.append(
            jnp.concatenate(
                [
                    jnp.where(flags[0] != 0, top, jnp.zeros_like(top)),
                    adj[k, own],
                    jnp.where(flags[1] != 0, bottom, jnp.zeros_like(bottom)),
                ],
                axis=0,
            )
        )

    def term_copy(s):
        core, side = place_of(s)
        at = 2 * side + core
        return remote(
            terms.at[s], out_ref.at[side, core], 10 + at, term_sem.at[at], (s, lat)
        )

    for s in reversed(range(slices)):
        spread = cols_conv(jnp.concatenate(adjoint, axis=0), 1)
        grad = rows_conv(jnp.concatenate(spread, axis=0), 1).astype(jnp.float32)
        g_re, g_im = grad[:rows], grad[rows:]
        t_re, t_im = factor(s)
        back_re = t_re * g_re + t_im * g_im
        back_im = t_re * g_im - t_im * g_re
        e_re = waves[s, 0, own].astype(jnp.float32)
        e_im = waves[s, 1, own].astype(jnp.float32)
        terms[s, 0] = (e_re * back_im[own] - e_im * back_re[own]).astype(jnp.bfloat16)
        terms[s, 1] = (-e_re * back_re[own] - e_im * back_im[own]).astype(jnp.bfloat16)
        pl.when(depth != s)(lambda: term_copy(s).start())

        @pl.when(depth == s)
        def _():
            out_ref[0, 0] = terms[s]

        adjoint = [back_re.astype(jnp.bfloat16), back_im.astype(jnp.bfloat16)]

    for copy in [far, start_copy] + near_copies + slot_copies(1) + adj_copies:
        copy.wait_send()
    for s in range(slices):
        pl.when(depth != s)(lambda: term_copy(s).wait_send())
    for at in range(1, 4):
        remote(
            terms.at[0], out_ref.at[at // 2, at % 2], 10 + at, term_sem.at[at], (beside, lat)
        ).wait_recv()


def section_terms(flags, taps, own_t, incident, measured, reach):
    slices, band_rows, window = 4, own_t.shape[2], own_t.shape[3]
    half_band = band_rows // 2
    rows = half_band + 2 * reach
    smem = pl.BlockSpec(memory_space=pltpu.SMEM)
    vmem = pl.BlockSpec(memory_space=pltpu.VMEM)
    return pl.pallas_call(
        main_kernel,
        out_shape=jax.ShapeDtypeStruct((2, 2, 2, half_band, window), jnp.bfloat16),
        in_specs=[smem, smem, vmem, vmem, vmem],
        out_specs=vmem,
        scratch_shapes=[
            pltpu.VMEM((2, 2, 2, band_rows + 2 * reach, window), jnp.bfloat16),
            pltpu.VMEM((2, band_rows + 2 * reach, window), jnp.bfloat16),
            pltpu.VMEM((slices, 2, rows, window), jnp.bfloat16),
            pltpu.VMEM((2, rows, window), jnp.bfloat16),
            pltpu.VMEM((slices, 2, half_band, window), jnp.bfloat16),
            pltpu.VMEM((2, 2 * rows, 2 * rows), jnp.bfloat16),
            pltpu.VMEM((2, 768, 256), jnp.bfloat16),
            pltpu.SemaphoreType.DMA((14,)),
            pltpu.SemaphoreType.DMA((1,)),
            pltpu.SemaphoreType.DMA((2,)),
            pltpu.SemaphoreType.DMA((2, 2)),
            pltpu.SemaphoreType.DMA((1,)),
            pltpu.SemaphoreType.DMA((2,)),
            pltpu.SemaphoreType.DMA((4,)),
        ],
        compiler_params=pltpu.CompilerParams(
            vmem_limit_bytes=48 * 1024 * 1024, collective_id=0, has_side_effects=True
        ),
    )(flags, taps, own_t, incident, measured)


def place_kernel(scalars, own_ref, other_ref, out_ref):
    columns, window = out_ref.shape[3], own_ref.shape[3]
    for part in range(2):
        totals = [None, None]
        for q, ref in enumerate((own_ref, other_ref)):
            values = ref[0, part].astype(jnp.float32)
            wide = jnp.concatenate([values, jnp.zeros_like(values)], axis=1)
            wide = pltpu.roll(wide, scalars[2 + q], 1)
            for layer in range(2):
                term = jnp.where(scalars[q] == layer, wide, 0.0)
                totals[layer] = term if q == 0 else totals[layer] + term
        for layer in range(2):
            out_ref[part, layer] = totals[layer]


def placed(scalars, own, other, columns):
    half_band, window = own.shape[2:]
    per_half = half_band // ROW_BLOCK

    def pick(r, sc):
        return (lax.rem(r // per_half + sc[4], 2), 0, lax.rem(r, per_half), 0)

    spec = pl.BlockSpec((1, 2, ROW_BLOCK, window), pick)
    return pl.pallas_call(
        place_kernel,
        out_shape=jax.ShapeDtypeStruct((2, 2, 2 * half_band, columns), jnp.float32),
        grid_spec=pltpu.PrefetchScalarGridSpec(
            num_scalar_prefetch=1,
            grid=(2 * per_half,),
            in_specs=[spec, spec],
            out_specs=pl.BlockSpec((2, 2, ROW_BLOCK, columns), lambda r, sc: (0, 0, r, 0)),
        ),
    )(scalars, own, other)


def local_fast(potential, incident, measured, offsets, kernel):
    lat_count = lax.axis_size("lat")
    lat_index = lax.axis_index("lat")
    depth_index = lax.axis_index("depth")
    band_rows, columns = potential.shape[3:]
    window = incident.shape[3]
    half_width = (kernel.shape[1] - 1) // 2
    half_band = band_rows // 2
    reach = 4 * half_width
    probe, half = depth_index // 2, depth_index % 2
    order = jnp.stack([probe, 1 - probe])
    first_band = offsets[:, 0][order] // band_rows
    place_band = (lat_index - first_band) % lat_count
    own_layer = (first_band + place_band) // lat_count
    scalars = jnp.concatenate([own_layer, offsets[:, 1][order], half[None]]).astype(jnp.int32)

    own_t = transmissions(scalars, potential[:, 0], window)
    top_ok = (half == 1) | (place_band[0] > 0)
    bottom_ok = (half == 0) | (place_band[0] < lat_count - 1)
    flags = jnp.stack([top_ok, bottom_ok, top_ok & bottom_ok]).astype(jnp.int32)
    terms = section_terms(flags, kernel.astype(jnp.float32), own_t, incident, measured, reach)
    return placed(scalars, terms[0], terms[1], columns)[:, None]


def solution(mesh):
    def run(*args):
        potential, incident, _, _, kernel = args
        body = local_fast if fits(mesh, potential.shape, incident.shape, kernel.shape) else local
        in_specs = (
            P(None, "depth", None, "lat", None),
            P(None, None, "lat", None),
            P(None, "lat", None),
            P(),
            P(),
        )
        out_specs = P(None, "depth", None, "lat", None)
        return jax.shard_map(
            body, mesh=mesh, in_specs=in_specs, out_specs=out_specs, check_vma=False
        )(*args)

    return run
```

```python
import functools

import jax
import jax.numpy as jnp
from jax import lax
from jax.experimental import pallas as pl
from jax.experimental.pallas import tpu as pltpu
from jax.sharding import PartitionSpec as P


def with_halo(cells, sides, width):
    for axis, dim in sides:
        count = lax.axis_size(axis)
        head = lax.slice_in_dim(cells, 0, width, axis=dim)
        tail = lax.slice_in_dim(cells, cells.shape[dim] - width, cells.shape[dim], axis=dim)
        cells = jnp.concatenate(
            [
                lax.ppermute(tail, axis, [(i, (i + 1) % count) for i in range(count)]),
                cells,
                lax.ppermute(head, axis, [((i + 1) % count, i) for i in range(count)]),
            ],
            axis=dim,
        )
    return cells


def from_behind(array, axis, by):
    count = lax.axis_size(axis)
    pairs = [(i, i + by) for i in range(count) if 0 <= i + by < count]
    return lax.ppermute(array, axis, pairs)


def rounded(field_in):
    return lax.optimization_barrier(field_in.astype(jnp.bfloat16)).astype(jnp.float32)


def band_matrix(taps_re, taps_im, row_count, col_count, half_width, transposed):
    row_index = lax.broadcasted_iota(jnp.int32, (row_count, col_count), 0)
    col_index = lax.broadcasted_iota(jnp.int32, (row_count, col_count), 1)
    offset = row_index - col_index if transposed else col_index - row_index
    chooser = (offset[:, :, None] == jnp.arange(2 * half_width + 1, dtype=jnp.int32)).astype(
        jnp.float32
    )
    real_part = jnp.sum(chooser * taps_re, axis=2).astype(jnp.bfloat16)
    imag_part = jnp.sum(chooser * taps_im, axis=2).astype(jnp.bfloat16)
    return (real_part, imag_part)


def along_rows(field_in, real_mat, imag_mat):
    direct = jnp.einsum("rq,xpqc->xprc", real_mat, field_in, preferred_element_type=jnp.float32)
    crossed = jnp.einsum("rq,xpqc->xprc", imag_mat, field_in, preferred_element_type=jnp.float32)
    return jnp.stack([direct[0] - crossed[1], crossed[0] + direct[1]])


def along_cols(field_in, real_slab, imag_slab, half_width):
    columns = field_in.shape[-1]
    blocks = columns // 128
    padded = jnp.pad(field_in, ((0, 0), (0, 0), (0, 0), (half_width, 128 - half_width)))
    main_part = padded[..., :columns].reshape(field_in.shape[:-1] + (blocks, 128))
    extra_part = padded[..., 128 : columns + 128].reshape(field_in.shape[:-1] + (blocks, 128))[
        ..., : 2 * half_width
    ]
    slab_rows = jnp.concatenate([main_part, extra_part], axis=-1)
    direct = jnp.einsum("xprbq,qo->xprbo", slab_rows, real_slab, preferred_element_type=jnp.float32)
    crossed = jnp.einsum(
        "xprbq,qo->xprbo", slab_rows, imag_slab, preferred_element_type=jnp.float32
    )
    joined = jnp.stack([direct[0] - crossed[1], crossed[0] + direct[1]])
    return joined.reshape(field_in.shape)


def local(potential, incident, measured, offsets, kernel):
    lat_count = lax.axis_size("lat")
    depth_count = lax.axis_size("depth")
    lat_index = lax.axis_index("lat")
    depth_index = lax.axis_index("depth")
    band_rows = potential.shape[3]
    window = incident.shape[3]
    probe_count = incident.shape[1]
    half_width = (kernel.shape[1] - 1) // 2
    taps_re = kernel[0].astype(jnp.float32)
    taps_im = kernel[1].astype(jnp.float32)
    back_re = taps_re[::-1]
    back_im = -taps_im[::-1]
    row_pixel = offsets[:, 0]
    col_pixel = offsets[:, 1]
    first_band = row_pixel // band_rows
    place_band = (lat_index - first_band) % lat_count
    layer_pot = potential[:, 0]
    reach_steps = 2
    margin = reach_steps * half_width
    full_rows = band_rows + 2 * margin
    most_out = full_rows - 2 * half_width
    row_forward = band_matrix(taps_re, taps_im, most_out, full_rows, half_width, False)
    row_adjoint = band_matrix(back_re, back_im, most_out, full_rows, half_width, False)
    column_forward = band_matrix(taps_re, taps_im, 128 + 2 * half_width, 128, half_width, True)
    column_adjoint = band_matrix(back_re, back_im, 128 + 2 * half_width, 128, half_width, True)
    local_rows = jnp.arange(full_rows, dtype=jnp.int32) - margin
    window_row = place_band[:, None] * band_rows + local_rows[None, :]
    valid_rows = (window_row >= 0) & (window_row < window)
    keep_mask = valid_rows[None, :, :, None]
    padded_pot = with_halo(layer_pot, (("lat", 2),), margin)
    local_rows = jnp.arange(band_rows + 2 * margin, dtype=jnp.int32) - margin
    side_rows = (local_rows >= band_rows).astype(jnp.int32) - (local_rows < 0).astype(jnp.int32)
    halves = jnp.clip(
        (first_band[:, None] + place_band[:, None] + side_rows[None, :]) // lat_count, 0, 1
    )

    def cut_window(col_start):
        return lax.dynamic_slice_in_dim(padded_pot, col_start, window, 3)

    windows = jax.vmap(cut_window)(col_pixel)
    chosen = jnp.where((halves == 0)[:, None, :, None], windows[:, :, 0], windows[:, :, 1])
    damping = jnp.exp(-chosen[:, 1])
    phase_part = chosen[:, 0]
    transmit = jnp.stack([damping * jnp.cos(phase_part), damping * jnp.sin(phase_part)])

    def forward_segment(wave_ext, extent):
        low_row = margin - extent
        rows_in = band_rows + 2 * extent
        rows_out = rows_in - 2 * half_width
        factor = transmit[:, :, low_row : low_row + rows_in]
        inside = keep_mask[:, :, low_row : low_row + rows_in]
        values = wave_ext.astype(jnp.float32)
        product = jnp.stack(
            [
                factor[0] * values[0] - factor[1] * values[1],
                factor[0] * values[1] + factor[1] * values[0],
            ]
        )
        product = jnp.where(inside, product, 0.0).astype(jnp.bfloat16)
        spread = along_rows(
            product, row_forward[0][:rows_out, :rows_in], row_forward[1][:rows_out, :rows_in]
        ).astype(jnp.bfloat16)
        return along_cols(spread, column_forward[0], column_forward[1], half_width).astype(
            jnp.bfloat16
        )

    def backward_segment(adjoint, extent, entry):
        low_row = margin - extent
        rows_in = band_rows + 2 * extent
        rows_out = rows_in - 2 * half_width
        inside = keep_mask[:, :, low_row : low_row + rows_in]
        masked = jnp.where(inside, adjoint, jnp.zeros_like(adjoint))
        spread = along_cols(masked, column_adjoint[0], column_adjoint[1], half_width).astype(
            jnp.bfloat16
        )
        local_grad = rounded(
            along_rows(
                spread, row_adjoint[0][:rows_out, :rows_in], row_adjoint[1][:rows_out, :rows_in]
            )
        )
        factor = transmit[:, :, low_row + half_width : low_row + half_width + rows_out]
        earlier = jnp.stack(
            [
                factor[0] * local_grad[0] + factor[1] * local_grad[1],
                factor[0] * local_grad[1] - factor[1] * local_grad[0],
            ]
        ).astype(jnp.bfloat16)
        centre = extent - half_width
        own_rows = local_grad[:, :, centre : centre + band_rows]
        own_factor = factor[:, :, centre : centre + band_rows]
        entry_wave = entry.astype(jnp.float32)
        cross_re = entry_wave[0] * own_rows[0] + entry_wave[1] * own_rows[1]
        cross_im = entry_wave[0] * own_rows[1] - entry_wave[1] * own_rows[0]
        turned_re = own_factor[0] * cross_re + own_factor[1] * cross_im
        turned_im = own_factor[0] * cross_im - own_factor[1] * cross_re
        return (earlier, jnp.stack([turned_im, -turned_re]))

    start_wave = incident.astype(jnp.bfloat16)
    zeros_wave = jnp.zeros_like(start_wave)
    blocks = depth_count // reach_steps

    def forward_block(block_index, carry):
        moving, stored, leaving = carry
        entering = jnp.where(depth_index == 0, start_wave, moving)
        wave_ext = with_halo(entering, (("lat", 2),), margin)
        for sub_step in range(reach_steps):
            extent = margin - sub_step * half_width
            result = forward_segment(wave_ext, extent)
            active = depth_index == block_index * reach_steps + sub_step
            stored = jnp.where(active, wave_ext[:, :, extent : extent + band_rows], stored)
            if sub_step == reach_steps - 1:
                leaving = jnp.where(active, result, leaving)
            wave_ext = from_behind(result, "depth", 1)
        return (wave_ext, stored, leaving)

    moving, stored, leaving = lax.fori_loop(
        0, blocks, forward_block, (zeros_wave, zeros_wave, zeros_wave)
    )
    exit_vals = leaving.astype(jnp.float32)
    residual = exit_vals[0] * exit_vals[0] + exit_vals[1] * exit_vals[1] - measured
    seed_wave = (2.0 * residual[None] * exit_vals).astype(jnp.bfloat16)
    zeros_term = jnp.zeros(start_wave.shape, jnp.float32)

    def backward_block(block_index, carry):
        moving_back, collected = carry
        entering = jnp.where(depth_index == depth_count - 1, seed_wave, moving_back)
        adjoint = with_halo(entering, (("lat", 2),), margin)
        for sub_step in range(reach_steps):
            extent = margin - sub_step * half_width
            earlier, grad_term = backward_segment(adjoint, extent, stored)
            active = depth_index == depth_count - 1 - (block_index * reach_steps + sub_step)
            collected = jnp.where(active, grad_term, collected)
            adjoint = from_behind(earlier, "depth", -1)
        return (adjoint, collected)

    moving_back, gathered = lax.fori_loop(0, blocks, backward_block, (zeros_wave, zeros_term))
    own_half = (first_band + place_band) // lat_count
    gradient = jnp.zeros_like(layer_pot)

    def accumulate(probe_index, running):
        portion = lax.dynamic_index_in_dim(gathered, probe_index, 1, keepdims=False)
        zero_index = jnp.zeros((), jnp.int32)
        corner = (zero_index, own_half[probe_index], zero_index, col_pixel[probe_index])
        current = lax.dynamic_slice(running, corner, (2, 1, band_rows, window))
        return lax.dynamic_update_slice(running, current + portion[:, None], corner)

    gradient = lax.fori_loop(0, probe_count, accumulate, gradient)
    return gradient[:, None]


ROW_BLOCK = 32


def fits(mesh, potential_shape, incident_shape, kernel_shape):
    depth_count, lat_count = mesh.shape["depth"], mesh.shape["lat"]
    slices, window, columns = potential_shape[1], incident_shape[3], potential_shape[4]
    half_width = (kernel_shape[1] - 1) // 2
    if incident_shape[1] != 2 or depth_count != 4 or slices != 4:
        return False
    half_band = potential_shape[3] // lat_count // 2
    reach = slices * half_width
    return (
        half_width <= 8
        and 2 * reach <= half_band
        and reach % 16 == 0
        and half_band % ROW_BLOCK == 0
        and window % 128 == 0
        and columns == 2 * window
    )


def series(square, divisors):
    total = 1.0 / divisors[-1]
    for divisor in divisors[-2::-1]:
        total = total * square + 1.0 / divisor
    return total


def probe_place(offsets, probe, lat, lat_count, band_rows):
    first_band = offsets[probe, 0] // band_rows
    place_band = lax.rem(lat - first_band + lat_count, lat_count)
    return place_band, (first_band + place_band) // lat_count, offsets[probe, 1]


def write_transmission(pot, layer, col, row, dst, dst_row):
    window = dst.shape[2]
    last = pot.shape[3] // 128 - 1
    block, lane = col // 128, lax.rem(col, 128)
    turn_by = lax.rem(128 - lane, 128)
    here = lax.broadcasted_iota(jnp.int32, (ROW_BLOCK, 128), 1) < 128 - lane
    rows = pl.ds(row, ROW_BLOCK)

    def turned(b):
        at = pl.multiple_of(128 * jnp.minimum(block + b, last), 128)
        return [pltpu.roll(pot[k, layer, rows, pl.ds(at, 128)], turn_by, 1) for k in range(2)]

    low = turned(0)
    for b in range(window // 128):
        high = turned(b + 1)
        phase, absorb = [jnp.where(here, low[k], high[k]) for k in range(2)]
        damping = jnp.exp(-absorb)
        turn = 0.5 * phase
        square = turn * turn
        sine = turn * series(square, (1, -6, 120, -5040, 362880, -39916800, 6227020800))
        cosine = series(square, (1, -2, 24, -720, 40320, -3628800, 479001600))
        at = pl.ds(128 * b, 128)
        out_rows = pl.ds(dst_row, ROW_BLOCK)
        dst[0, out_rows, at] = (damping * (1.0 - 2.0 * sine * sine)).astype(dst.dtype)
        dst[1, out_rows, at] = (2.0 * damping * sine * cosine).astype(dst.dtype)
        low = high


def transmission_kernel(offsets, pot_ref, out_ref):
    depth, lat = lax.axis_index("depth"), lax.axis_index("lat")
    band_rows = ROW_BLOCK * pl.num_programs(0)
    for q in range(2):
        place = lax.rem(depth // 2 + q, 2)
        _, layer, col = probe_place(offsets, place, lat, lax.axis_size("lat"), band_rows)
        write_transmission(pot_ref, layer, col, 0, out_ref.at[q], 0)


def transmissions(offsets, potential, window):
    band_rows, columns = potential.shape[3:]
    return pl.pallas_call(
        transmission_kernel,
        out_shape=jax.ShapeDtypeStruct((2, 2, band_rows, window), jnp.bfloat16),
        grid=(band_rows // ROW_BLOCK,),
        in_specs=[
            pl.BlockSpec(memory_space=pltpu.SMEM),
            pl.BlockSpec((2, 2, ROW_BLOCK, columns), lambda r: (0, 0, r, 0)),
        ],
        out_specs=pl.BlockSpec((2, 2, ROW_BLOCK, window), lambda r: (0, 0, r, 0)),
    )(offsets, potential[:, 0])


def band(taps, rows, cols, start, half_width):
    offset = (
        lax.broadcasted_iota(jnp.int32, (rows, cols), 0)
        - lax.broadcasted_iota(jnp.int32, (rows, cols), 1)
        - start
        + half_width
    )
    total = jnp.zeros((rows, cols), jnp.float32)
    for tap_index, tap in enumerate(taps):
        total = jnp.where(offset == tap_index, tap, total)
    return total


def main_kernel(
    offsets, taps_ref, trans_hbm, incident_hbm, measured_hbm, out_ref,
    incident, measured, far_t, t_all, start, waves, adj, terms, row_mat, col_mat,
    send_sem, load_sem, far_sem, beside_sem, edge_sem, start_sem, adj_sem, term_sem,
):
    slices, _, rows, window = waves.shape
    tap_count = taps_ref.shape[1]
    half_width = (tap_count - 1) // 2
    band_rows = far_t.shape[1]
    half_band = band_rows // 2
    reach = (rows - half_band) // 2
    blocks = window // 128
    depth, lat = lax.axis_index("depth"), lax.axis_index("lat")
    lat_count = lax.axis_size("lat")
    probe, half = depth // 2, lax.rem(depth, 2)
    other_half = 1 - half
    beside = 2 * probe + other_half
    across = 2 * (1 - probe) + half
    before, after = lax.rem(lat + lat_count - 1, lat_count), lax.rem(lat + 1, lat_count)
    near = lax.rem(lat + 2 * half + lat_count - 1, lat_count)

    def remote(src, dst, send, recv, to):
        return pltpu.make_async_remote_copy(
            src_ref=src,
            dst_ref=dst,
            send_sem=send_sem.at[send],
            recv_sem=recv,
            device_id=to,
            device_id_type=pl.DeviceIdType.MESH,
        )

    own_rows = pl.ds(pl.multiple_of(half_band * half, 16), half_band)
    loads = [
        pltpu.make_async_copy(src, dst, load_sem.at[i])
        for i, (src, dst) in enumerate(
            [
                (trans_hbm.at[1], far_t),
                (trans_hbm.at[0], t_all.at[0, 0, :, pl.ds(reach, band_rows)]),
                (incident_hbm.at[:, probe], incident),
                (measured_hbm.at[probe, own_rows], measured),
            ]
        )
    ]
    for load in loads:
        load.start()

    barrier = pltpu.get_barrier_semaphore()
    senders = [
        (beside, lat),
        (across, lat),
        (2 * (1 - probe) + other_half, lat),
        (2 * probe, near),
        (2 * probe + 1, near),
    ]
    for to in senders:
        pl.semaphore_signal(
            barrier, inc=1, device_id=to, device_id_type=pl.DeviceIdType.MESH
        )
    pl.semaphore_wait(barrier, len(senders))

    inner = pl.ds(reach, band_rows)
    place_row = band_rows * lat
    at_row = offsets[probe, 0]
    at_top = (at_row == place_row) | (at_row == place_row + window)
    at_bottom = (at_row == place_row + band_rows) | (at_row == place_row + band_rows - window)
    top_ok = jnp.logical_not(at_top) | (half == 1)
    bottom_ok = jnp.logical_not(at_bottom) | (half == 0)

    far = remote(far_t, t_all.at[0, 1, :, inner], 0, far_sem.at[0], (across, lat))
    loads[0].wait()
    far.start()
    loads[2].wait()
    start[:, inner] = incident[...].astype(jnp.bfloat16)
    loads[1].wait()

    shared = pl.ds(pl.multiple_of(reach + (half_band - reach) * other_half, 16), half_band + reach)
    edge_rows = pl.ds(pl.multiple_of((band_rows + reach) * half, 16), reach)
    tail, head = pl.ds(band_rows, reach), pl.ds(reach, reach)
    low, high = pl.ds(0, reach), pl.ds(band_rows + reach, reach)

    def slot_copies(side):
        return [
            remote(
                t_all.at[0, side, :, shared], t_all.at[1, side, :, shared],
                1 + side, beside_sem.at[side], (beside, lat),
            ),
            remote(
                t_all.at[0, side, :, tail], t_all.at[half, side, :, low],
                3 + side, edge_sem.at[half, side], (2 * probe, after),
            ),
            remote(
                t_all.at[0, side, :, head], t_all.at[other_half, side, :, high],
                5 + side, edge_sem.at[other_half, side], (2 * probe + 1, before),
            ),
        ]

    def finish_slot(side):
        slot_copies(side)[0].wait_recv()
        for core in range(2):
            remote(
                t_all.at[0, side, :, tail], t_all.at[core, side, :, edge_rows],
                3, edge_sem.at[core, side], (beside, lat),
            ).wait_recv()
            edge = t_all[core, side, :, edge_rows]
            t_all[core, side, :, edge_rows] = jnp.where(top_ok & bottom_ok, edge, jnp.zeros_like(edge))

    start_rows = pl.ds(pl.multiple_of(reach + (band_rows - reach) * other_half, 16), reach)
    toward = lax.rem(lat + 1 - 2 * half + lat_count, lat_count)
    start_copy = remote(
        start.at[:, start_rows], start.at[:, edge_rows], 7, start_sem.at[0], (depth, toward)
    )
    near_copies = slot_copies(0)
    for copy in [start_copy] + near_copies:
        copy.start()

    taps = taps_ref[...].astype(jnp.float32)
    re = [taps[0:1, i : i + 1] for i in range(tap_count)]
    im = [taps[1:2, i : i + 1] for i in range(tap_count)]
    ways = ((re, im), (re[::-1], [-tap for tap in im[::-1]]))
    for way, (tap_re, tap_im) in enumerate(ways):
        real = band(tap_re[::-1], rows, rows, 0, half_width)
        imag = band(tap_im[::-1], rows, rows, 0, half_width)
        row_mat[way] = jnp.concatenate(
            [
                jnp.concatenate([real, -imag], axis=1),
                jnp.concatenate([imag, real], axis=1),
            ],
            axis=0,
        ).astype(jnp.bfloat16)
        real = band(tap_re, 384, 128, 128, half_width)
        imag = band(tap_im, 384, 128, 128, half_width)
        col_mat[way, :384, :128] = real.astype(jnp.bfloat16)
        col_mat[way, :384, 128:] = imag.astype(jnp.bfloat16)
        col_mat[way, 384:, :128] = (-imag).astype(jnp.bfloat16)
        col_mat[way, 384:, 128:] = real.astype(jnp.bfloat16)

    def rows_conv(field, way):
        return jnp.dot(row_mat[way], field, preferred_element_type=jnp.float32).astype(
            jnp.bfloat16
        )

    def cols_conv(field, way):
        edge = jnp.zeros((rows, 128), jnp.bfloat16)
        padded = [
            jnp.concatenate([edge, field[k * rows : (k + 1) * rows], edge], axis=1)
            for k in range(2)
        ]
        slabs = jnp.concatenate(
            [
                jnp.concatenate([part[:, 128 * b : 128 * b + 384] for part in padded], axis=1)
                for b in range(blocks)
            ],
            axis=0,
        )
        out = jnp.dot(slabs, col_mat[way], preferred_element_type=jnp.float32)
        out = out.astype(jnp.bfloat16)
        return [
            jnp.concatenate(
                [out[b * rows : (b + 1) * rows, 128 * k : 128 * k + 128] for b in range(blocks)],
                axis=1,
            )
            for k in range(2)
        ]

    extent = pl.ds(pl.multiple_of(half_band * half, 16), rows)

    def place_of(s):
        return lax.rem(s % 2 + half, 2), lax.rem(s // 2 + probe, 2)

    def factor(s):
        core, side = place_of(s)
        both = t_all[core, side, :, extent].astype(jnp.float32)
        return both[0], both[1]

    def relay():
        far.wait_recv()
        for copy in slot_copies(1):
            copy.start()
        finish_slot(1)

    start_copy.wait_recv()
    finish_slot(0)
    pl.when(probe == 1)(relay)
    waves[0] = start[:, extent]
    wave = None
    for s in range(slices):
        if s == slices // 2:
            pl.when(probe == 0)(relay)
        t_re, t_im = factor(s)
        w_re, w_im = waves[s, 0].astype(jnp.float32), waves[s, 1].astype(jnp.float32)
        product = jnp.concatenate([t_re * w_re - t_im * w_im, t_re * w_im + t_im * w_re], axis=0)
        wave = cols_conv(rows_conv(product.astype(jnp.bfloat16), 0), 0)
        if s + 1 < slices:
            waves[s + 1, 0], waves[s + 1, 1] = wave

    own = slice(reach, rows - reach)
    w_re, w_im = [part[own].astype(jnp.float32) for part in wave]
    loads[3].wait()
    residual = 2.0 * (w_re * w_re + w_im * w_im - measured[...])
    adj[0, own] = (residual * w_re).astype(jnp.bfloat16)
    adj[1, own] = (residual * w_im).astype(jnp.bfloat16)
    up_lat = lax.rem(lat + half + lat_count - 1, lat_count)
    down_lat = lax.rem(lat + half, lat_count)
    adj_copies = [
        remote(
            adj.at[:, pl.ds(reach, reach)], adj.at[:, pl.ds(rows - reach, reach)],
            8, adj_sem.at[1], (beside, up_lat),
        ),
        remote(
            adj.at[:, pl.ds(rows - 2 * reach, reach)], adj.at[:, pl.ds(0, reach)],
            9, adj_sem.at[0], (beside, down_lat),
        ),
    ]
    for copy in adj_copies:
        copy.start()
    for copy in adj_copies:
        copy.wait_recv()
    adjoint = []
    for k in range(2):
        top, bottom = adj[k, :reach], adj[k, rows - reach :]
        adjoint.append(
            jnp.concatenate(
                [
                    jnp.where(top_ok, top, jnp.zeros_like(top)),
                    adj[k, own],
                    jnp.where(bottom_ok, bottom, jnp.zeros_like(bottom)),
                ],
                axis=0,
            )
        )

    def term_copy(s):
        core, side = place_of(s)
        at = 2 * side + core
        return remote(
            terms.at[s], out_ref.at[side, core], 9 + at, term_sem.at[at], (s, lat)
        )

    for s in reversed(range(slices)):
        spread = cols_conv(jnp.concatenate(adjoint, axis=0), 1)
        grad = rows_conv(jnp.concatenate(spread, axis=0), 1).astype(jnp.float32)
        g_re, g_im = grad[:rows], grad[rows:]
        t_re, t_im = factor(s)
        back_re = t_re * g_re + t_im * g_im
        back_im = t_re * g_im - t_im * g_re
        e_re = waves[s, 0, own].astype(jnp.float32)
        e_im = waves[s, 1, own].astype(jnp.float32)
        terms[s, 0] = (e_re * back_im[own] - e_im * back_re[own]).astype(jnp.bfloat16)
        terms[s, 1] = (-e_re * back_re[own] - e_im * back_im[own]).astype(jnp.bfloat16)
        pl.when(depth != s)(lambda: term_copy(s).start())

        @pl.when(depth == s)
        def _():
            out_ref[0, 0] = terms[s]

        adjoint = [back_re.astype(jnp.bfloat16), back_im.astype(jnp.bfloat16)]

    for copy in [far, start_copy] + near_copies + slot_copies(1) + adj_copies:
        copy.wait_send()
    for s in range(slices):
        pl.when(depth != s)(lambda: term_copy(s).wait_send())
    for at in range(1, 4):
        remote(
            terms.at[0], out_ref.at[at // 2, at % 2], 9 + at, term_sem.at[at], (beside, lat)
        ).wait_recv()


def section_terms(offsets, taps, trans, incident, measured, reach):
    slices, band_rows, window = 4, trans.shape[2], trans.shape[3]
    half_band = band_rows // 2
    rows = half_band + 2 * reach
    smem = pl.BlockSpec(memory_space=pltpu.SMEM)
    vmem = pl.BlockSpec(memory_space=pltpu.VMEM)
    hbm = pl.BlockSpec(memory_space=pl.ANY)
    return pl.pallas_call(
        main_kernel,
        out_shape=jax.ShapeDtypeStruct((2, 2, 2, half_band, window), jnp.bfloat16),
        in_specs=[smem, vmem, hbm, hbm, hbm],
        out_specs=vmem,
        scratch_shapes=[
            pltpu.VMEM((2, band_rows, window), jnp.float32),
            pltpu.VMEM((half_band, window), jnp.float32),
            pltpu.VMEM((2, band_rows, window), jnp.bfloat16),
            pltpu.VMEM((2, 2, 2, band_rows + 2 * reach, window), jnp.bfloat16),
            pltpu.VMEM((2, band_rows + 2 * reach, window), jnp.bfloat16),
            pltpu.VMEM((slices, 2, rows, window), jnp.bfloat16),
            pltpu.VMEM((2, rows, window), jnp.bfloat16),
            pltpu.VMEM((slices, 2, half_band, window), jnp.bfloat16),
            pltpu.VMEM((2, 2 * rows, 2 * rows), jnp.bfloat16),
            pltpu.VMEM((2, 768, 256), jnp.bfloat16),
            pltpu.SemaphoreType.DMA((13,)),
            pltpu.SemaphoreType.DMA((4,)),
            pltpu.SemaphoreType.DMA((1,)),
            pltpu.SemaphoreType.DMA((2,)),
            pltpu.SemaphoreType.DMA((2, 2)),
            pltpu.SemaphoreType.DMA((1,)),
            pltpu.SemaphoreType.DMA((2,)),
            pltpu.SemaphoreType.DMA((4,)),
        ],
        compiler_params=pltpu.CompilerParams(
            vmem_limit_bytes=48 * 1024 * 1024, collective_id=0, has_side_effects=True
        ),
    )(offsets, taps, trans, incident, measured)


def place_kernel(offsets, terms_ref, out_ref):
    columns, window = out_ref.shape[3], terms_ref.shape[4]
    half_band = terms_ref.shape[3]
    per_half = half_band // ROW_BLOCK
    depth, lat = lax.axis_index("depth"), lax.axis_index("lat")
    probe, half = depth // 2, lax.rem(depth, 2)
    r = pl.program_id(0)
    core = lax.rem(r // per_half + half, 2)
    rows = pl.ds(pl.multiple_of(ROW_BLOCK * lax.rem(r, per_half), ROW_BLOCK), ROW_BLOCK)
    last = columns // 128 - 1
    lanes = lax.broadcasted_iota(jnp.int32, (ROW_BLOCK, 128), 1)
    out_ref[...] = jnp.zeros_like(out_ref)
    for q in range(2):
        place = lax.rem(probe + q, 2)
        _, layer, col = probe_place(offsets, place, lat, lax.axis_size("lat"), 2 * half_band)
        block, lane = col // 128, lax.rem(col, 128)
        for part in range(2):
            low = jnp.zeros((ROW_BLOCK, 128), jnp.float32)
            for b in range(window // 128 + 1):
                high = jnp.zeros((ROW_BLOCK, 128), jnp.float32)
                if b < window // 128:
                    values = terms_ref[q, core, part, rows, pl.ds(128 * b, 128)]
                    high = pltpu.roll(values.astype(jnp.float32), lane, 1)
                piece = jnp.where(lanes < lane, low, high)
                at = pl.ds(pl.multiple_of(128 * jnp.minimum(block + b, last), 128), 128)
                out_ref[part, layer, :, at] += piece
                low = high


def placed(offsets, terms, columns):
    half_band = terms.shape[3]
    return pl.pallas_call(
        place_kernel,
        out_shape=jax.ShapeDtypeStruct((2, 2, 2 * half_band, columns), jnp.float32),
        grid=(2 * half_band // ROW_BLOCK,),
        in_specs=[
            pl.BlockSpec(memory_space=pltpu.SMEM),
            pl.BlockSpec(terms.shape, lambda r: (0, 0, 0, 0, 0)),
        ],
        out_specs=pl.BlockSpec((2, 2, ROW_BLOCK, columns), lambda r: (0, 0, r, 0)),
    )(offsets, terms)


def local_fast(potential, incident, measured, offsets, kernel):
    reach = 4 * ((kernel.shape[1] - 1) // 2)
    trans = transmissions(offsets, potential, incident.shape[3])
    terms = section_terms(offsets, kernel, trans, incident, measured, reach)
    return placed(offsets, terms, potential.shape[4])[:, None]


def solution(mesh):
    def run(*args):
        potential, incident, _, _, kernel = args
        body = local_fast if fits(mesh, potential.shape, incident.shape, kernel.shape) else local
        in_specs = (
            P(None, "depth", None, "lat", None),
            P(None, None, "lat", None),
            P(None, "lat", None),
            P(),
            P(),
        )
        out_specs = P(None, "depth", None, "lat", None)
        return jax.shard_map(
            body, mesh=mesh, in_specs=in_specs, out_specs=out_specs, check_vma=False
        )(*args)

    return run
```

```python
import functools

import jax
import jax.numpy as jnp
from jax import lax
from jax.experimental import pallas as pl
from jax.experimental.pallas import tpu as pltpu
from jax.sharding import PartitionSpec as P


def with_halo(cells, sides, width):
    for axis, dim in sides:
        count = lax.axis_size(axis)
        head = lax.slice_in_dim(cells, 0, width, axis=dim)
        tail = lax.slice_in_dim(cells, cells.shape[dim] - width, cells.shape[dim], axis=dim)
        cells = jnp.concatenate(
            [
                lax.ppermute(tail, axis, [(i, (i + 1) % count) for i in range(count)]),
                cells,
                lax.ppermute(head, axis, [((i + 1) % count, i) for i in range(count)]),
            ],
            axis=dim,
        )
    return cells


def from_behind(array, axis, by):
    count = lax.axis_size(axis)
    pairs = [(i, i + by) for i in range(count) if 0 <= i + by < count]
    return lax.ppermute(array, axis, pairs)


def rounded(field_in):
    return lax.optimization_barrier(field_in.astype(jnp.bfloat16)).astype(jnp.float32)


def band_matrix(taps_re, taps_im, row_count, col_count, half_width, transposed):
    row_index = lax.broadcasted_iota(jnp.int32, (row_count, col_count), 0)
    col_index = lax.broadcasted_iota(jnp.int32, (row_count, col_count), 1)
    offset = row_index - col_index if transposed else col_index - row_index
    chooser = (offset[:, :, None] == jnp.arange(2 * half_width + 1, dtype=jnp.int32)).astype(
        jnp.float32
    )
    real_part = jnp.sum(chooser * taps_re, axis=2).astype(jnp.bfloat16)
    imag_part = jnp.sum(chooser * taps_im, axis=2).astype(jnp.bfloat16)
    return (real_part, imag_part)


def along_rows(field_in, real_mat, imag_mat):
    direct = jnp.einsum("rq,xpqc->xprc", real_mat, field_in, preferred_element_type=jnp.float32)
    crossed = jnp.einsum("rq,xpqc->xprc", imag_mat, field_in, preferred_element_type=jnp.float32)
    return jnp.stack([direct[0] - crossed[1], crossed[0] + direct[1]])


def along_cols(field_in, real_slab, imag_slab, half_width):
    columns = field_in.shape[-1]
    blocks = columns // 128
    padded = jnp.pad(field_in, ((0, 0), (0, 0), (0, 0), (half_width, 128 - half_width)))
    main_part = padded[..., :columns].reshape(field_in.shape[:-1] + (blocks, 128))
    extra_part = padded[..., 128 : columns + 128].reshape(field_in.shape[:-1] + (blocks, 128))[
        ..., : 2 * half_width
    ]
    slab_rows = jnp.concatenate([main_part, extra_part], axis=-1)
    direct = jnp.einsum("xprbq,qo->xprbo", slab_rows, real_slab, preferred_element_type=jnp.float32)
    crossed = jnp.einsum(
        "xprbq,qo->xprbo", slab_rows, imag_slab, preferred_element_type=jnp.float32
    )
    joined = jnp.stack([direct[0] - crossed[1], crossed[0] + direct[1]])
    return joined.reshape(field_in.shape)


def local(potential, incident, measured, offsets, kernel):
    lat_count = lax.axis_size("lat")
    depth_count = lax.axis_size("depth")
    lat_index = lax.axis_index("lat")
    depth_index = lax.axis_index("depth")
    band_rows = potential.shape[3]
    window = incident.shape[3]
    probe_count = incident.shape[1]
    half_width = (kernel.shape[1] - 1) // 2
    taps_re = kernel[0].astype(jnp.float32)
    taps_im = kernel[1].astype(jnp.float32)
    back_re = taps_re[::-1]
    back_im = -taps_im[::-1]
    row_pixel = offsets[:, 0]
    col_pixel = offsets[:, 1]
    first_band = row_pixel // band_rows
    place_band = (lat_index - first_band) % lat_count
    layer_pot = potential[:, 0]
    reach_steps = 2
    margin = reach_steps * half_width
    full_rows = band_rows + 2 * margin
    most_out = full_rows - 2 * half_width
    row_forward = band_matrix(taps_re, taps_im, most_out, full_rows, half_width, False)
    row_adjoint = band_matrix(back_re, back_im, most_out, full_rows, half_width, False)
    column_forward = band_matrix(taps_re, taps_im, 128 + 2 * half_width, 128, half_width, True)
    column_adjoint = band_matrix(back_re, back_im, 128 + 2 * half_width, 128, half_width, True)
    local_rows = jnp.arange(full_rows, dtype=jnp.int32) - margin
    window_row = place_band[:, None] * band_rows + local_rows[None, :]
    valid_rows = (window_row >= 0) & (window_row < window)
    keep_mask = valid_rows[None, :, :, None]
    padded_pot = with_halo(layer_pot, (("lat", 2),), margin)
    local_rows = jnp.arange(band_rows + 2 * margin, dtype=jnp.int32) - margin
    side_rows = (local_rows >= band_rows).astype(jnp.int32) - (local_rows < 0).astype(jnp.int32)
    halves = jnp.clip(
        (first_band[:, None] + place_band[:, None] + side_rows[None, :]) // lat_count, 0, 1
    )

    def cut_window(col_start):
        return lax.dynamic_slice_in_dim(padded_pot, col_start, window, 3)

    windows = jax.vmap(cut_window)(col_pixel)
    chosen = jnp.where((halves == 0)[:, None, :, None], windows[:, :, 0], windows[:, :, 1])
    damping = jnp.exp(-chosen[:, 1])
    phase_part = chosen[:, 0]
    transmit = jnp.stack([damping * jnp.cos(phase_part), damping * jnp.sin(phase_part)])

    def forward_segment(wave_ext, extent):
        low_row = margin - extent
        rows_in = band_rows + 2 * extent
        rows_out = rows_in - 2 * half_width
        factor = transmit[:, :, low_row : low_row + rows_in]
        inside = keep_mask[:, :, low_row : low_row + rows_in]
        values = wave_ext.astype(jnp.float32)
        product = jnp.stack(
            [
                factor[0] * values[0] - factor[1] * values[1],
                factor[0] * values[1] + factor[1] * values[0],
            ]
        )
        product = jnp.where(inside, product, 0.0).astype(jnp.bfloat16)
        spread = along_rows(
            product, row_forward[0][:rows_out, :rows_in], row_forward[1][:rows_out, :rows_in]
        ).astype(jnp.bfloat16)
        return along_cols(spread, column_forward[0], column_forward[1], half_width).astype(
            jnp.bfloat16
        )

    def backward_segment(adjoint, extent, entry):
        low_row = margin - extent
        rows_in = band_rows + 2 * extent
        rows_out = rows_in - 2 * half_width
        inside = keep_mask[:, :, low_row : low_row + rows_in]
        masked = jnp.where(inside, adjoint, jnp.zeros_like(adjoint))
        spread = along_cols(masked, column_adjoint[0], column_adjoint[1], half_width).astype(
            jnp.bfloat16
        )
        local_grad = rounded(
            along_rows(
                spread, row_adjoint[0][:rows_out, :rows_in], row_adjoint[1][:rows_out, :rows_in]
            )
        )
        factor = transmit[:, :, low_row + half_width : low_row + half_width + rows_out]
        earlier = jnp.stack(
            [
                factor[0] * local_grad[0] + factor[1] * local_grad[1],
                factor[0] * local_grad[1] - factor[1] * local_grad[0],
            ]
        ).astype(jnp.bfloat16)
        centre = extent - half_width
        own_rows = local_grad[:, :, centre : centre + band_rows]
        own_factor = factor[:, :, centre : centre + band_rows]
        entry_wave = entry.astype(jnp.float32)
        cross_re = entry_wave[0] * own_rows[0] + entry_wave[1] * own_rows[1]
        cross_im = entry_wave[0] * own_rows[1] - entry_wave[1] * own_rows[0]
        turned_re = own_factor[0] * cross_re + own_factor[1] * cross_im
        turned_im = own_factor[0] * cross_im - own_factor[1] * cross_re
        return (earlier, jnp.stack([turned_im, -turned_re]))

    start_wave = incident.astype(jnp.bfloat16)
    zeros_wave = jnp.zeros_like(start_wave)
    blocks = depth_count // reach_steps

    def forward_block(block_index, carry):
        moving, stored, leaving = carry
        entering = jnp.where(depth_index == 0, start_wave, moving)
        wave_ext = with_halo(entering, (("lat", 2),), margin)
        for sub_step in range(reach_steps):
            extent = margin - sub_step * half_width
            result = forward_segment(wave_ext, extent)
            active = depth_index == block_index * reach_steps + sub_step
            stored = jnp.where(active, wave_ext[:, :, extent : extent + band_rows], stored)
            if sub_step == reach_steps - 1:
                leaving = jnp.where(active, result, leaving)
            wave_ext = from_behind(result, "depth", 1)
        return (wave_ext, stored, leaving)

    moving, stored, leaving = lax.fori_loop(
        0, blocks, forward_block, (zeros_wave, zeros_wave, zeros_wave)
    )
    exit_vals = leaving.astype(jnp.float32)
    residual = exit_vals[0] * exit_vals[0] + exit_vals[1] * exit_vals[1] - measured
    seed_wave = (2.0 * residual[None] * exit_vals).astype(jnp.bfloat16)
    zeros_term = jnp.zeros(start_wave.shape, jnp.float32)

    def backward_block(block_index, carry):
        moving_back, collected = carry
        entering = jnp.where(depth_index == depth_count - 1, seed_wave, moving_back)
        adjoint = with_halo(entering, (("lat", 2),), margin)
        for sub_step in range(reach_steps):
            extent = margin - sub_step * half_width
            earlier, grad_term = backward_segment(adjoint, extent, stored)
            active = depth_index == depth_count - 1 - (block_index * reach_steps + sub_step)
            collected = jnp.where(active, grad_term, collected)
            adjoint = from_behind(earlier, "depth", -1)
        return (adjoint, collected)

    moving_back, gathered = lax.fori_loop(0, blocks, backward_block, (zeros_wave, zeros_term))
    own_half = (first_band + place_band) // lat_count
    gradient = jnp.zeros_like(layer_pot)

    def accumulate(probe_index, running):
        portion = lax.dynamic_index_in_dim(gathered, probe_index, 1, keepdims=False)
        zero_index = jnp.zeros((), jnp.int32)
        corner = (zero_index, own_half[probe_index], zero_index, col_pixel[probe_index])
        current = lax.dynamic_slice(running, corner, (2, 1, band_rows, window))
        return lax.dynamic_update_slice(running, current + portion[:, None], corner)

    gradient = lax.fori_loop(0, probe_count, accumulate, gradient)
    return gradient[:, None]


ROW_BLOCK = 32


def fits(mesh, potential_shape, incident_shape, kernel_shape):
    depth_count, lat_count = mesh.shape["depth"], mesh.shape["lat"]
    slices, window, columns = potential_shape[1], incident_shape[3], potential_shape[4]
    half_width = (kernel_shape[1] - 1) // 2
    if incident_shape[1] != 2 or depth_count != 4 or slices != 4:
        return False
    half_band = potential_shape[3] // lat_count // 2
    reach = slices * half_width
    return (
        half_width <= 8
        and 2 * reach <= half_band
        and reach % 16 == 0
        and half_band % ROW_BLOCK == 0
        and window % 256 == 0
        and 8 * half_width <= 128
        and columns == 2 * window
    )


def series(square, divisors):
    total = 1.0 / divisors[-1]
    for divisor in divisors[-2::-1]:
        total = total * square + 1.0 / divisor
    return total


def probe_place(offsets, probe, lat, lat_count, band_rows):
    first_band = offsets[probe, 0] // band_rows
    place_band = lax.rem(lat - first_band + lat_count, lat_count)
    return place_band, (first_band + place_band) // lat_count, offsets[probe, 1]


def write_transmission(pot, layer, col, row, dst, dst_row):
    window = dst.shape[2]
    last = pot.shape[3] // 128 - 1
    block, lane = col // 128, lax.rem(col, 128)
    turn_by = lax.rem(128 - lane, 128)
    here = lax.broadcasted_iota(jnp.int32, (ROW_BLOCK, 128), 1) < 128 - lane
    rows = pl.ds(row, ROW_BLOCK)

    def turned(b):
        at = pl.multiple_of(128 * jnp.minimum(block + b, last), 128)
        return [pltpu.roll(pot[k, layer, rows, pl.ds(at, 128)], turn_by, 1) for k in range(2)]

    low = turned(0)
    for b in range(window // 128):
        high = turned(b + 1)
        phase, absorb = [jnp.where(here, low[k], high[k]) for k in range(2)]
        damping = jnp.exp(-absorb)
        turn = 0.5 * phase
        square = turn * turn
        sine = turn * series(square, (1, -6, 120, -5040, 362880, -39916800, 6227020800))
        cosine = series(square, (1, -2, 24, -720, 40320, -3628800, 479001600))
        at = pl.ds(128 * b, 128)
        out_rows = pl.ds(dst_row, ROW_BLOCK)
        dst[0, out_rows, at] = (damping * (1.0 - 2.0 * sine * sine)).astype(dst.dtype)
        dst[1, out_rows, at] = (2.0 * damping * sine * cosine).astype(dst.dtype)
        low = high


def transmission_kernel(offsets, pot_ref, out_ref):
    depth, lat = lax.axis_index("depth"), lax.axis_index("lat")
    band_rows = ROW_BLOCK * pl.num_programs(0)
    for q in range(2):
        place = lax.rem(depth // 2 + q, 2)
        _, layer, col = probe_place(offsets, place, lat, lax.axis_size("lat"), band_rows)
        write_transmission(pot_ref, layer, col, 0, out_ref.at[q], 0)


def transmissions(offsets, potential, window):
    band_rows, columns = potential.shape[3:]
    return pl.pallas_call(
        transmission_kernel,
        out_shape=jax.ShapeDtypeStruct((2, 2, band_rows, window), jnp.bfloat16),
        grid=(band_rows // ROW_BLOCK,),
        in_specs=[
            pl.BlockSpec(memory_space=pltpu.SMEM),
            pl.BlockSpec((2, 2, ROW_BLOCK, columns), lambda r: (0, 0, r, 0)),
        ],
        out_specs=pl.BlockSpec((2, 2, ROW_BLOCK, window), lambda r: (0, 0, r, 0)),
    )(offsets, potential[:, 0])


def band(taps, rows, cols, start, half_width):
    offset = (
        lax.broadcasted_iota(jnp.int32, (rows, cols), 0)
        - lax.broadcasted_iota(jnp.int32, (rows, cols), 1)
        - start
        + half_width
    )
    total = jnp.zeros((rows, cols), jnp.float32)
    for tap_index, tap in enumerate(taps):
        total = jnp.where(offset == tap_index, tap, total)
    return total


def main_kernel(
    offsets, taps_ref, trans_hbm, incident_hbm, measured_hbm, out_ref,
    incident, measured, far_t, t_all, start, waves, adj, terms, row_mat, col_mat,
    send_sem, load_sem, far_sem, beside_sem, edge_sem, start_sem, adj_sem, term_sem,
):
    slices, _, rows, width = waves.shape
    window = incident.shape[2]
    share = window // 2
    tap_count = taps_ref.shape[1]
    half_width = (tap_count - 1) // 2
    band_rows = far_t.shape[1]
    half_band = band_rows // 2
    reach = (rows - half_band) // 2
    blocks = width // 128
    depth, lat = lax.axis_index("depth"), lax.axis_index("lat")
    lat_count = lax.axis_size("lat")
    probe, half = depth // 2, lax.rem(depth, 2)
    other_half = 1 - half
    beside = 2 * probe + other_half
    across = 2 * (1 - probe) + half
    before, after = lax.rem(lat + lat_count - 1, lat_count), lax.rem(lat + 1, lat_count)
    near = lax.rem(lat + 2 * half + lat_count - 1, lat_count)

    def remote(src, dst, send, recv, to):
        return pltpu.make_async_remote_copy(
            src_ref=src,
            dst_ref=dst,
            send_sem=send_sem.at[send],
            recv_sem=recv,
            device_id=to,
            device_id_type=pl.DeviceIdType.MESH,
        )

    own_rows = pl.ds(pl.multiple_of(half_band * half, 16), half_band)
    loads = [
        pltpu.make_async_copy(src, dst, load_sem.at[i])
        for i, (src, dst) in enumerate(
            [
                (trans_hbm.at[1], far_t),
                (trans_hbm.at[0], t_all.at[0, 0, :, pl.ds(reach, band_rows)]),
                (incident_hbm.at[:, probe], incident),
                (measured_hbm.at[probe, own_rows], measured),
            ]
        )
    ]
    for load in loads:
        load.start()

    barrier = pltpu.get_barrier_semaphore()
    senders = [
        (beside, lat),
        (across, lat),
        (2 * (1 - probe) + other_half, lat),
        (2 * probe, near),
        (2 * probe + 1, near),
    ]
    for to in senders:
        pl.semaphore_signal(
            barrier, inc=1, device_id=to, device_id_type=pl.DeviceIdType.MESH
        )
    pl.semaphore_wait(barrier, len(senders))

    inner = pl.ds(reach, band_rows)
    place_row = band_rows * lat
    at_row = offsets[probe, 0]
    at_top = (at_row == place_row) | (at_row == place_row + window)
    at_bottom = (at_row == place_row + band_rows) | (at_row == place_row + band_rows - window)
    top_ok = jnp.logical_not(at_top) | (half == 1)
    bottom_ok = jnp.logical_not(at_bottom) | (half == 0)

    fresh = [pl.ds(0, width), pl.ds(width, window - width)]
    first = [0, window - width]
    far = [
        remote(
            far_t.at[:, :, cols], t_all.at[0, 1, :, inner, cols],
            13 + n, far_sem.at[n], (across, lat),
        )
        for n, cols in enumerate(fresh)
    ]
    loads[0].wait()
    far[0].start()
    loads[2].wait()
    start[:, inner] = incident[...].astype(jnp.bfloat16)
    loads[1].wait()

    shared = pl.ds(pl.multiple_of(reach + (half_band - reach) * other_half, 16), half_band + reach)
    edge_rows = pl.ds(pl.multiple_of((band_rows + reach) * half, 16), reach)
    tail, head = pl.ds(band_rows, reach), pl.ds(reach, reach)
    low, high = pl.ds(0, reach), pl.ds(band_rows + reach, reach)

    groups = [(0, pl.ds(0, window)), (1, fresh[0]), (1, fresh[1])]

    def slot_copies(group):
        side, cols = groups[group]
        return [
            remote(
                t_all.at[0, side, :, shared, cols], t_all.at[1, side, :, shared, cols],
                3 * group, beside_sem.at[group], (beside, lat),
            ),
            remote(
                t_all.at[0, side, :, tail, cols], t_all.at[half, side, :, low, cols],
                3 * group + 1, edge_sem.at[half, group], (2 * probe, after),
            ),
            remote(
                t_all.at[0, side, :, head, cols], t_all.at[other_half, side, :, high, cols],
                3 * group + 2, edge_sem.at[other_half, group], (2 * probe + 1, before),
            ),
        ]

    def finish_slot(group):
        side, cols = groups[group]
        slot_copies(group)[0].wait_recv()
        for core in range(2):
            remote(
                t_all.at[0, side, :, tail, cols], t_all.at[core, side, :, edge_rows, cols],
                3 * group + 1, edge_sem.at[core, group], (beside, lat),
            ).wait_recv()
            edge = t_all[core, side, :, edge_rows, cols]
            t_all[core, side, :, edge_rows, cols] = jnp.where(
                top_ok & bottom_ok, edge, jnp.zeros_like(edge)
            )

    start_rows = pl.ds(pl.multiple_of(reach + (band_rows - reach) * other_half, 16), reach)
    toward = lax.rem(lat + 1 - 2 * half + lat_count, lat_count)
    start_copy = remote(
        start.at[:, start_rows], start.at[:, edge_rows], 9, start_sem.at[0], (depth, toward)
    )
    near_copies = slot_copies(0)
    for copy in [start_copy] + near_copies:
        copy.start()

    taps = taps_ref[...].astype(jnp.float32)
    re = [taps[0:1, i : i + 1] for i in range(tap_count)]
    im = [taps[1:2, i : i + 1] for i in range(tap_count)]
    ways = ((re, im), (re[::-1], [-tap for tap in im[::-1]]))
    for way, (tap_re, tap_im) in enumerate(ways):
        real = band(tap_re[::-1], rows, rows, 0, half_width)
        imag = band(tap_im[::-1], rows, rows, 0, half_width)
        row_mat[way] = jnp.concatenate(
            [
                jnp.concatenate([real, -imag], axis=1),
                jnp.concatenate([imag, real], axis=1),
            ],
            axis=0,
        ).astype(jnp.bfloat16)
        real = band(tap_re, 384, 128, 128, half_width)
        imag = band(tap_im, 384, 128, 128, half_width)
        col_mat[way, :384, :128] = real.astype(jnp.bfloat16)
        col_mat[way, :384, 128:] = imag.astype(jnp.bfloat16)
        col_mat[way, 384:, :128] = (-imag).astype(jnp.bfloat16)
        col_mat[way, 384:, 128:] = real.astype(jnp.bfloat16)

    def rows_conv(field, way):
        return jnp.dot(row_mat[way], field, preferred_element_type=jnp.float32).astype(
            jnp.bfloat16
        )

    def cols_conv(field, way):
        edge = jnp.zeros((rows, 128), jnp.bfloat16)
        padded = [
            jnp.concatenate([edge, field[k * rows : (k + 1) * rows], edge], axis=1)
            for k in range(2)
        ]
        slabs = jnp.concatenate(
            [
                jnp.concatenate([part[:, 128 * b : 128 * b + 384] for part in padded], axis=1)
                for b in range(blocks)
            ],
            axis=0,
        )
        out = jnp.dot(slabs, col_mat[way], preferred_element_type=jnp.float32)
        out = out.astype(jnp.bfloat16)
        return [
            jnp.concatenate(
                [out[b * rows : (b + 1) * rows, 128 * k : 128 * k + 128] for b in range(blocks)],
                axis=1,
            )
            for k in range(2)
        ]

    extent = pl.ds(pl.multiple_of(half_band * half, 16), rows)

    def place_of(s):
        return lax.rem(s % 2 + half, 2), lax.rem(s // 2 + probe, 2)

    def factor(s, cols):
        core, side = place_of(s)
        both = t_all[core, side, :, extent, cols].astype(jnp.float32)
        return both[0], both[1]

    def term_copy(n, s):
        core, side = place_of(s)
        at = 2 * side + core
        cols = pl.ds(share * n, share)
        return remote(
            terms.at[s, :, :, cols], out_ref.at[side, core, :, :, cols],
            15 + 4 * n + at, term_sem.at[n, at], (s, lat),
        )

    def adjoint_copies(n):
        return [
            remote(
                adj.at[n, :, pl.ds(reach, reach)], adj.at[n, :, pl.ds(rows - reach, reach)],
                23 + n, adj_sem.at[n, 1], (beside, up_lat),
            ),
            remote(
                adj.at[n, :, pl.ds(rows - 2 * reach, reach)], adj.at[n, :, pl.ds(0, reach)],
                25 + n, adj_sem.at[n, 0], (beside, down_lat),
            ),
        ]

    up_lat = lax.rem(lat + half + lat_count - 1, lat_count)
    down_lat = lax.rem(lat + half, lat_count)
    own = slice(reach, rows - reach)
    far[0].wait_send()
    far[1].start()
    far[0].wait_recv()
    for copy in slot_copies(1):
        copy.start()
    start_copy.wait_recv()
    finish_slot(0)

    for n in range(2):
        cols = pl.ds(first[n], width)
        if n == 0:
            pl.when(probe == 1)(lambda: finish_slot(1))
        else:
            finish_slot(2)
        waves[0] = start[:, extent, cols]
        wave = None
        for s in range(slices):
            if s == slices // 2 and n == 0:
                pl.when(probe == 0)(lambda: finish_slot(1))
            t_re, t_im = factor(s, cols)
            w_re, w_im = waves[s, 0].astype(jnp.float32), waves[s, 1].astype(jnp.float32)
            product = jnp.concatenate(
                [t_re * w_re - t_im * w_im, t_re * w_im + t_im * w_re], axis=0
            )
            wave = cols_conv(rows_conv(product.astype(jnp.bfloat16), 0), 0)
            if s + 1 < slices:
                waves[s + 1, 0], waves[s + 1, 1] = wave

        w_re, w_im = [part[own].astype(jnp.float32) for part in wave]
        if n == 0:
            loads[3].wait()
        residual = 2.0 * (w_re * w_re + w_im * w_im - measured[:, cols])
        adj[n, 0, own] = (residual * w_re).astype(jnp.bfloat16)
        adj[n, 1, own] = (residual * w_im).astype(jnp.bfloat16)
        for copy in adjoint_copies(n):
            copy.start()
        if n == 0:
            far[1].wait_recv()
            for copy in slot_copies(2):
                copy.start()
        for copy in adjoint_copies(n):
            copy.wait_recv()
        adjoint = []
        for k in range(2):
            top, bottom = adj[n, k, :reach], adj[n, k, rows - reach :]
            adjoint.append(
                jnp.concatenate(
                    [
                        jnp.where(top_ok, top, jnp.zeros_like(top)),
                        adj[n, k, own],
                        jnp.where(bottom_ok, bottom, jnp.zeros_like(bottom)),
                    ],
                    axis=0,
                )
            )

        mine = slice(share * n - first[n], share * n - first[n] + share)
        kept = slice(share * n, share * n + share)
        for s in reversed(range(slices)):
            spread = cols_conv(jnp.concatenate(adjoint, axis=0), 1)
            grad = rows_conv(jnp.concatenate(spread, axis=0), 1).astype(jnp.float32)
            g_re, g_im = grad[:rows], grad[rows:]
            t_re, t_im = factor(s, cols)
            back_re = t_re * g_re + t_im * g_im
            back_im = t_re * g_im - t_im * g_re
            b_re, b_im = back_re[own, mine], back_im[own, mine]
            e_re = waves[s, 0, own, mine].astype(jnp.float32)
            e_im = waves[s, 1, own, mine].astype(jnp.float32)
            terms[s, 0, :, kept] = (e_re * b_im - e_im * b_re).astype(jnp.bfloat16)
            terms[s, 1, :, kept] = (-e_re * b_re - e_im * b_im).astype(jnp.bfloat16)
            pl.when(depth != s)(lambda: term_copy(n, s).start())

            @pl.when(depth == s)
            def _():
                out_ref[0, 0, :, :, kept] = terms[s, :, :, kept]

            adjoint = [back_re.astype(jnp.bfloat16), back_im.astype(jnp.bfloat16)]

    for copy in [far[1], start_copy] + near_copies + slot_copies(1) + slot_copies(2):
        copy.wait_send()
    for n in range(2):
        for copy in adjoint_copies(n):
            copy.wait_send()
        for s in range(slices):
            pl.when(depth != s)(lambda: term_copy(n, s).wait_send())
        cols = pl.ds(share * n, share)
        for at in range(1, 4):
            remote(
                terms.at[0, :, :, cols], out_ref.at[at // 2, at % 2, :, :, cols],
                15 + 4 * n + at, term_sem.at[n, at], (beside, lat),
            ).wait_recv()


def section_terms(offsets, taps, trans, incident, measured, reach):
    slices, band_rows, window = 4, trans.shape[2], trans.shape[3]
    half_band = band_rows // 2
    rows = half_band + 2 * reach
    width = window // 2 + 128
    smem = pl.BlockSpec(memory_space=pltpu.SMEM)
    vmem = pl.BlockSpec(memory_space=pltpu.VMEM)
    hbm = pl.BlockSpec(memory_space=pl.ANY)
    return pl.pallas_call(
        main_kernel,
        out_shape=jax.ShapeDtypeStruct((2, 2, 2, half_band, window), jnp.bfloat16),
        in_specs=[smem, vmem, hbm, hbm, hbm],
        out_specs=vmem,
        scratch_shapes=[
            pltpu.VMEM((2, band_rows, window), jnp.float32),
            pltpu.VMEM((half_band, window), jnp.float32),
            pltpu.VMEM((2, band_rows, window), jnp.bfloat16),
            pltpu.VMEM((2, 2, 2, band_rows + 2 * reach, window), jnp.bfloat16),
            pltpu.VMEM((2, band_rows + 2 * reach, window), jnp.bfloat16),
            pltpu.VMEM((slices, 2, rows, width), jnp.bfloat16),
            pltpu.VMEM((2, 2, rows, width), jnp.bfloat16),
            pltpu.VMEM((slices, 2, half_band, window), jnp.bfloat16),
            pltpu.VMEM((2, 2 * rows, 2 * rows), jnp.bfloat16),
            pltpu.VMEM((2, 768, 256), jnp.bfloat16),
            pltpu.SemaphoreType.DMA((27,)),
            pltpu.SemaphoreType.DMA((4,)),
            pltpu.SemaphoreType.DMA((2,)),
            pltpu.SemaphoreType.DMA((3,)),
            pltpu.SemaphoreType.DMA((2, 3)),
            pltpu.SemaphoreType.DMA((1,)),
            pltpu.SemaphoreType.DMA((2, 2)),
            pltpu.SemaphoreType.DMA((2, 4)),
        ],
        compiler_params=pltpu.CompilerParams(
            vmem_limit_bytes=60 * 1024 * 1024, collective_id=0, has_side_effects=True
        ),
    )(offsets, taps, trans, incident, measured)


def place_kernel(offsets, terms_ref, out_ref):
    columns, window = out_ref.shape[3], terms_ref.shape[4]
    half_band = terms_ref.shape[3]
    per_half = half_band // ROW_BLOCK
    depth, lat = lax.axis_index("depth"), lax.axis_index("lat")
    probe, half = depth // 2, lax.rem(depth, 2)
    r = pl.program_id(0)
    core = lax.rem(r // per_half + half, 2)
    rows = pl.ds(pl.multiple_of(ROW_BLOCK * lax.rem(r, per_half), ROW_BLOCK), ROW_BLOCK)
    last = columns // 128 - 1
    lanes = lax.broadcasted_iota(jnp.int32, (ROW_BLOCK, 128), 1)
    out_ref[...] = jnp.zeros_like(out_ref)
    for q in range(2):
        place = lax.rem(probe + q, 2)
        _, layer, col = probe_place(offsets, place, lat, lax.axis_size("lat"), 2 * half_band)
        block, lane = col // 128, lax.rem(col, 128)
        for part in range(2):
            low = jnp.zeros((ROW_BLOCK, 128), jnp.float32)
            for b in range(window // 128 + 1):
                high = jnp.zeros((ROW_BLOCK, 128), jnp.float32)
                if b < window // 128:
                    values = terms_ref[q, core, part, rows, pl.ds(128 * b, 128)]
                    high = pltpu.roll(values.astype(jnp.float32), lane, 1)
                piece = jnp.where(lanes < lane, low, high)
                at = pl.ds(pl.multiple_of(128 * jnp.minimum(block + b, last), 128), 128)
                out_ref[part, layer, :, at] += piece
                low = high


def placed(offsets, terms, columns):
    half_band = terms.shape[3]
    return pl.pallas_call(
        place_kernel,
        out_shape=jax.ShapeDtypeStruct((2, 2, 2 * half_band, columns), jnp.float32),
        grid=(2 * half_band // ROW_BLOCK,),
        in_specs=[
            pl.BlockSpec(memory_space=pltpu.SMEM),
            pl.BlockSpec(terms.shape, lambda r: (0, 0, 0, 0, 0)),
        ],
        out_specs=pl.BlockSpec((2, 2, ROW_BLOCK, columns), lambda r: (0, 0, r, 0)),
    )(offsets, terms)


def local_fast(potential, incident, measured, offsets, kernel):
    reach = 4 * ((kernel.shape[1] - 1) // 2)
    trans = transmissions(offsets, potential, incident.shape[3])
    terms = section_terms(offsets, kernel, trans, incident, measured, reach)
    return placed(offsets, terms, potential.shape[4])[:, None]


def solution(mesh):
    def run(*args):
        potential, incident, _, _, kernel = args
        body = local_fast if fits(mesh, potential.shape, incident.shape, kernel.shape) else local
        in_specs = (
            P(None, "depth", None, "lat", None),
            P(None, None, "lat", None),
            P(None, "lat", None),
            P(),
            P(),
        )
        out_specs = P(None, "depth", None, "lat", None)
        return jax.shard_map(
            body, mesh=mesh, in_specs=in_specs, out_specs=out_specs, check_vma=False
        )(*args)

    return run
```

```python
import functools

import jax
import jax.numpy as jnp
from jax import lax
from jax.experimental import pallas as pl
from jax.experimental.pallas import tpu as pltpu
from jax.sharding import PartitionSpec as P


def with_halo(cells, sides, width):
    for axis, dim in sides:
        count = lax.axis_size(axis)
        head = lax.slice_in_dim(cells, 0, width, axis=dim)
        tail = lax.slice_in_dim(cells, cells.shape[dim] - width, cells.shape[dim], axis=dim)
        cells = jnp.concatenate(
            [
                lax.ppermute(tail, axis, [(i, (i + 1) % count) for i in range(count)]),
                cells,
                lax.ppermute(head, axis, [((i + 1) % count, i) for i in range(count)]),
            ],
            axis=dim,
        )
    return cells


def from_behind(array, axis, by):
    count = lax.axis_size(axis)
    pairs = [(i, i + by) for i in range(count) if 0 <= i + by < count]
    return lax.ppermute(array, axis, pairs)


def rounded(field_in):
    return lax.optimization_barrier(field_in.astype(jnp.bfloat16)).astype(jnp.float32)


def band_matrix(taps_re, taps_im, row_count, col_count, half_width, transposed):
    row_index = lax.broadcasted_iota(jnp.int32, (row_count, col_count), 0)
    col_index = lax.broadcasted_iota(jnp.int32, (row_count, col_count), 1)
    offset = row_index - col_index if transposed else col_index - row_index
    chooser = (offset[:, :, None] == jnp.arange(2 * half_width + 1, dtype=jnp.int32)).astype(
        jnp.float32
    )
    real_part = jnp.sum(chooser * taps_re, axis=2).astype(jnp.bfloat16)
    imag_part = jnp.sum(chooser * taps_im, axis=2).astype(jnp.bfloat16)
    return (real_part, imag_part)


def along_rows(field_in, real_mat, imag_mat):
    direct = jnp.einsum("rq,xpqc->xprc", real_mat, field_in, preferred_element_type=jnp.float32)
    crossed = jnp.einsum("rq,xpqc->xprc", imag_mat, field_in, preferred_element_type=jnp.float32)
    return jnp.stack([direct[0] - crossed[1], crossed[0] + direct[1]])


def along_cols(field_in, real_slab, imag_slab, half_width):
    columns = field_in.shape[-1]
    blocks = columns // 128
    padded = jnp.pad(field_in, ((0, 0), (0, 0), (0, 0), (half_width, 128 - half_width)))
    main_part = padded[..., :columns].reshape(field_in.shape[:-1] + (blocks, 128))
    extra_part = padded[..., 128 : columns + 128].reshape(field_in.shape[:-1] + (blocks, 128))[
        ..., : 2 * half_width
    ]
    slab_rows = jnp.concatenate([main_part, extra_part], axis=-1)
    direct = jnp.einsum("xprbq,qo->xprbo", slab_rows, real_slab, preferred_element_type=jnp.float32)
    crossed = jnp.einsum(
        "xprbq,qo->xprbo", slab_rows, imag_slab, preferred_element_type=jnp.float32
    )
    joined = jnp.stack([direct[0] - crossed[1], crossed[0] + direct[1]])
    return joined.reshape(field_in.shape)


def local(potential, incident, measured, offsets, kernel):
    lat_count = lax.axis_size("lat")
    depth_count = lax.axis_size("depth")
    lat_index = lax.axis_index("lat")
    depth_index = lax.axis_index("depth")
    band_rows = potential.shape[3]
    window = incident.shape[3]
    probe_count = incident.shape[1]
    half_width = (kernel.shape[1] - 1) // 2
    taps_re = kernel[0].astype(jnp.float32)
    taps_im = kernel[1].astype(jnp.float32)
    back_re = taps_re[::-1]
    back_im = -taps_im[::-1]
    row_pixel = offsets[:, 0]
    col_pixel = offsets[:, 1]
    first_band = row_pixel // band_rows
    place_band = (lat_index - first_band) % lat_count
    layer_pot = potential[:, 0]
    reach_steps = 2
    margin = reach_steps * half_width
    full_rows = band_rows + 2 * margin
    most_out = full_rows - 2 * half_width
    row_forward = band_matrix(taps_re, taps_im, most_out, full_rows, half_width, False)
    row_adjoint = band_matrix(back_re, back_im, most_out, full_rows, half_width, False)
    column_forward = band_matrix(taps_re, taps_im, 128 + 2 * half_width, 128, half_width, True)
    column_adjoint = band_matrix(back_re, back_im, 128 + 2 * half_width, 128, half_width, True)
    local_rows = jnp.arange(full_rows, dtype=jnp.int32) - margin
    window_row = place_band[:, None] * band_rows + local_rows[None, :]
    valid_rows = (window_row >= 0) & (window_row < window)
    keep_mask = valid_rows[None, :, :, None]
    padded_pot = with_halo(layer_pot, (("lat", 2),), margin)
    local_rows = jnp.arange(band_rows + 2 * margin, dtype=jnp.int32) - margin
    side_rows = (local_rows >= band_rows).astype(jnp.int32) - (local_rows < 0).astype(jnp.int32)
    halves = jnp.clip(
        (first_band[:, None] + place_band[:, None] + side_rows[None, :]) // lat_count, 0, 1
    )

    def cut_window(col_start):
        return lax.dynamic_slice_in_dim(padded_pot, col_start, window, 3)

    windows = jax.vmap(cut_window)(col_pixel)
    chosen = jnp.where((halves == 0)[:, None, :, None], windows[:, :, 0], windows[:, :, 1])
    damping = jnp.exp(-chosen[:, 1])
    phase_part = chosen[:, 0]
    transmit = jnp.stack([damping * jnp.cos(phase_part), damping * jnp.sin(phase_part)])

    def forward_segment(wave_ext, extent):
        low_row = margin - extent
        rows_in = band_rows + 2 * extent
        rows_out = rows_in - 2 * half_width
        factor = transmit[:, :, low_row : low_row + rows_in]
        inside = keep_mask[:, :, low_row : low_row + rows_in]
        values = wave_ext.astype(jnp.float32)
        product = jnp.stack(
            [
                factor[0] * values[0] - factor[1] * values[1],
                factor[0] * values[1] + factor[1] * values[0],
            ]
        )
        product = jnp.where(inside, product, 0.0).astype(jnp.bfloat16)
        spread = along_rows(
            product, row_forward[0][:rows_out, :rows_in], row_forward[1][:rows_out, :rows_in]
        ).astype(jnp.bfloat16)
        return along_cols(spread, column_forward[0], column_forward[1], half_width).astype(
            jnp.bfloat16
        )

    def backward_segment(adjoint, extent, entry):
        low_row = margin - extent
        rows_in = band_rows + 2 * extent
        rows_out = rows_in - 2 * half_width
        inside = keep_mask[:, :, low_row : low_row + rows_in]
        masked = jnp.where(inside, adjoint, jnp.zeros_like(adjoint))
        spread = along_cols(masked, column_adjoint[0], column_adjoint[1], half_width).astype(
            jnp.bfloat16
        )
        local_grad = rounded(
            along_rows(
                spread, row_adjoint[0][:rows_out, :rows_in], row_adjoint[1][:rows_out, :rows_in]
            )
        )
        factor = transmit[:, :, low_row + half_width : low_row + half_width + rows_out]
        earlier = jnp.stack(
            [
                factor[0] * local_grad[0] + factor[1] * local_grad[1],
                factor[0] * local_grad[1] - factor[1] * local_grad[0],
            ]
        ).astype(jnp.bfloat16)
        centre = extent - half_width
        own_rows = local_grad[:, :, centre : centre + band_rows]
        own_factor = factor[:, :, centre : centre + band_rows]
        entry_wave = entry.astype(jnp.float32)
        cross_re = entry_wave[0] * own_rows[0] + entry_wave[1] * own_rows[1]
        cross_im = entry_wave[0] * own_rows[1] - entry_wave[1] * own_rows[0]
        turned_re = own_factor[0] * cross_re + own_factor[1] * cross_im
        turned_im = own_factor[0] * cross_im - own_factor[1] * cross_re
        return (earlier, jnp.stack([turned_im, -turned_re]))

    start_wave = incident.astype(jnp.bfloat16)
    zeros_wave = jnp.zeros_like(start_wave)
    blocks = depth_count // reach_steps

    def forward_block(block_index, carry):
        moving, stored, leaving = carry
        entering = jnp.where(depth_index == 0, start_wave, moving)
        wave_ext = with_halo(entering, (("lat", 2),), margin)
        for sub_step in range(reach_steps):
            extent = margin - sub_step * half_width
            result = forward_segment(wave_ext, extent)
            active = depth_index == block_index * reach_steps + sub_step
            stored = jnp.where(active, wave_ext[:, :, extent : extent + band_rows], stored)
            if sub_step == reach_steps - 1:
                leaving = jnp.where(active, result, leaving)
            wave_ext = from_behind(result, "depth", 1)
        return (wave_ext, stored, leaving)

    moving, stored, leaving = lax.fori_loop(
        0, blocks, forward_block, (zeros_wave, zeros_wave, zeros_wave)
    )
    exit_vals = leaving.astype(jnp.float32)
    residual = exit_vals[0] * exit_vals[0] + exit_vals[1] * exit_vals[1] - measured
    seed_wave = (2.0 * residual[None] * exit_vals).astype(jnp.bfloat16)
    zeros_term = jnp.zeros(start_wave.shape, jnp.float32)

    def backward_block(block_index, carry):
        moving_back, collected = carry
        entering = jnp.where(depth_index == depth_count - 1, seed_wave, moving_back)
        adjoint = with_halo(entering, (("lat", 2),), margin)
        for sub_step in range(reach_steps):
            extent = margin - sub_step * half_width
            earlier, grad_term = backward_segment(adjoint, extent, stored)
            active = depth_index == depth_count - 1 - (block_index * reach_steps + sub_step)
            collected = jnp.where(active, grad_term, collected)
            adjoint = from_behind(earlier, "depth", -1)
        return (adjoint, collected)

    moving_back, gathered = lax.fori_loop(0, blocks, backward_block, (zeros_wave, zeros_term))
    own_half = (first_band + place_band) // lat_count
    gradient = jnp.zeros_like(layer_pot)

    def accumulate(probe_index, running):
        portion = lax.dynamic_index_in_dim(gathered, probe_index, 1, keepdims=False)
        zero_index = jnp.zeros((), jnp.int32)
        corner = (zero_index, own_half[probe_index], zero_index, col_pixel[probe_index])
        current = lax.dynamic_slice(running, corner, (2, 1, band_rows, window))
        return lax.dynamic_update_slice(running, current + portion[:, None], corner)

    gradient = lax.fori_loop(0, probe_count, accumulate, gradient)
    return gradient[:, None]


ROW_BLOCK = 32


def fits(mesh, potential_shape, incident_shape, kernel_shape):
    depth_count, lat_count = mesh.shape["depth"], mesh.shape["lat"]
    slices, window, columns = potential_shape[1], incident_shape[3], potential_shape[4]
    half_width = (kernel_shape[1] - 1) // 2
    if incident_shape[1] != 2 or depth_count != 4 or slices != 4:
        return False
    half_band = potential_shape[3] // lat_count // 2
    reach = slices * half_width
    return (
        half_width <= 8
        and 2 * reach <= half_band
        and reach % 16 == 0
        and half_band % ROW_BLOCK == 0
        and window % 256 == 0
        and 8 * half_width <= 128
        and columns == 2 * window
    )


def series(square, divisors):
    total = 1.0 / divisors[-1]
    for divisor in divisors[-2::-1]:
        total = total * square + 1.0 / divisor
    return total


def probe_place(offsets, probe, lat, lat_count, band_rows):
    first_band = offsets[probe, 0] // band_rows
    place_band = lax.rem(lat - first_band + lat_count, lat_count)
    return place_band, (first_band + place_band) // lat_count, offsets[probe, 1]


def write_transmission(pot, layer, col, row, dst, dst_row):
    window = dst.shape[2]
    last = pot.shape[3] // 128 - 1
    block, lane = col // 128, lax.rem(col, 128)
    turn_by = lax.rem(128 - lane, 128)
    here = lax.broadcasted_iota(jnp.int32, (ROW_BLOCK, 128), 1) < 128 - lane
    rows = pl.ds(row, ROW_BLOCK)

    def turned(b):
        at = pl.multiple_of(128 * jnp.minimum(block + b, last), 128)
        return [pltpu.roll(pot[k, layer, rows, pl.ds(at, 128)], turn_by, 1) for k in range(2)]

    blocks = [turned(b) for b in range(window // 128 + 1)]
    for b in range(0, window // 128, 2):
        phase, absorb = [
            jnp.concatenate(
                [jnp.where(here, blocks[i][k], blocks[i + 1][k]) for i in (b, b + 1)], axis=1
            )
            for k in range(2)
        ]
        damping = jnp.exp(-absorb)
        turn = 0.5 * phase
        square = turn * turn
        sine = turn * series(square, (1, -6, 120, -5040, 362880, -39916800, 6227020800))
        cosine = series(square, (1, -2, 24, -720, 40320, -3628800, 479001600))
        at = pl.ds(128 * b, 256)
        out_rows = pl.ds(dst_row, ROW_BLOCK)
        bent = 2.0 * damping * sine
        dst[0, out_rows, at] = (damping - bent * sine).astype(dst.dtype)
        dst[1, out_rows, at] = (bent * cosine).astype(dst.dtype)


def transmission_kernel(offsets, pot_ref, out_ref):
    depth, lat = lax.axis_index("depth"), lax.axis_index("lat")
    band_rows = ROW_BLOCK * pl.num_programs(0)
    for q in range(2):
        place = lax.rem(depth // 2 + q, 2)
        _, layer, col = probe_place(offsets, place, lat, lax.axis_size("lat"), band_rows)
        write_transmission(pot_ref, layer, col, 0, out_ref.at[q], 0)


def transmissions(offsets, potential, window):
    band_rows, columns = potential.shape[3:]
    return pl.pallas_call(
        transmission_kernel,
        out_shape=jax.ShapeDtypeStruct((2, 2, band_rows, window), jnp.bfloat16),
        grid=(band_rows // ROW_BLOCK,),
        in_specs=[
            pl.BlockSpec(memory_space=pltpu.SMEM),
            pl.BlockSpec((2, 2, ROW_BLOCK, columns), lambda r: (0, 0, r, 0)),
        ],
        out_specs=pl.BlockSpec((2, 2, ROW_BLOCK, window), lambda r: (0, 0, r, 0)),
    )(offsets, potential[:, 0])


def band(taps, rows, cols, start, half_width):
    offset = (
        lax.broadcasted_iota(jnp.int32, (rows, cols), 0)
        - lax.broadcasted_iota(jnp.int32, (rows, cols), 1)
        - start
        + half_width
    )
    total = jnp.zeros((rows, cols), jnp.float32)
    for tap_index, tap in enumerate(taps):
        total = jnp.where(offset == tap_index, tap, total)
    return total


def main_kernel(
    offsets, taps_ref, trans_hbm, incident_hbm, measured_hbm, out_ref,
    incident, measured, far_t, t_all, start, waves, adj, terms, row_mat, col_mat,
    send_sem, load_sem, far_sem, beside_sem, edge_sem, start_sem, adj_sem, term_sem,
):
    slices, _, rows, width = waves.shape
    window = incident.shape[2]
    share = window // 2
    tap_count = taps_ref.shape[1]
    half_width = (tap_count - 1) // 2
    band_rows = far_t.shape[1]
    half_band = band_rows // 2
    reach = (rows - half_band) // 2
    blocks = width // 128
    depth, lat = lax.axis_index("depth"), lax.axis_index("lat")
    lat_count = lax.axis_size("lat")
    probe, half = depth // 2, lax.rem(depth, 2)
    other_half = 1 - half
    beside = 2 * probe + other_half
    across = 2 * (1 - probe) + half
    before, after = lax.rem(lat + lat_count - 1, lat_count), lax.rem(lat + 1, lat_count)
    near = lax.rem(lat + 2 * half + lat_count - 1, lat_count)

    def remote(src, dst, send, recv, to):
        return pltpu.make_async_remote_copy(
            src_ref=src,
            dst_ref=dst,
            send_sem=send_sem.at[send],
            recv_sem=recv,
            device_id=to,
            device_id_type=pl.DeviceIdType.MESH,
        )

    own_rows = pl.ds(pl.multiple_of(half_band * half, 16), half_band)
    loads = [
        pltpu.make_async_copy(src, dst, load_sem.at[i])
        for i, (src, dst) in enumerate(
            [
                (trans_hbm.at[1], far_t),
                (trans_hbm.at[0], t_all.at[0, 0, :, pl.ds(reach, band_rows)]),
                (incident_hbm.at[:, probe], incident),
                (measured_hbm.at[probe, own_rows], measured),
            ]
        )
    ]
    for load in loads:
        load.start()

    barrier = pltpu.get_barrier_semaphore()
    senders = [
        (beside, lat),
        (across, lat),
        (2 * (1 - probe) + other_half, lat),
        (2 * probe, near),
        (2 * probe + 1, near),
    ]
    for to in senders:
        pl.semaphore_signal(
            barrier, inc=1, device_id=to, device_id_type=pl.DeviceIdType.MESH
        )
    pl.semaphore_wait(barrier, len(senders))

    inner = pl.ds(reach, band_rows)
    place_row = band_rows * lat
    at_row = offsets[probe, 0]
    at_top = (at_row == place_row) | (at_row == place_row + window)
    at_bottom = (at_row == place_row + band_rows) | (at_row == place_row + band_rows - window)
    top_ok = jnp.logical_not(at_top) | (half == 1)
    bottom_ok = jnp.logical_not(at_bottom) | (half == 0)

    fresh = [pl.ds(0, width), pl.ds(width, window - width)]
    first = [0, window - width]
    far = [
        remote(
            far_t.at[:, :, cols], t_all.at[0, 1, :, inner, cols],
            13 + n, far_sem.at[n], (across, lat),
        )
        for n, cols in enumerate(fresh)
    ]
    loads[0].wait()
    far[0].start()
    loads[2].wait()
    start[:, inner] = incident[...].astype(jnp.bfloat16)
    loads[1].wait()

    shared = pl.ds(pl.multiple_of(reach + (half_band - reach) * other_half, 16), half_band + reach)
    edge_rows = pl.ds(pl.multiple_of((band_rows + reach) * half, 16), reach)
    tail, head = pl.ds(band_rows, reach), pl.ds(reach, reach)
    low, high = pl.ds(0, reach), pl.ds(band_rows + reach, reach)

    groups = [(0, pl.ds(0, window)), (1, fresh[0]), (1, fresh[1])]

    def slot_copies(group):
        side, cols = groups[group]
        return [
            remote(
                t_all.at[0, side, :, shared, cols], t_all.at[1, side, :, shared, cols],
                3 * group, beside_sem.at[group], (beside, lat),
            ),
            remote(
                t_all.at[0, side, :, tail, cols], t_all.at[half, side, :, low, cols],
                3 * group + 1, edge_sem.at[half, group], (2 * probe, after),
            ),
            remote(
                t_all.at[0, side, :, head, cols], t_all.at[other_half, side, :, high, cols],
                3 * group + 2, edge_sem.at[other_half, group], (2 * probe + 1, before),
            ),
        ]

    def finish_slot(group):
        side, cols = groups[group]
        slot_copies(group)[0].wait_recv()
        for core in range(2):
            remote(
                t_all.at[0, side, :, tail, cols], t_all.at[core, side, :, edge_rows, cols],
                3 * group + 1, edge_sem.at[core, group], (beside, lat),
            ).wait_recv()
            edge = t_all[core, side, :, edge_rows, cols]
            t_all[core, side, :, edge_rows, cols] = jnp.where(
                top_ok & bottom_ok, edge, jnp.zeros_like(edge)
            )

    start_rows = pl.ds(pl.multiple_of(reach + (band_rows - reach) * other_half, 16), reach)
    toward = lax.rem(lat + 1 - 2 * half + lat_count, lat_count)
    start_copy = remote(
        start.at[:, start_rows], start.at[:, edge_rows], 9, start_sem.at[0], (depth, toward)
    )
    near_copies = slot_copies(0)
    for copy in [start_copy] + near_copies:
        copy.start()

    taps = taps_ref[...].astype(jnp.float32)
    re = [taps[0:1, i : i + 1] for i in range(tap_count)]
    im = [taps[1:2, i : i + 1] for i in range(tap_count)]
    ways = ((re, im), (re[::-1], [-tap for tap in im[::-1]]))
    for way, (tap_re, tap_im) in enumerate(ways):
        real = band(tap_re[::-1], rows, rows, 0, half_width)
        imag = band(tap_im[::-1], rows, rows, 0, half_width)
        row_mat[way] = jnp.concatenate(
            [
                jnp.concatenate([real, -imag], axis=1),
                jnp.concatenate([imag, real], axis=1),
            ],
            axis=0,
        ).astype(jnp.bfloat16)
        real = band(tap_re, 384, 128, 128, half_width)
        imag = band(tap_im, 384, 128, 128, half_width)
        col_mat[way, :384, :128] = real.astype(jnp.bfloat16)
        col_mat[way, :384, 128:] = imag.astype(jnp.bfloat16)
        col_mat[way, 384:, :128] = (-imag).astype(jnp.bfloat16)
        col_mat[way, 384:, 128:] = real.astype(jnp.bfloat16)

    def rows_conv(field, way):
        return jnp.dot(row_mat[way], field, preferred_element_type=jnp.float32).astype(
            jnp.bfloat16
        )

    def cols_conv(field, way):
        edge = jnp.zeros((rows, 128), jnp.bfloat16)
        padded = [
            jnp.concatenate([edge, field[k * rows : (k + 1) * rows], edge], axis=1)
            for k in range(2)
        ]
        slabs = jnp.concatenate(
            [
                jnp.concatenate([part[:, 128 * b : 128 * b + 384] for part in padded], axis=1)
                for b in range(blocks)
            ],
            axis=0,
        )
        out = jnp.dot(slabs, col_mat[way], preferred_element_type=jnp.float32)
        out = out.astype(jnp.bfloat16)
        return [
            jnp.concatenate(
                [out[b * rows : (b + 1) * rows, 128 * k : 128 * k + 128] for b in range(blocks)],
                axis=1,
            )
            for k in range(2)
        ]

    extent = pl.ds(pl.multiple_of(half_band * half, 16), rows)

    def place_of(s):
        return lax.rem(s % 2 + half, 2), lax.rem(s // 2 + probe, 2)

    def factor(s, cols):
        core, side = place_of(s)
        both = t_all[core, side, :, extent, cols].astype(jnp.float32)
        return both[0], both[1]

    def term_copy(n, s):
        core, side = place_of(s)
        at = 2 * side + core
        cols = pl.ds(share * n, share)
        return remote(
            terms.at[s, :, :, cols], out_ref.at[side, core, :, :, cols],
            15 + 4 * n + at, term_sem.at[n, at], (s, lat),
        )

    def adjoint_copies(n):
        return [
            remote(
                adj.at[n, :, pl.ds(reach, reach)], adj.at[n, :, pl.ds(rows - reach, reach)],
                23 + n, adj_sem.at[n, 1], (beside, up_lat),
            ),
            remote(
                adj.at[n, :, pl.ds(rows - 2 * reach, reach)], adj.at[n, :, pl.ds(0, reach)],
                25 + n, adj_sem.at[n, 0], (beside, down_lat),
            ),
        ]

    up_lat = lax.rem(lat + half + lat_count - 1, lat_count)
    down_lat = lax.rem(lat + half, lat_count)
    own = slice(reach, rows - reach)
    far[0].wait_send()
    far[1].start()
    far[0].wait_recv()
    for copy in slot_copies(1):
        copy.start()
    start_copy.wait_recv()
    finish_slot(0)

    for n in range(2):
        cols = pl.ds(first[n], width)
        if n == 0:
            pl.when(probe == 1)(lambda: finish_slot(1))
        else:
            finish_slot(2)
        waves[0] = start[:, extent, cols]
        wave = None
        for s in range(slices):
            if s == slices // 2 and n == 0:
                pl.when(probe == 0)(lambda: finish_slot(1))
            t_re, t_im = factor(s, cols)
            w_re, w_im = waves[s, 0].astype(jnp.float32), waves[s, 1].astype(jnp.float32)
            product = jnp.concatenate(
                [t_re * w_re - t_im * w_im, t_re * w_im + t_im * w_re], axis=0
            )
            wave = cols_conv(rows_conv(product.astype(jnp.bfloat16), 0), 0)
            if s + 1 < slices:
                waves[s + 1, 0], waves[s + 1, 1] = wave

        w_re, w_im = [part[own].astype(jnp.float32) for part in wave]
        if n == 0:
            loads[3].wait()
        residual = 2.0 * (w_re * w_re + w_im * w_im - measured[:, cols])
        adj[n, 0, own] = (residual * w_re).astype(jnp.bfloat16)
        adj[n, 1, own] = (residual * w_im).astype(jnp.bfloat16)
        for copy in adjoint_copies(n):
            copy.start()
        if n == 0:
            far[1].wait_recv()
            for copy in slot_copies(2):
                copy.start()
        for copy in adjoint_copies(n):
            copy.wait_recv()
        adjoint = []
        for k in range(2):
            top, bottom = adj[n, k, :reach], adj[n, k, rows - reach :]
            adjoint.append(
                jnp.concatenate(
                    [
                        jnp.where(top_ok, top, jnp.zeros_like(top)),
                        adj[n, k, own],
                        jnp.where(bottom_ok, bottom, jnp.zeros_like(bottom)),
                    ],
                    axis=0,
                )
            )

        mine = slice(share * n - first[n], share * n - first[n] + share)
        kept = slice(share * n, share * n + share)
        for s in reversed(range(slices)):
            spread = cols_conv(jnp.concatenate(adjoint, axis=0), 1)
            grad = rows_conv(jnp.concatenate(spread, axis=0), 1).astype(jnp.float32)
            g_re, g_im = grad[:rows], grad[rows:]
            t_re, t_im = factor(s, cols)
            back_re = t_re * g_re + t_im * g_im
            back_im = t_re * g_im - t_im * g_re
            b_re, b_im = back_re[own, mine], back_im[own, mine]
            e_re = waves[s, 0, own, mine].astype(jnp.float32)
            e_im = waves[s, 1, own, mine].astype(jnp.float32)
            terms[s, 0, :, kept] = (e_re * b_im - e_im * b_re).astype(jnp.bfloat16)
            terms[s, 1, :, kept] = (-e_re * b_re - e_im * b_im).astype(jnp.bfloat16)
            pl.when(depth != s)(lambda: term_copy(n, s).start())

            @pl.when(depth == s)
            def _():
                out_ref[0, 0, :, :, kept] = terms[s, :, :, kept]

            adjoint = [back_re.astype(jnp.bfloat16), back_im.astype(jnp.bfloat16)]

    for copy in [far[1], start_copy] + near_copies + slot_copies(1) + slot_copies(2):
        copy.wait_send()
    for n in range(2):
        for copy in adjoint_copies(n):
            copy.wait_send()
        for s in range(slices):
            pl.when(depth != s)(lambda: term_copy(n, s).wait_send())
        cols = pl.ds(share * n, share)
        for at in range(1, 4):
            remote(
                terms.at[0, :, :, cols], out_ref.at[at // 2, at % 2, :, :, cols],
                15 + 4 * n + at, term_sem.at[n, at], (beside, lat),
            ).wait_recv()


def section_terms(offsets, taps, trans, incident, measured, reach):
    slices, band_rows, window = 4, trans.shape[2], trans.shape[3]
    half_band = band_rows // 2
    rows = half_band + 2 * reach
    width = window // 2 + 128
    smem = pl.BlockSpec(memory_space=pltpu.SMEM)
    vmem = pl.BlockSpec(memory_space=pltpu.VMEM)
    hbm = pl.BlockSpec(memory_space=pl.ANY)
    return pl.pallas_call(
        main_kernel,
        out_shape=jax.ShapeDtypeStruct((2, 2, 2, half_band, window), jnp.bfloat16),
        in_specs=[smem, vmem, hbm, hbm, hbm],
        out_specs=vmem,
        scratch_shapes=[
            pltpu.VMEM((2, band_rows, window), jnp.float32),
            pltpu.VMEM((half_band, window), jnp.float32),
            pltpu.VMEM((2, band_rows, window), jnp.bfloat16),
            pltpu.VMEM((2, 2, 2, band_rows + 2 * reach, window), jnp.bfloat16),
            pltpu.VMEM((2, band_rows + 2 * reach, window), jnp.bfloat16),
            pltpu.VMEM((slices, 2, rows, width), jnp.bfloat16),
            pltpu.VMEM((2, 2, rows, width), jnp.bfloat16),
            pltpu.VMEM((slices, 2, half_band, window), jnp.bfloat16),
            pltpu.VMEM((2, 2 * rows, 2 * rows), jnp.bfloat16),
            pltpu.VMEM((2, 768, 256), jnp.bfloat16),
            pltpu.SemaphoreType.DMA((27,)),
            pltpu.SemaphoreType.DMA((4,)),
            pltpu.SemaphoreType.DMA((2,)),
            pltpu.SemaphoreType.DMA((3,)),
            pltpu.SemaphoreType.DMA((2, 3)),
            pltpu.SemaphoreType.DMA((1,)),
            pltpu.SemaphoreType.DMA((2, 2)),
            pltpu.SemaphoreType.DMA((2, 4)),
        ],
        compiler_params=pltpu.CompilerParams(
            vmem_limit_bytes=60 * 1024 * 1024, collective_id=0, has_side_effects=True
        ),
    )(offsets, taps, trans, incident, measured)


def place_kernel(offsets, terms_ref, out_ref):
    columns, window = out_ref.shape[3], terms_ref.shape[4]
    half_band = terms_ref.shape[3]
    per_half = half_band // ROW_BLOCK
    depth, lat = lax.axis_index("depth"), lax.axis_index("lat")
    probe, half = depth // 2, lax.rem(depth, 2)
    r = pl.program_id(0)
    core = lax.rem(r // per_half + half, 2)
    rows = pl.ds(pl.multiple_of(ROW_BLOCK * lax.rem(r, per_half), ROW_BLOCK), ROW_BLOCK)
    last = columns // 128 - 1
    lanes = lax.broadcasted_iota(jnp.int32, (ROW_BLOCK, 128), 1)
    out_ref[...] = jnp.zeros_like(out_ref)
    for q in range(2):
        place = lax.rem(probe + q, 2)
        _, layer, col = probe_place(offsets, place, lat, lax.axis_size("lat"), 2 * half_band)
        block, lane = col // 128, lax.rem(col, 128)
        for part in range(2):
            turned = [jnp.zeros((ROW_BLOCK, 128), jnp.float32)]
            for b in range(window // 128):
                values = terms_ref[q, core, part, rows, pl.ds(128 * b, 128)]
                turned.append(pltpu.roll(values.astype(jnp.float32), lane, 1))
            pieces = [jnp.where(lanes < lane, low, high) for low, high in zip(turned, turned[1:])]
            wide = jnp.concatenate(pieces, axis=1)
            past = jnp.where(lanes < lane, turned[-1], 0.0)
            at = pl.ds(pl.multiple_of(128 * block, 128), window)
            end = pl.multiple_of(128 * jnp.minimum(block + window // 128, last), 128)
            if q == 1:
                wide = wide + out_ref[part, layer, :, at]
            out_ref[part, layer, :, at] = wide
            out_ref[part, layer, :, pl.ds(end, 128)] += past


def placed(offsets, terms, columns):
    half_band = terms.shape[3]
    return pl.pallas_call(
        place_kernel,
        out_shape=jax.ShapeDtypeStruct((2, 2, 2 * half_band, columns), jnp.float32),
        grid=(2 * half_band // ROW_BLOCK,),
        in_specs=[
            pl.BlockSpec(memory_space=pltpu.SMEM),
            pl.BlockSpec(terms.shape, lambda r: (0, 0, 0, 0, 0)),
        ],
        out_specs=pl.BlockSpec((2, 2, ROW_BLOCK, columns), lambda r: (0, 0, r, 0)),
    )(offsets, terms)


def local_fast(potential, incident, measured, offsets, kernel):
    reach = 4 * ((kernel.shape[1] - 1) // 2)
    trans = transmissions(offsets, potential, incident.shape[3])
    terms = section_terms(offsets, kernel, trans, incident, measured, reach)
    return placed(offsets, terms, potential.shape[4])[:, None]


def solution(mesh):
    def run(*args):
        potential, incident, _, _, kernel = args
        body = local_fast if fits(mesh, potential.shape, incident.shape, kernel.shape) else local
        in_specs = (
            P(None, "depth", None, "lat", None),
            P(None, None, "lat", None),
            P(None, "lat", None),
            P(),
            P(),
        )
        out_specs = P(None, "depth", None, "lat", None)
        return jax.shard_map(
            body, mesh=mesh, in_specs=in_specs, out_specs=out_specs, check_vma=False
        )(*args)

    return run
```

```python
import functools

import jax
import jax.numpy as jnp
from jax import lax
from jax.experimental import pallas as pl
from jax.experimental.pallas import tpu as pltpu
from jax.sharding import PartitionSpec as P


def with_halo(cells, sides, width):
    for axis, dim in sides:
        count = lax.axis_size(axis)
        head = lax.slice_in_dim(cells, 0, width, axis=dim)
        tail = lax.slice_in_dim(cells, cells.shape[dim] - width, cells.shape[dim], axis=dim)
        cells = jnp.concatenate(
            [
                lax.ppermute(tail, axis, [(i, (i + 1) % count) for i in range(count)]),
                cells,
                lax.ppermute(head, axis, [((i + 1) % count, i) for i in range(count)]),
            ],
            axis=dim,
        )
    return cells


def from_behind(array, axis, by):
    count = lax.axis_size(axis)
    pairs = [(i, i + by) for i in range(count) if 0 <= i + by < count]
    return lax.ppermute(array, axis, pairs)


def rounded(field_in):
    return lax.optimization_barrier(field_in.astype(jnp.bfloat16)).astype(jnp.float32)


def band_matrix(taps_re, taps_im, row_count, col_count, half_width, transposed):
    row_index = lax.broadcasted_iota(jnp.int32, (row_count, col_count), 0)
    col_index = lax.broadcasted_iota(jnp.int32, (row_count, col_count), 1)
    offset = row_index - col_index if transposed else col_index - row_index
    chooser = (offset[:, :, None] == jnp.arange(2 * half_width + 1, dtype=jnp.int32)).astype(
        jnp.float32
    )
    real_part = jnp.sum(chooser * taps_re, axis=2).astype(jnp.bfloat16)
    imag_part = jnp.sum(chooser * taps_im, axis=2).astype(jnp.bfloat16)
    return (real_part, imag_part)


def along_rows(field_in, real_mat, imag_mat):
    direct = jnp.einsum("rq,xpqc->xprc", real_mat, field_in, preferred_element_type=jnp.float32)
    crossed = jnp.einsum("rq,xpqc->xprc", imag_mat, field_in, preferred_element_type=jnp.float32)
    return jnp.stack([direct[0] - crossed[1], crossed[0] + direct[1]])


def along_cols(field_in, real_slab, imag_slab, half_width):
    columns = field_in.shape[-1]
    blocks = columns // 128
    padded = jnp.pad(field_in, ((0, 0), (0, 0), (0, 0), (half_width, 128 - half_width)))
    main_part = padded[..., :columns].reshape(field_in.shape[:-1] + (blocks, 128))
    extra_part = padded[..., 128 : columns + 128].reshape(field_in.shape[:-1] + (blocks, 128))[
        ..., : 2 * half_width
    ]
    slab_rows = jnp.concatenate([main_part, extra_part], axis=-1)
    direct = jnp.einsum("xprbq,qo->xprbo", slab_rows, real_slab, preferred_element_type=jnp.float32)
    crossed = jnp.einsum(
        "xprbq,qo->xprbo", slab_rows, imag_slab, preferred_element_type=jnp.float32
    )
    joined = jnp.stack([direct[0] - crossed[1], crossed[0] + direct[1]])
    return joined.reshape(field_in.shape)


def local(potential, incident, measured, offsets, kernel):
    lat_count = lax.axis_size("lat")
    depth_count = lax.axis_size("depth")
    lat_index = lax.axis_index("lat")
    depth_index = lax.axis_index("depth")
    band_rows = potential.shape[3]
    window = incident.shape[3]
    probe_count = incident.shape[1]
    half_width = (kernel.shape[1] - 1) // 2
    taps_re = kernel[0].astype(jnp.float32)
    taps_im = kernel[1].astype(jnp.float32)
    back_re = taps_re[::-1]
    back_im = -taps_im[::-1]
    row_pixel = offsets[:, 0]
    col_pixel = offsets[:, 1]
    first_band = row_pixel // band_rows
    place_band = (lat_index - first_band) % lat_count
    layer_pot = potential[:, 0]
    reach_steps = 2
    margin = reach_steps * half_width
    full_rows = band_rows + 2 * margin
    most_out = full_rows - 2 * half_width
    row_forward = band_matrix(taps_re, taps_im, most_out, full_rows, half_width, False)
    row_adjoint = band_matrix(back_re, back_im, most_out, full_rows, half_width, False)
    column_forward = band_matrix(taps_re, taps_im, 128 + 2 * half_width, 128, half_width, True)
    column_adjoint = band_matrix(back_re, back_im, 128 + 2 * half_width, 128, half_width, True)
    local_rows = jnp.arange(full_rows, dtype=jnp.int32) - margin
    window_row = place_band[:, None] * band_rows + local_rows[None, :]
    valid_rows = (window_row >= 0) & (window_row < window)
    keep_mask = valid_rows[None, :, :, None]
    padded_pot = with_halo(layer_pot, (("lat", 2),), margin)
    local_rows = jnp.arange(band_rows + 2 * margin, dtype=jnp.int32) - margin
    side_rows = (local_rows >= band_rows).astype(jnp.int32) - (local_rows < 0).astype(jnp.int32)
    halves = jnp.clip(
        (first_band[:, None] + place_band[:, None] + side_rows[None, :]) // lat_count, 0, 1
    )

    def cut_window(col_start):
        return lax.dynamic_slice_in_dim(padded_pot, col_start, window, 3)

    windows = jax.vmap(cut_window)(col_pixel)
    chosen = jnp.where((halves == 0)[:, None, :, None], windows[:, :, 0], windows[:, :, 1])
    damping = jnp.exp(-chosen[:, 1])
    phase_part = chosen[:, 0]
    transmit = jnp.stack([damping * jnp.cos(phase_part), damping * jnp.sin(phase_part)])

    def forward_segment(wave_ext, extent):
        low_row = margin - extent
        rows_in = band_rows + 2 * extent
        rows_out = rows_in - 2 * half_width
        factor = transmit[:, :, low_row : low_row + rows_in]
        inside = keep_mask[:, :, low_row : low_row + rows_in]
        values = wave_ext.astype(jnp.float32)
        product = jnp.stack(
            [
                factor[0] * values[0] - factor[1] * values[1],
                factor[0] * values[1] + factor[1] * values[0],
            ]
        )
        product = jnp.where(inside, product, 0.0).astype(jnp.bfloat16)
        spread = along_rows(
            product, row_forward[0][:rows_out, :rows_in], row_forward[1][:rows_out, :rows_in]
        ).astype(jnp.bfloat16)
        return along_cols(spread, column_forward[0], column_forward[1], half_width).astype(
            jnp.bfloat16
        )

    def backward_segment(adjoint, extent, entry):
        low_row = margin - extent
        rows_in = band_rows + 2 * extent
        rows_out = rows_in - 2 * half_width
        inside = keep_mask[:, :, low_row : low_row + rows_in]
        masked = jnp.where(inside, adjoint, jnp.zeros_like(adjoint))
        spread = along_cols(masked, column_adjoint[0], column_adjoint[1], half_width).astype(
            jnp.bfloat16
        )
        local_grad = rounded(
            along_rows(
                spread, row_adjoint[0][:rows_out, :rows_in], row_adjoint[1][:rows_out, :rows_in]
            )
        )
        factor = transmit[:, :, low_row + half_width : low_row + half_width + rows_out]
        earlier = jnp.stack(
            [
                factor[0] * local_grad[0] + factor[1] * local_grad[1],
                factor[0] * local_grad[1] - factor[1] * local_grad[0],
            ]
        ).astype(jnp.bfloat16)
        centre = extent - half_width
        own_rows = local_grad[:, :, centre : centre + band_rows]
        own_factor = factor[:, :, centre : centre + band_rows]
        entry_wave = entry.astype(jnp.float32)
        cross_re = entry_wave[0] * own_rows[0] + entry_wave[1] * own_rows[1]
        cross_im = entry_wave[0] * own_rows[1] - entry_wave[1] * own_rows[0]
        turned_re = own_factor[0] * cross_re + own_factor[1] * cross_im
        turned_im = own_factor[0] * cross_im - own_factor[1] * cross_re
        return (earlier, jnp.stack([turned_im, -turned_re]))

    start_wave = incident.astype(jnp.bfloat16)
    zeros_wave = jnp.zeros_like(start_wave)
    blocks = depth_count // reach_steps

    def forward_block(block_index, carry):
        moving, stored, leaving = carry
        entering = jnp.where(depth_index == 0, start_wave, moving)
        wave_ext = with_halo(entering, (("lat", 2),), margin)
        for sub_step in range(reach_steps):
            extent = margin - sub_step * half_width
            result = forward_segment(wave_ext, extent)
            active = depth_index == block_index * reach_steps + sub_step
            stored = jnp.where(active, wave_ext[:, :, extent : extent + band_rows], stored)
            if sub_step == reach_steps - 1:
                leaving = jnp.where(active, result, leaving)
            wave_ext = from_behind(result, "depth", 1)
        return (wave_ext, stored, leaving)

    moving, stored, leaving = lax.fori_loop(
        0, blocks, forward_block, (zeros_wave, zeros_wave, zeros_wave)
    )
    exit_vals = leaving.astype(jnp.float32)
    residual = exit_vals[0] * exit_vals[0] + exit_vals[1] * exit_vals[1] - measured
    seed_wave = (2.0 * residual[None] * exit_vals).astype(jnp.bfloat16)
    zeros_term = jnp.zeros(start_wave.shape, jnp.float32)

    def backward_block(block_index, carry):
        moving_back, collected = carry
        entering = jnp.where(depth_index == depth_count - 1, seed_wave, moving_back)
        adjoint = with_halo(entering, (("lat", 2),), margin)
        for sub_step in range(reach_steps):
            extent = margin - sub_step * half_width
            earlier, grad_term = backward_segment(adjoint, extent, stored)
            active = depth_index == depth_count - 1 - (block_index * reach_steps + sub_step)
            collected = jnp.where(active, grad_term, collected)
            adjoint = from_behind(earlier, "depth", -1)
        return (adjoint, collected)

    moving_back, gathered = lax.fori_loop(0, blocks, backward_block, (zeros_wave, zeros_term))
    own_half = (first_band + place_band) // lat_count
    gradient = jnp.zeros_like(layer_pot)

    def accumulate(probe_index, running):
        portion = lax.dynamic_index_in_dim(gathered, probe_index, 1, keepdims=False)
        zero_index = jnp.zeros((), jnp.int32)
        corner = (zero_index, own_half[probe_index], zero_index, col_pixel[probe_index])
        current = lax.dynamic_slice(running, corner, (2, 1, band_rows, window))
        return lax.dynamic_update_slice(running, current + portion[:, None], corner)

    gradient = lax.fori_loop(0, probe_count, accumulate, gradient)
    return gradient[:, None]


ROW_BLOCK = 32


def fits(mesh, potential_shape, incident_shape, kernel_shape):
    depth_count, lat_count = mesh.shape["depth"], mesh.shape["lat"]
    slices, window, columns = potential_shape[1], incident_shape[3], potential_shape[4]
    half_width = (kernel_shape[1] - 1) // 2
    if incident_shape[1] != 2 or depth_count != 4 or slices != 4:
        return False
    half_band = potential_shape[3] // lat_count // 2
    reach = slices * half_width
    return (
        half_width <= 8
        and 2 * reach <= half_band
        and reach % 16 == 0
        and half_band % ROW_BLOCK == 0
        and window % 256 == 0
        and 8 * half_width <= 128
        and columns == 2 * window
    )


def series(square, divisors):
    total = 1.0 / divisors[-1]
    for divisor in divisors[-2::-1]:
        total = total * square + 1.0 / divisor
    return total


def probe_place(offsets, probe, lat, lat_count, band_rows):
    first_band = offsets[probe, 0] // band_rows
    place_band = lax.rem(lat - first_band + lat_count, lat_count)
    return place_band, (first_band + place_band) // lat_count, offsets[probe, 1]


def write_transmission(pot, block, lane, dst):
    window = dst.shape[2]
    last = pot.shape[2] // 128 - 1
    turn_by = lax.rem(128 - lane, 128)
    here = lax.broadcasted_iota(jnp.int32, (ROW_BLOCK, 128), 1) < 128 - lane

    def turned(b):
        at = pl.multiple_of(128 * jnp.minimum(block + b, last), 128)
        return [pltpu.roll(pot[k, :, pl.ds(at, 128)], turn_by, 1) for k in range(2)]

    blocks = [turned(b) for b in range(window // 128 + 1)]
    for b in range(0, window // 128, 2):
        phase, absorb = [
            jnp.concatenate(
                [jnp.where(here, blocks[i][k], blocks[i + 1][k]) for i in (b, b + 1)], axis=1
            )
            for k in range(2)
        ]
        damping = jnp.exp(-absorb)
        turn = 0.5 * phase
        square = turn * turn
        sine = turn * series(square, (1, -6, 120, -5040, 362880, -39916800, 6227020800))
        cosine = series(square, (1, -2, 24, -720, 40320, -3628800, 479001600))
        at = pl.ds(128 * b, 256)
        bent = 2.0 * damping * sine
        dst[0, :, at] = (damping - bent * sine).astype(dst.dtype)
        dst[1, :, at] = (bent * cosine).astype(dst.dtype)


def transmission_kernel(offsets, pot_hbm, out_hbm, pot, out, in_sem, out_sem):
    depth, lat = lax.axis_index("depth"), lax.axis_index("lat")
    chunks = pot.shape[1]
    band_rows = ROW_BLOCK * chunks
    columns, fetched = pot_hbm.shape[4], pot.shape[4]
    places = []
    for q in range(2):
        place = lax.rem(depth // 2 + q, 2)
        _, layer, col = probe_place(offsets, place, lat, lax.axis_size("lat"), band_rows)
        places.append((layer, jnp.minimum(col // 128, (columns - fetched) // 128), col))

    def copy_in(q, r):
        layer, begin, _ = places[q]
        cols = pl.ds(pl.multiple_of(128 * begin, 128), fetched)
        src = pot_hbm.at[:, 0, layer, pl.ds(ROW_BLOCK * r, ROW_BLOCK), cols]
        return pltpu.make_async_copy(src, pot.at[q, r], in_sem.at[q, r])

    def copy_out(q, r):
        dst = out_hbm.at[q, :, pl.ds(ROW_BLOCK * r, ROW_BLOCK)]
        return pltpu.make_async_copy(out.at[q, r], dst, out_sem.at[q, r])

    order = [(q, r) for q in range(2) for r in range(chunks)]
    for q, r in order:
        copy_in(q, r).start()
    for q, r in order:
        _, begin, col = places[q]
        copy_in(q, r).wait()
        write_transmission(pot.at[q, r], col // 128 - begin, lax.rem(col, 128), out.at[q, r])
        copy_out(q, r).start()
    for q, r in order:
        copy_out(q, r).wait()


def transmissions(offsets, potential, window):
    band_rows = potential.shape[3]
    chunks = band_rows // ROW_BLOCK
    return pl.pallas_call(
        transmission_kernel,
        out_shape=jax.ShapeDtypeStruct((2, 2, band_rows, window), jnp.bfloat16),
        in_specs=[
            pl.BlockSpec(memory_space=pltpu.SMEM),
            pl.BlockSpec(memory_space=pl.ANY),
        ],
        out_specs=pl.BlockSpec(memory_space=pl.ANY),
        scratch_shapes=[
            pltpu.VMEM((2, chunks, 2, ROW_BLOCK, window + 128), jnp.float32),
            pltpu.VMEM((2, chunks, 2, ROW_BLOCK, window), jnp.bfloat16),
            pltpu.SemaphoreType.DMA((2, chunks)),
            pltpu.SemaphoreType.DMA((2, chunks)),
        ],
        compiler_params=pltpu.CompilerParams(vmem_limit_bytes=60 * 1024 * 1024),
    )(offsets, potential)


def band(taps, rows, cols, start, half_width):
    offset = (
        lax.broadcasted_iota(jnp.int32, (rows, cols), 0)
        - lax.broadcasted_iota(jnp.int32, (rows, cols), 1)
        - start
        + half_width
    )
    total = jnp.zeros((rows, cols), jnp.float32)
    for tap_index, tap in enumerate(taps):
        total = jnp.where(offset == tap_index, tap, total)
    return total


def main_kernel(
    offsets, taps_ref, trans_hbm, incident_hbm, measured_hbm, out_ref,
    incident, measured, far_t, t_all, start, waves, adj, terms, row_mat, col_mat,
    send_sem, load_sem, far_sem, beside_sem, edge_sem, start_sem, adj_sem, term_sem,
):
    slices, _, rows, width = waves.shape
    window = incident.shape[2]
    share = window // 2
    tap_count = taps_ref.shape[1]
    half_width = (tap_count - 1) // 2
    band_rows = far_t.shape[1]
    half_band = band_rows // 2
    reach = (rows - half_band) // 2
    blocks = width // 128
    depth, lat = lax.axis_index("depth"), lax.axis_index("lat")
    lat_count = lax.axis_size("lat")
    probe, half = depth // 2, lax.rem(depth, 2)
    other_half = 1 - half
    beside = 2 * probe + other_half
    across = 2 * (1 - probe) + half
    before, after = lax.rem(lat + lat_count - 1, lat_count), lax.rem(lat + 1, lat_count)
    near = lax.rem(lat + 2 * half + lat_count - 1, lat_count)

    def remote(src, dst, send, recv, to):
        return pltpu.make_async_remote_copy(
            src_ref=src,
            dst_ref=dst,
            send_sem=send_sem.at[send],
            recv_sem=recv,
            device_id=to,
            device_id_type=pl.DeviceIdType.MESH,
        )

    own_rows = pl.ds(pl.multiple_of(half_band * half, 16), half_band)
    loads = [
        pltpu.make_async_copy(src, dst, load_sem.at[i])
        for i, (src, dst) in enumerate(
            [
                (trans_hbm.at[1], far_t),
                (trans_hbm.at[0], t_all.at[0, 0, :, pl.ds(reach, band_rows)]),
                (incident_hbm.at[:, probe], incident),
                (measured_hbm.at[probe, own_rows], measured),
            ]
        )
    ]
    for load in loads:
        load.start()

    barrier = pltpu.get_barrier_semaphore()
    senders = [
        (beside, lat),
        (across, lat),
        (2 * (1 - probe) + other_half, lat),
        (2 * probe, near),
        (2 * probe + 1, near),
    ]
    for to in senders:
        pl.semaphore_signal(
            barrier, inc=1, device_id=to, device_id_type=pl.DeviceIdType.MESH
        )
    pl.semaphore_wait(barrier, len(senders))

    inner = pl.ds(reach, band_rows)
    place_row = band_rows * lat
    at_row = offsets[probe, 0]
    at_top = (at_row == place_row) | (at_row == place_row + window)
    at_bottom = (at_row == place_row + band_rows) | (at_row == place_row + band_rows - window)
    top_ok = jnp.logical_not(at_top) | (half == 1)
    bottom_ok = jnp.logical_not(at_bottom) | (half == 0)

    fresh = [pl.ds(0, width), pl.ds(width, window - width)]
    first = [0, window - width]
    far = [
        remote(
            far_t.at[:, :, cols], t_all.at[0, 1, :, inner, cols],
            13 + n, far_sem.at[n], (across, lat),
        )
        for n, cols in enumerate(fresh)
    ]
    loads[0].wait()
    far[0].start()
    loads[2].wait()
    start[:, inner] = incident[...].astype(jnp.bfloat16)
    loads[1].wait()

    shared = pl.ds(pl.multiple_of(reach + (half_band - reach) * other_half, 16), half_band + reach)
    edge_rows = pl.ds(pl.multiple_of((band_rows + reach) * half, 16), reach)
    tail, head = pl.ds(band_rows, reach), pl.ds(reach, reach)
    low, high = pl.ds(0, reach), pl.ds(band_rows + reach, reach)

    groups = [(0, pl.ds(0, window)), (1, fresh[0]), (1, fresh[1])]

    def slot_copies(group):
        side, cols = groups[group]
        return [
            remote(
                t_all.at[0, side, :, shared, cols], t_all.at[1, side, :, shared, cols],
                3 * group, beside_sem.at[group], (beside, lat),
            ),
            remote(
                t_all.at[0, side, :, tail, cols], t_all.at[half, side, :, low, cols],
                3 * group + 1, edge_sem.at[half, group], (2 * probe, after),
            ),
            remote(
                t_all.at[0, side, :, head, cols], t_all.at[other_half, side, :, high, cols],
                3 * group + 2, edge_sem.at[other_half, group], (2 * probe + 1, before),
            ),
        ]

    def finish_slot(group):
        side, cols = groups[group]
        slot_copies(group)[0].wait_recv()
        for core in range(2):
            remote(
                t_all.at[0, side, :, tail, cols], t_all.at[core, side, :, edge_rows, cols],
                3 * group + 1, edge_sem.at[core, group], (beside, lat),
            ).wait_recv()
            edge = t_all[core, side, :, edge_rows, cols]
            t_all[core, side, :, edge_rows, cols] = jnp.where(
                top_ok & bottom_ok, edge, jnp.zeros_like(edge)
            )

    start_rows = pl.ds(pl.multiple_of(reach + (band_rows - reach) * other_half, 16), reach)
    toward = lax.rem(lat + 1 - 2 * half + lat_count, lat_count)
    start_copy = remote(
        start.at[:, start_rows], start.at[:, edge_rows], 9, start_sem.at[0], (depth, toward)
    )
    near_copies = slot_copies(0)
    for copy in [start_copy] + near_copies:
        copy.start()

    taps = taps_ref[...].astype(jnp.float32)
    re = [taps[0:1, i : i + 1] for i in range(tap_count)]
    im = [taps[1:2, i : i + 1] for i in range(tap_count)]
    ways = ((re, im), (re[::-1], [-tap for tap in im[::-1]]))
    for way, (tap_re, tap_im) in enumerate(ways):
        real = band(tap_re[::-1], rows, rows, 0, half_width)
        imag = band(tap_im[::-1], rows, rows, 0, half_width)
        row_mat[way] = jnp.concatenate(
            [
                jnp.concatenate([real, -imag], axis=1),
                jnp.concatenate([imag, real], axis=1),
            ],
            axis=0,
        ).astype(jnp.bfloat16)
        real = band(tap_re, 384, 128, 128, half_width)
        imag = band(tap_im, 384, 128, 128, half_width)
        col_mat[way, :384, :128] = real.astype(jnp.bfloat16)
        col_mat[way, :384, 128:] = imag.astype(jnp.bfloat16)
        col_mat[way, 384:, :128] = (-imag).astype(jnp.bfloat16)
        col_mat[way, 384:, 128:] = real.astype(jnp.bfloat16)

    def rows_conv(field, way):
        return jnp.dot(row_mat[way], field, preferred_element_type=jnp.float32).astype(
            jnp.bfloat16
        )

    def cols_conv(field, way):
        edge = jnp.zeros((rows, 128), jnp.bfloat16)
        padded = [
            jnp.concatenate([edge, field[k * rows : (k + 1) * rows], edge], axis=1)
            for k in range(2)
        ]
        slabs = jnp.concatenate(
            [
                jnp.concatenate([part[:, 128 * b : 128 * b + 384] for part in padded], axis=1)
                for b in range(blocks)
            ],
            axis=0,
        )
        out = jnp.dot(slabs, col_mat[way], preferred_element_type=jnp.float32)
        out = out.astype(jnp.bfloat16)
        return [
            jnp.concatenate(
                [out[b * rows : (b + 1) * rows, 128 * k : 128 * k + 128] for b in range(blocks)],
                axis=1,
            )
            for k in range(2)
        ]

    extent = pl.ds(pl.multiple_of(half_band * half, 16), rows)

    def place_of(s):
        return lax.rem(s % 2 + half, 2), lax.rem(s // 2 + probe, 2)

    def factor(s, cols):
        core, side = place_of(s)
        both = t_all[core, side, :, extent, cols].astype(jnp.float32)
        return both[0], both[1]

    def term_copy(n, s):
        core, side = place_of(s)
        at = 2 * side + core
        cols = pl.ds(share * n, share)
        return remote(
            terms.at[s, :, :, cols], out_ref.at[side, core, :, :, cols],
            15 + 4 * n + at, term_sem.at[n, at], (s, lat),
        )

    def adjoint_copies(n):
        return [
            remote(
                adj.at[n, :, pl.ds(reach, reach)], adj.at[n, :, pl.ds(rows - reach, reach)],
                23 + n, adj_sem.at[n, 1], (beside, up_lat),
            ),
            remote(
                adj.at[n, :, pl.ds(rows - 2 * reach, reach)], adj.at[n, :, pl.ds(0, reach)],
                25 + n, adj_sem.at[n, 0], (beside, down_lat),
            ),
        ]

    up_lat = lax.rem(lat + half + lat_count - 1, lat_count)
    down_lat = lax.rem(lat + half, lat_count)
    own = slice(reach, rows - reach)
    far[0].wait_send()
    far[1].start()
    far[0].wait_recv()
    for copy in slot_copies(1):
        copy.start()
    start_copy.wait_recv()
    finish_slot(0)

    for n in range(2):
        cols = pl.ds(first[n], width)
        if n == 0:
            pl.when(probe == 1)(lambda: finish_slot(1))
        else:
            finish_slot(2)
        waves[0] = start[:, extent, cols]
        wave = None
        for s in range(slices):
            if s == slices // 2 and n == 0:
                pl.when(probe == 0)(lambda: finish_slot(1))
            t_re, t_im = factor(s, cols)
            w_re, w_im = waves[s, 0].astype(jnp.float32), waves[s, 1].astype(jnp.float32)
            product = jnp.concatenate(
                [t_re * w_re - t_im * w_im, t_re * w_im + t_im * w_re], axis=0
            )
            wave = cols_conv(rows_conv(product.astype(jnp.bfloat16), 0), 0)
            if s + 1 < slices:
                waves[s + 1, 0], waves[s + 1, 1] = wave

        w_re, w_im = [part[own].astype(jnp.float32) for part in wave]
        if n == 0:
            loads[3].wait()
        residual = 2.0 * (w_re * w_re + w_im * w_im - measured[:, cols])
        adj[n, 0, own] = (residual * w_re).astype(jnp.bfloat16)
        adj[n, 1, own] = (residual * w_im).astype(jnp.bfloat16)
        for copy in adjoint_copies(n):
            copy.start()
        if n == 0:
            far[1].wait_recv()
            for copy in slot_copies(2):
                copy.start()
        for copy in adjoint_copies(n):
            copy.wait_recv()
        adjoint = []
        for k in range(2):
            top, bottom = adj[n, k, :reach], adj[n, k, rows - reach :]
            adjoint.append(
                jnp.concatenate(
                    [
                        jnp.where(top_ok, top, jnp.zeros_like(top)),
                        adj[n, k, own],
                        jnp.where(bottom_ok, bottom, jnp.zeros_like(bottom)),
                    ],
                    axis=0,
                )
            )

        mine = slice(share * n - first[n], share * n - first[n] + share)
        kept = slice(share * n, share * n + share)
        for s in reversed(range(slices)):
            spread = cols_conv(jnp.concatenate(adjoint, axis=0), 1)
            grad = rows_conv(jnp.concatenate(spread, axis=0), 1).astype(jnp.float32)
            g_re, g_im = grad[:rows], grad[rows:]
            t_re, t_im = factor(s, cols)
            back_re = t_re * g_re + t_im * g_im
            back_im = t_re * g_im - t_im * g_re
            b_re, b_im = back_re[own, mine], back_im[own, mine]
            e_re = waves[s, 0, own, mine].astype(jnp.float32)
            e_im = waves[s, 1, own, mine].astype(jnp.float32)
            terms[s, 0, :, kept] = (e_re * b_im - e_im * b_re).astype(jnp.bfloat16)
            terms[s, 1, :, kept] = (-e_re * b_re - e_im * b_im).astype(jnp.bfloat16)
            pl.when(depth != s)(lambda: term_copy(n, s).start())

            @pl.when(depth == s)
            def _():
                out_ref[0, 0, :, :, kept] = terms[s, :, :, kept]

            adjoint = [back_re.astype(jnp.bfloat16), back_im.astype(jnp.bfloat16)]

    for copy in [far[1], start_copy] + near_copies + slot_copies(1) + slot_copies(2):
        copy.wait_send()
    for n in range(2):
        for copy in adjoint_copies(n):
            copy.wait_send()
        for s in range(slices):
            pl.when(depth != s)(lambda: term_copy(n, s).wait_send())
        cols = pl.ds(share * n, share)
        for at in range(1, 4):
            remote(
                terms.at[0, :, :, cols], out_ref.at[at // 2, at % 2, :, :, cols],
                15 + 4 * n + at, term_sem.at[n, at], (beside, lat),
            ).wait_recv()


def section_terms(offsets, taps, trans, incident, measured, reach):
    slices, band_rows, window = 4, trans.shape[2], trans.shape[3]
    half_band = band_rows // 2
    rows = half_band + 2 * reach
    width = window // 2 + 128
    smem = pl.BlockSpec(memory_space=pltpu.SMEM)
    vmem = pl.BlockSpec(memory_space=pltpu.VMEM)
    hbm = pl.BlockSpec(memory_space=pl.ANY)
    return pl.pallas_call(
        main_kernel,
        out_shape=jax.ShapeDtypeStruct((2, 2, 2, half_band, window), jnp.bfloat16),
        in_specs=[smem, vmem, hbm, hbm, hbm],
        out_specs=vmem,
        scratch_shapes=[
            pltpu.VMEM((2, band_rows, window), jnp.float32),
            pltpu.VMEM((half_band, window), jnp.float32),
            pltpu.VMEM((2, band_rows, window), jnp.bfloat16),
            pltpu.VMEM((2, 2, 2, band_rows + 2 * reach, window), jnp.bfloat16),
            pltpu.VMEM((2, band_rows + 2 * reach, window), jnp.bfloat16),
            pltpu.VMEM((slices, 2, rows, width), jnp.bfloat16),
            pltpu.VMEM((2, 2, rows, width), jnp.bfloat16),
            pltpu.VMEM((slices, 2, half_band, window), jnp.bfloat16),
            pltpu.VMEM((2, 2 * rows, 2 * rows), jnp.bfloat16),
            pltpu.VMEM((2, 768, 256), jnp.bfloat16),
            pltpu.SemaphoreType.DMA((27,)),
            pltpu.SemaphoreType.DMA((4,)),
            pltpu.SemaphoreType.DMA((2,)),
            pltpu.SemaphoreType.DMA((3,)),
            pltpu.SemaphoreType.DMA((2, 3)),
            pltpu.SemaphoreType.DMA((1,)),
            pltpu.SemaphoreType.DMA((2, 2)),
            pltpu.SemaphoreType.DMA((2, 4)),
        ],
        compiler_params=pltpu.CompilerParams(
            vmem_limit_bytes=60 * 1024 * 1024, collective_id=0, has_side_effects=True
        ),
    )(offsets, taps, trans, incident, measured)


def place_rows(offsets, probe, lat, half_band, core_terms, out_ref):
    columns, window = out_ref.shape[3], core_terms[0].shape[2]
    out_ref[...] = jnp.zeros_like(out_ref)
    last = columns // 128 - 1
    lanes = lax.broadcasted_iota(jnp.int32, (ROW_BLOCK, 128), 1)
    for q in range(2):
        place = lax.rem(probe + q, 2)
        _, layer, col = probe_place(offsets, place, lat, lax.axis_size("lat"), 2 * half_band)
        block, lane = col // 128, lax.rem(col, 128)
        for part in range(2):
            turned = [jnp.zeros((ROW_BLOCK, 128), jnp.float32)]
            for b in range(window // 128):
                values = core_terms[q][part, :, pl.ds(128 * b, 128)]
                turned.append(pltpu.roll(values.astype(jnp.float32), lane, 1))
            pieces = [jnp.where(lanes < lane, low, high) for low, high in zip(turned, turned[1:])]
            wide = jnp.concatenate(pieces, axis=1)
            past = jnp.where(lanes < lane, turned[-1], 0.0)
            at = pl.ds(pl.multiple_of(128 * block, 128), window)
            end = pl.multiple_of(128 * jnp.minimum(block + window // 128, last), 128)
            if q == 1:
                wide = wide + out_ref[part, layer, :, at]
            out_ref[part, layer, :, at] = wide
            out_ref[part, layer, :, pl.ds(end, 128)] += past


def place_kernel(offsets, terms_hbm, out_hbm, terms, out, in_sem, out_sem):
    depth, lat = lax.axis_index("depth"), lax.axis_index("lat")
    probe, half = depth // 2, lax.rem(depth, 2)
    chunks, half_band = out.shape[0], terms_hbm.shape[3]
    per_half = chunks // 2

    def copy_in(q, r):
        core = lax.rem(r // per_half + half, 2)
        rows = pl.ds(ROW_BLOCK * (r % per_half), ROW_BLOCK)
        src = terms_hbm.at[q, core, :, rows]
        return pltpu.make_async_copy(src, terms.at[q, r], in_sem.at[q, r])

    def copies_out(r):
        rows = pl.ds(ROW_BLOCK * r, ROW_BLOCK)
        return [
            pltpu.make_async_copy(
                out.at[r, part, layer],
                out_hbm.at[part, 0, layer, rows],
                out_sem.at[r, part, layer],
            )
            for part in range(2)
            for layer in range(2)
        ]

    for r in range(chunks):
        for q in range(2):
            copy_in(q, r).start()
    for r in range(chunks):
        for q in range(2):
            copy_in(q, r).wait()
        place_rows(offsets, probe, lat, half_band, [terms.at[0, r], terms.at[1, r]], out.at[r])
        for copy in copies_out(r):
            copy.start()
    for r in range(chunks):
        for copy in copies_out(r):
            copy.wait()


def placed(offsets, terms, columns):
    half_band, window = terms.shape[3:]
    chunks = 2 * half_band // ROW_BLOCK
    return pl.pallas_call(
        place_kernel,
        out_shape=jax.ShapeDtypeStruct((2, 1, 2, 2 * half_band, columns), jnp.float32),
        in_specs=[
            pl.BlockSpec(memory_space=pltpu.SMEM),
            pl.BlockSpec(memory_space=pl.ANY),
        ],
        out_specs=pl.BlockSpec(memory_space=pl.ANY),
        scratch_shapes=[
            pltpu.VMEM((2, chunks, 2, ROW_BLOCK, window), jnp.bfloat16),
            pltpu.VMEM((chunks, 2, 2, ROW_BLOCK, columns), jnp.float32),
            pltpu.SemaphoreType.DMA((2, chunks)),
            pltpu.SemaphoreType.DMA((chunks, 2, 2)),
        ],
        compiler_params=pltpu.CompilerParams(vmem_limit_bytes=60 * 1024 * 1024),
    )(offsets, terms)


def local_fast(potential, incident, measured, offsets, kernel):
    reach = 4 * ((kernel.shape[1] - 1) // 2)
    trans = transmissions(offsets, potential, incident.shape[3])
    terms = section_terms(offsets, kernel, trans, incident, measured, reach)
    return placed(offsets, terms, potential.shape[4])


def solution(mesh):
    def run(*args):
        potential, incident, _, _, kernel = args
        body = local_fast if fits(mesh, potential.shape, incident.shape, kernel.shape) else local
        in_specs = (
            P(None, "depth", None, "lat", None),
            P(None, None, "lat", None),
            P(None, "lat", None),
            P(),
            P(),
        )
        out_specs = P(None, "depth", None, "lat", None)
        return jax.shard_map(
            body, mesh=mesh, in_specs=in_specs, out_specs=out_specs, check_vma=False
        )(*args)

    return run
```

```python
import functools

import jax
import jax.numpy as jnp
from jax import lax
from jax.experimental import pallas as pl
from jax.experimental.pallas import tpu as pltpu
from jax.sharding import PartitionSpec as P


def with_halo(cells, sides, width):
    for axis, dim in sides:
        count = lax.axis_size(axis)
        head = lax.slice_in_dim(cells, 0, width, axis=dim)
        tail = lax.slice_in_dim(cells, cells.shape[dim] - width, cells.shape[dim], axis=dim)
        cells = jnp.concatenate(
            [
                lax.ppermute(tail, axis, [(i, (i + 1) % count) for i in range(count)]),
                cells,
                lax.ppermute(head, axis, [((i + 1) % count, i) for i in range(count)]),
            ],
            axis=dim,
        )
    return cells


def from_behind(array, axis, by):
    count = lax.axis_size(axis)
    pairs = [(i, i + by) for i in range(count) if 0 <= i + by < count]
    return lax.ppermute(array, axis, pairs)


def rounded(field_in):
    return lax.optimization_barrier(field_in.astype(jnp.bfloat16)).astype(jnp.float32)


def band_matrix(taps_re, taps_im, row_count, col_count, half_width, transposed):
    row_index = lax.broadcasted_iota(jnp.int32, (row_count, col_count), 0)
    col_index = lax.broadcasted_iota(jnp.int32, (row_count, col_count), 1)
    offset = row_index - col_index if transposed else col_index - row_index
    chooser = (offset[:, :, None] == jnp.arange(2 * half_width + 1, dtype=jnp.int32)).astype(
        jnp.float32
    )
    real_part = jnp.sum(chooser * taps_re, axis=2).astype(jnp.bfloat16)
    imag_part = jnp.sum(chooser * taps_im, axis=2).astype(jnp.bfloat16)
    return (real_part, imag_part)


def along_rows(field_in, real_mat, imag_mat):
    direct = jnp.einsum("rq,xpqc->xprc", real_mat, field_in, preferred_element_type=jnp.float32)
    crossed = jnp.einsum("rq,xpqc->xprc", imag_mat, field_in, preferred_element_type=jnp.float32)
    return jnp.stack([direct[0] - crossed[1], crossed[0] + direct[1]])


def along_cols(field_in, real_slab, imag_slab, half_width):
    columns = field_in.shape[-1]
    blocks = columns // 128
    padded = jnp.pad(field_in, ((0, 0), (0, 0), (0, 0), (half_width, 128 - half_width)))
    main_part = padded[..., :columns].reshape(field_in.shape[:-1] + (blocks, 128))
    extra_part = padded[..., 128 : columns + 128].reshape(field_in.shape[:-1] + (blocks, 128))[
        ..., : 2 * half_width
    ]
    slab_rows = jnp.concatenate([main_part, extra_part], axis=-1)
    direct = jnp.einsum("xprbq,qo->xprbo", slab_rows, real_slab, preferred_element_type=jnp.float32)
    crossed = jnp.einsum(
        "xprbq,qo->xprbo", slab_rows, imag_slab, preferred_element_type=jnp.float32
    )
    joined = jnp.stack([direct[0] - crossed[1], crossed[0] + direct[1]])
    return joined.reshape(field_in.shape)


def local(potential, incident, measured, offsets, kernel):
    lat_count = lax.axis_size("lat")
    depth_count = lax.axis_size("depth")
    lat_index = lax.axis_index("lat")
    depth_index = lax.axis_index("depth")
    band_rows = potential.shape[3]
    window = incident.shape[3]
    probe_count = incident.shape[1]
    half_width = (kernel.shape[1] - 1) // 2
    taps_re = kernel[0].astype(jnp.float32)
    taps_im = kernel[1].astype(jnp.float32)
    back_re = taps_re[::-1]
    back_im = -taps_im[::-1]
    row_pixel = offsets[:, 0]
    col_pixel = offsets[:, 1]
    first_band = row_pixel // band_rows
    place_band = (lat_index - first_band) % lat_count
    layer_pot = potential[:, 0]
    reach_steps = 2
    margin = reach_steps * half_width
    full_rows = band_rows + 2 * margin
    most_out = full_rows - 2 * half_width
    row_forward = band_matrix(taps_re, taps_im, most_out, full_rows, half_width, False)
    row_adjoint = band_matrix(back_re, back_im, most_out, full_rows, half_width, False)
    column_forward = band_matrix(taps_re, taps_im, 128 + 2 * half_width, 128, half_width, True)
    column_adjoint = band_matrix(back_re, back_im, 128 + 2 * half_width, 128, half_width, True)
    local_rows = jnp.arange(full_rows, dtype=jnp.int32) - margin
    window_row = place_band[:, None] * band_rows + local_rows[None, :]
    valid_rows = (window_row >= 0) & (window_row < window)
    keep_mask = valid_rows[None, :, :, None]
    padded_pot = with_halo(layer_pot, (("lat", 2),), margin)
    local_rows = jnp.arange(band_rows + 2 * margin, dtype=jnp.int32) - margin
    side_rows = (local_rows >= band_rows).astype(jnp.int32) - (local_rows < 0).astype(jnp.int32)
    halves = jnp.clip(
        (first_band[:, None] + place_band[:, None] + side_rows[None, :]) // lat_count, 0, 1
    )

    def cut_window(col_start):
        return lax.dynamic_slice_in_dim(padded_pot, col_start, window, 3)

    windows = jax.vmap(cut_window)(col_pixel)
    chosen = jnp.where((halves == 0)[:, None, :, None], windows[:, :, 0], windows[:, :, 1])
    damping = jnp.exp(-chosen[:, 1])
    phase_part = chosen[:, 0]
    transmit = jnp.stack([damping * jnp.cos(phase_part), damping * jnp.sin(phase_part)])

    def forward_segment(wave_ext, extent):
        low_row = margin - extent
        rows_in = band_rows + 2 * extent
        rows_out = rows_in - 2 * half_width
        factor = transmit[:, :, low_row : low_row + rows_in]
        inside = keep_mask[:, :, low_row : low_row + rows_in]
        values = wave_ext.astype(jnp.float32)
        product = jnp.stack(
            [
                factor[0] * values[0] - factor[1] * values[1],
                factor[0] * values[1] + factor[1] * values[0],
            ]
        )
        product = jnp.where(inside, product, 0.0).astype(jnp.bfloat16)
        spread = along_rows(
            product, row_forward[0][:rows_out, :rows_in], row_forward[1][:rows_out, :rows_in]
        ).astype(jnp.bfloat16)
        return along_cols(spread, column_forward[0], column_forward[1], half_width).astype(
            jnp.bfloat16
        )

    def backward_segment(adjoint, extent, entry):
        low_row = margin - extent
        rows_in = band_rows + 2 * extent
        rows_out = rows_in - 2 * half_width
        inside = keep_mask[:, :, low_row : low_row + rows_in]
        masked = jnp.where(inside, adjoint, jnp.zeros_like(adjoint))
        spread = along_cols(masked, column_adjoint[0], column_adjoint[1], half_width).astype(
            jnp.bfloat16
        )
        local_grad = rounded(
            along_rows(
                spread, row_adjoint[0][:rows_out, :rows_in], row_adjoint[1][:rows_out, :rows_in]
            )
        )
        factor = transmit[:, :, low_row + half_width : low_row + half_width + rows_out]
        earlier = jnp.stack(
            [
                factor[0] * local_grad[0] + factor[1] * local_grad[1],
                factor[0] * local_grad[1] - factor[1] * local_grad[0],
            ]
        ).astype(jnp.bfloat16)
        centre = extent - half_width
        own_rows = local_grad[:, :, centre : centre + band_rows]
        own_factor = factor[:, :, centre : centre + band_rows]
        entry_wave = entry.astype(jnp.float32)
        cross_re = entry_wave[0] * own_rows[0] + entry_wave[1] * own_rows[1]
        cross_im = entry_wave[0] * own_rows[1] - entry_wave[1] * own_rows[0]
        turned_re = own_factor[0] * cross_re + own_factor[1] * cross_im
        turned_im = own_factor[0] * cross_im - own_factor[1] * cross_re
        return (earlier, jnp.stack([turned_im, -turned_re]))

    start_wave = incident.astype(jnp.bfloat16)
    zeros_wave = jnp.zeros_like(start_wave)
    blocks = depth_count // reach_steps

    def forward_block(block_index, carry):
        moving, stored, leaving = carry
        entering = jnp.where(depth_index == 0, start_wave, moving)
        wave_ext = with_halo(entering, (("lat", 2),), margin)
        for sub_step in range(reach_steps):
            extent = margin - sub_step * half_width
            result = forward_segment(wave_ext, extent)
            active = depth_index == block_index * reach_steps + sub_step
            stored = jnp.where(active, wave_ext[:, :, extent : extent + band_rows], stored)
            if sub_step == reach_steps - 1:
                leaving = jnp.where(active, result, leaving)
            wave_ext = from_behind(result, "depth", 1)
        return (wave_ext, stored, leaving)

    moving, stored, leaving = lax.fori_loop(
        0, blocks, forward_block, (zeros_wave, zeros_wave, zeros_wave)
    )
    exit_vals = leaving.astype(jnp.float32)
    residual = exit_vals[0] * exit_vals[0] + exit_vals[1] * exit_vals[1] - measured
    seed_wave = (2.0 * residual[None] * exit_vals).astype(jnp.bfloat16)
    zeros_term = jnp.zeros(start_wave.shape, jnp.float32)

    def backward_block(block_index, carry):
        moving_back, collected = carry
        entering = jnp.where(depth_index == depth_count - 1, seed_wave, moving_back)
        adjoint = with_halo(entering, (("lat", 2),), margin)
        for sub_step in range(reach_steps):
            extent = margin - sub_step * half_width
            earlier, grad_term = backward_segment(adjoint, extent, stored)
            active = depth_index == depth_count - 1 - (block_index * reach_steps + sub_step)
            collected = jnp.where(active, grad_term, collected)
            adjoint = from_behind(earlier, "depth", -1)
        return (adjoint, collected)

    moving_back, gathered = lax.fori_loop(0, blocks, backward_block, (zeros_wave, zeros_term))
    own_half = (first_band + place_band) // lat_count
    gradient = jnp.zeros_like(layer_pot)

    def accumulate(probe_index, running):
        portion = lax.dynamic_index_in_dim(gathered, probe_index, 1, keepdims=False)
        zero_index = jnp.zeros((), jnp.int32)
        corner = (zero_index, own_half[probe_index], zero_index, col_pixel[probe_index])
        current = lax.dynamic_slice(running, corner, (2, 1, band_rows, window))
        return lax.dynamic_update_slice(running, current + portion[:, None], corner)

    gradient = lax.fori_loop(0, probe_count, accumulate, gradient)
    return gradient[:, None]


ROW_BLOCK = 32


def fits(mesh, potential_shape, incident_shape, kernel_shape):
    depth_count, lat_count = mesh.shape["depth"], mesh.shape["lat"]
    slices, window, columns = potential_shape[1], incident_shape[3], potential_shape[4]
    half_width = (kernel_shape[1] - 1) // 2
    if incident_shape[1] != 2 or depth_count != 4 or slices != 4:
        return False
    half_band = potential_shape[3] // lat_count // 2
    reach = slices * half_width
    return (
        half_width <= 8
        and 2 * reach <= half_band
        and reach % 16 == 0
        and half_band % ROW_BLOCK == 0
        and window % 256 == 0
        and 8 * half_width <= 128
        and columns == 2 * window
    )


def series(square, divisors):
    total = 1.0 / divisors[-1]
    for divisor in divisors[-2::-1]:
        total = total * square + 1.0 / divisor
    return total


def probe_place(offsets, probe, lat, lat_count, band_rows):
    first_band = offsets[probe, 0] // band_rows
    place_band = lax.rem(lat - first_band + lat_count, lat_count)
    return place_band, (first_band + place_band) // lat_count, offsets[probe, 1]


def transmission(phase, absorb):
    damping = jnp.exp(-absorb)
    turn = 0.5 * phase
    square = turn * turn
    sine = turn * series(square, (1, -6, 120, -5040, 362880, -39916800, 6227020800))
    cosine = series(square, (1, -2, 24, -720, 40320, -3628800, 479001600))
    bent = 2.0 * damping * sine
    return damping - bent * sine, bent * cosine


def write_window(pot, block, lane, dst, convert):
    window = dst.shape[2]
    last = pot.shape[2] // 128 - 1
    turn_by = lax.rem(128 - lane, 128)
    here = lax.broadcasted_iota(jnp.int32, (ROW_BLOCK, 128), 1) < 128 - lane

    def turned(b):
        at = pl.multiple_of(128 * jnp.minimum(block + b, last), 128)
        return [pltpu.roll(pot[k, :, pl.ds(at, 128)], turn_by, 1) for k in range(2)]

    blocks = [turned(b) for b in range(window // 128 + 1)]
    for b in range(0, window // 128, 2):
        phase, absorb = [
            jnp.concatenate(
                [jnp.where(here, blocks[i][k], blocks[i + 1][k]) for i in (b, b + 1)], axis=1
            )
            for k in range(2)
        ]
        values = transmission(phase, absorb) if convert else (phase, absorb)
        for k in range(2):
            dst[k, :, pl.ds(128 * b, 256)] = values[k].astype(dst.dtype)


def transmission_kernel(offsets, pot_hbm, own_hbm, far_hbm, pot, own, far, in_sem, out_sem):
    depth, lat = lax.axis_index("depth"), lax.axis_index("lat")
    chunks = pot.shape[1]
    band_rows = ROW_BLOCK * chunks
    columns, fetched = pot_hbm.shape[4], pot.shape[4]
    places = []
    for q in range(2):
        place = lax.rem(depth // 2 + q, 2)
        _, layer, col = probe_place(offsets, place, lat, lax.axis_size("lat"), band_rows)
        places.append((layer, jnp.minimum(col // 128, (columns - fetched) // 128), col))

    def copy_in(q, r):
        layer, begin, _ = places[q]
        cols = pl.ds(pl.multiple_of(128 * begin, 128), fetched)
        src = pot_hbm.at[:, 0, layer, pl.ds(ROW_BLOCK * r, ROW_BLOCK), cols]
        return pltpu.make_async_copy(src, pot.at[q, r], in_sem.at[q, r])

    def copy_out(q, r):
        src, dst = ((own, own_hbm), (far, far_hbm))[q]
        dst = dst.at[:, pl.ds(ROW_BLOCK * r, ROW_BLOCK)]
        return pltpu.make_async_copy(src.at[r], dst, out_sem.at[q, r])

    order = [(q, r) for q in range(2) for r in range(chunks)]
    for q, r in order:
        copy_in(q, r).start()
    for q, r in order:
        _, begin, col = places[q]
        copy_in(q, r).wait()
        dst = (own, far)[q].at[r]
        write_window(pot.at[q, r], col // 128 - begin, lax.rem(col, 128), dst, q == 1)
        copy_out(q, r).start()
    for q, r in order:
        copy_out(q, r).wait()


def transmissions(offsets, potential, window):
    band_rows = potential.shape[3]
    chunks = band_rows // ROW_BLOCK
    return pl.pallas_call(
        transmission_kernel,
        out_shape=[
            jax.ShapeDtypeStruct((2, band_rows, window), jnp.float32),
            jax.ShapeDtypeStruct((2, band_rows, window), jnp.bfloat16),
        ],
        in_specs=[
            pl.BlockSpec(memory_space=pltpu.SMEM),
            pl.BlockSpec(memory_space=pl.ANY),
        ],
        out_specs=[pl.BlockSpec(memory_space=pl.ANY)] * 2,
        scratch_shapes=[
            pltpu.VMEM((2, chunks, 2, ROW_BLOCK, window + 128), jnp.float32),
            pltpu.VMEM((chunks, 2, ROW_BLOCK, window), jnp.float32),
            pltpu.VMEM((chunks, 2, ROW_BLOCK, window), jnp.bfloat16),
            pltpu.SemaphoreType.DMA((2, chunks)),
            pltpu.SemaphoreType.DMA((2, chunks)),
        ],
        compiler_params=pltpu.CompilerParams(vmem_limit_bytes=60 * 1024 * 1024),
    )(offsets, potential)


def band(taps, rows, cols, start, half_width):
    offset = (
        lax.broadcasted_iota(jnp.int32, (rows, cols), 0)
        - lax.broadcasted_iota(jnp.int32, (rows, cols), 1)
        - start
        + half_width
    )
    total = jnp.zeros((rows, cols), jnp.float32)
    for tap_index, tap in enumerate(taps):
        total = jnp.where(offset == tap_index, tap, total)
    return total


def main_kernel(
    offsets, taps_ref, own_hbm, far_hbm, incident_hbm, measured_hbm, out_ref,
    incident, measured, own_raw, far_t, t_all, start, waves, adj, terms, row_mat, col_mat,
    send_sem, load_sem, far_sem, beside_sem, edge_sem, start_sem, adj_sem, term_sem,
):
    slices, _, rows, width = waves.shape
    window = incident.shape[2]
    share = window // 2
    tap_count = taps_ref.shape[1]
    half_width = (tap_count - 1) // 2
    band_rows = far_t.shape[1]
    half_band = band_rows // 2
    reach = (rows - half_band) // 2
    blocks = width // 128
    depth, lat = lax.axis_index("depth"), lax.axis_index("lat")
    lat_count = lax.axis_size("lat")
    probe, half = depth // 2, lax.rem(depth, 2)
    other_half = 1 - half
    beside = 2 * probe + other_half
    across = 2 * (1 - probe) + half
    before, after = lax.rem(lat + lat_count - 1, lat_count), lax.rem(lat + 1, lat_count)
    near = lax.rem(lat + 2 * half + lat_count - 1, lat_count)

    def remote(src, dst, send, recv, to):
        return pltpu.make_async_remote_copy(
            src_ref=src,
            dst_ref=dst,
            send_sem=send_sem.at[send],
            recv_sem=recv,
            device_id=to,
            device_id_type=pl.DeviceIdType.MESH,
        )

    own_rows = pl.ds(pl.multiple_of(half_band * half, 16), half_band)
    loads = [
        pltpu.make_async_copy(src, dst, load_sem.at[i])
        for i, (src, dst) in enumerate(
            [
                (far_hbm, far_t),
                (own_hbm, own_raw),
                (incident_hbm.at[:, probe], incident),
                (measured_hbm.at[probe, own_rows], measured),
            ]
        )
    ]
    for load in loads:
        load.start()

    barrier = pltpu.get_barrier_semaphore()
    senders = [
        (beside, lat),
        (across, lat),
        (2 * (1 - probe) + other_half, lat),
        (2 * probe, near),
        (2 * probe + 1, near),
    ]
    for to in senders:
        pl.semaphore_signal(
            barrier, inc=1, device_id=to, device_id_type=pl.DeviceIdType.MESH
        )
    pl.semaphore_wait(barrier, len(senders))

    inner = pl.ds(reach, band_rows)
    place_row = band_rows * lat
    at_row = offsets[probe, 0]
    at_top = (at_row == place_row) | (at_row == place_row + window)
    at_bottom = (at_row == place_row + band_rows) | (at_row == place_row + band_rows - window)
    top_ok = jnp.logical_not(at_top) | (half == 1)
    bottom_ok = jnp.logical_not(at_bottom) | (half == 0)

    fresh = [pl.ds(0, width), pl.ds(width, window - width)]
    first = [0, window - width]
    far = [
        remote(
            far_t.at[:, :, cols], t_all.at[0, 1, :, inner, cols],
            13 + n, far_sem.at[n], (across, lat),
        )
        for n, cols in enumerate(fresh)
    ]
    loads[0].wait()
    far[0].start()
    loads[2].wait()
    start[:, inner] = incident[...].astype(jnp.bfloat16)
    loads[1].wait()

    @pl.loop(0, band_rows // 16)
    def _(r):
        rows_in = pl.ds(pl.multiple_of(16 * r, 16), 16)
        rows_out = pl.ds(pl.multiple_of(reach + 16 * r, 16), 16)
        for b in range(0, window, 256):
            at = pl.ds(b, 256)
            values = transmission(own_raw[0, rows_in, at], own_raw[1, rows_in, at])
            t_all[0, 0, 0, rows_out, at] = values[0].astype(jnp.bfloat16)
            t_all[0, 0, 1, rows_out, at] = values[1].astype(jnp.bfloat16)

    shared = pl.ds(pl.multiple_of(reach + (half_band - reach) * other_half, 16), half_band + reach)
    edge_rows = pl.ds(pl.multiple_of((band_rows + reach) * half, 16), reach)
    tail, head = pl.ds(band_rows, reach), pl.ds(reach, reach)
    low, high = pl.ds(0, reach), pl.ds(band_rows + reach, reach)

    groups = [(0, pl.ds(0, window)), (1, fresh[0]), (1, fresh[1])]

    def slot_copies(group):
        side, cols = groups[group]
        return [
            remote(
                t_all.at[0, side, :, shared, cols], t_all.at[1, side, :, shared, cols],
                3 * group, beside_sem.at[group], (beside, lat),
            ),
            remote(
                t_all.at[0, side, :, tail, cols], t_all.at[half, side, :, low, cols],
                3 * group + 1, edge_sem.at[half, group], (2 * probe, after),
            ),
            remote(
                t_all.at[0, side, :, head, cols], t_all.at[other_half, side, :, high, cols],
                3 * group + 2, edge_sem.at[other_half, group], (2 * probe + 1, before),
            ),
        ]

    def finish_slot(group):
        side, cols = groups[group]
        slot_copies(group)[0].wait_recv()
        for core in range(2):
            remote(
                t_all.at[0, side, :, tail, cols], t_all.at[core, side, :, edge_rows, cols],
                3 * group + 1, edge_sem.at[core, group], (beside, lat),
            ).wait_recv()
            edge = t_all[core, side, :, edge_rows, cols]
            t_all[core, side, :, edge_rows, cols] = jnp.where(
                top_ok & bottom_ok, edge, jnp.zeros_like(edge)
            )

    start_rows = pl.ds(pl.multiple_of(reach + (band_rows - reach) * other_half, 16), reach)
    toward = lax.rem(lat + 1 - 2 * half + lat_count, lat_count)
    start_copy = remote(
        start.at[:, start_rows], start.at[:, edge_rows], 9, start_sem.at[0], (depth, toward)
    )
    near_copies = slot_copies(0)
    for copy in [start_copy] + near_copies:
        copy.start()

    taps = taps_ref[...].astype(jnp.float32)
    re = [taps[0:1, i : i + 1] for i in range(tap_count)]
    im = [taps[1:2, i : i + 1] for i in range(tap_count)]
    ways = ((re, im), (re[::-1], [-tap for tap in im[::-1]]))
    for way, (tap_re, tap_im) in enumerate(ways):
        real = band(tap_re[::-1], rows, rows, 0, half_width)
        imag = band(tap_im[::-1], rows, rows, 0, half_width)
        row_mat[way] = jnp.concatenate(
            [
                jnp.concatenate([real, -imag], axis=1),
                jnp.concatenate([imag, real], axis=1),
            ],
            axis=0,
        ).astype(jnp.bfloat16)
        real = band(tap_re, 384, 128, 128, half_width)
        imag = band(tap_im, 384, 128, 128, half_width)
        col_mat[way, :384, :128] = real.astype(jnp.bfloat16)
        col_mat[way, :384, 128:] = imag.astype(jnp.bfloat16)
        col_mat[way, 384:, :128] = (-imag).astype(jnp.bfloat16)
        col_mat[way, 384:, 128:] = real.astype(jnp.bfloat16)

    def rows_conv(field, way):
        return jnp.dot(row_mat[way], field, preferred_element_type=jnp.float32).astype(
            jnp.bfloat16
        )

    def cols_conv(field, way):
        edge = jnp.zeros((rows, 128), jnp.bfloat16)
        padded = [
            jnp.concatenate([edge, field[k * rows : (k + 1) * rows], edge], axis=1)
            for k in range(2)
        ]
        slabs = jnp.concatenate(
            [
                jnp.concatenate([part[:, 128 * b : 128 * b + 384] for part in padded], axis=1)
                for b in range(blocks)
            ],
            axis=0,
        )
        out = jnp.dot(slabs, col_mat[way], preferred_element_type=jnp.float32)
        out = out.astype(jnp.bfloat16)
        return [
            jnp.concatenate(
                [out[b * rows : (b + 1) * rows, 128 * k : 128 * k + 128] for b in range(blocks)],
                axis=1,
            )
            for k in range(2)
        ]

    extent = pl.ds(pl.multiple_of(half_band * half, 16), rows)

    def place_of(s):
        return lax.rem(s % 2 + half, 2), lax.rem(s // 2 + probe, 2)

    def factor(s, cols):
        core, side = place_of(s)
        both = t_all[core, side, :, extent, cols].astype(jnp.float32)
        return both[0], both[1]

    def term_copy(n, s):
        core, side = place_of(s)
        at = 2 * side + core
        cols = pl.ds(share * n, share)
        return remote(
            terms.at[s, :, :, cols], out_ref.at[side, core, :, :, cols],
            15 + 4 * n + at, term_sem.at[n, at], (s, lat),
        )

    def adjoint_copies(n):
        return [
            remote(
                adj.at[n, :, pl.ds(reach, reach)], adj.at[n, :, pl.ds(rows - reach, reach)],
                23 + n, adj_sem.at[n, 1], (beside, up_lat),
            ),
            remote(
                adj.at[n, :, pl.ds(rows - 2 * reach, reach)], adj.at[n, :, pl.ds(0, reach)],
                25 + n, adj_sem.at[n, 0], (beside, down_lat),
            ),
        ]

    up_lat = lax.rem(lat + half + lat_count - 1, lat_count)
    down_lat = lax.rem(lat + half, lat_count)
    own = slice(reach, rows - reach)
    far[0].wait_send()
    far[1].start()
    far[0].wait_recv()
    for copy in slot_copies(1):
        copy.start()
    start_copy.wait_recv()
    finish_slot(0)

    for n in range(2):
        cols = pl.ds(first[n], width)
        if n == 0:
            pl.when(probe == 1)(lambda: finish_slot(1))
        else:
            finish_slot(2)
        waves[0] = start[:, extent, cols]
        wave = None
        for s in range(slices):
            if s == slices // 2 and n == 0:
                pl.when(probe == 0)(lambda: finish_slot(1))
            t_re, t_im = factor(s, cols)
            w_re, w_im = waves[s, 0].astype(jnp.float32), waves[s, 1].astype(jnp.float32)
            product = jnp.concatenate(
                [t_re * w_re - t_im * w_im, t_re * w_im + t_im * w_re], axis=0
            )
            wave = cols_conv(rows_conv(product.astype(jnp.bfloat16), 0), 0)
            if s + 1 < slices:
                waves[s + 1, 0], waves[s + 1, 1] = wave

        w_re, w_im = [part[own].astype(jnp.float32) for part in wave]
        if n == 0:
            loads[3].wait()
        residual = 2.0 * (w_re * w_re + w_im * w_im - measured[:, cols])
        adj[n, 0, own] = (residual * w_re).astype(jnp.bfloat16)
        adj[n, 1, own] = (residual * w_im).astype(jnp.bfloat16)
        for copy in adjoint_copies(n):
            copy.start()
        if n == 0:
            far[1].wait_recv()
            for copy in slot_copies(2):
                copy.start()
        for copy in adjoint_copies(n):
            copy.wait_recv()
        adjoint = []
        for k in range(2):
            top, bottom = adj[n, k, :reach], adj[n, k, rows - reach :]
            adjoint.append(
                jnp.concatenate(
                    [
                        jnp.where(top_ok, top, jnp.zeros_like(top)),
                        adj[n, k, own],
                        jnp.where(bottom_ok, bottom, jnp.zeros_like(bottom)),
                    ],
                    axis=0,
                )
            )

        mine = slice(share * n - first[n], share * n - first[n] + share)
        kept = slice(share * n, share * n + share)
        for s in reversed(range(slices)):
            spread = cols_conv(jnp.concatenate(adjoint, axis=0), 1)
            grad = rows_conv(jnp.concatenate(spread, axis=0), 1).astype(jnp.float32)
            g_re, g_im = grad[:rows], grad[rows:]
            t_re, t_im = factor(s, cols)
            back_re = t_re * g_re + t_im * g_im
            back_im = t_re * g_im - t_im * g_re
            b_re, b_im = back_re[own, mine], back_im[own, mine]
            e_re = waves[s, 0, own, mine].astype(jnp.float32)
            e_im = waves[s, 1, own, mine].astype(jnp.float32)
            terms[s, 0, :, kept] = (e_re * b_im - e_im * b_re).astype(jnp.bfloat16)
            terms[s, 1, :, kept] = (-e_re * b_re - e_im * b_im).astype(jnp.bfloat16)
            pl.when(depth != s)(lambda: term_copy(n, s).start())

            @pl.when(depth == s)
            def _():
                out_ref[0, 0, :, :, kept] = terms[s, :, :, kept]

            adjoint = [back_re.astype(jnp.bfloat16), back_im.astype(jnp.bfloat16)]

    for copy in [far[1], start_copy] + near_copies + slot_copies(1) + slot_copies(2):
        copy.wait_send()
    for n in range(2):
        for copy in adjoint_copies(n):
            copy.wait_send()
        for s in range(slices):
            pl.when(depth != s)(lambda: term_copy(n, s).wait_send())
        cols = pl.ds(share * n, share)
        for at in range(1, 4):
            remote(
                terms.at[0, :, :, cols], out_ref.at[at // 2, at % 2, :, :, cols],
                15 + 4 * n + at, term_sem.at[n, at], (beside, lat),
            ).wait_recv()


def section_terms(offsets, taps, own, far, incident, measured, reach):
    slices, band_rows, window = 4, far.shape[1], far.shape[2]
    half_band = band_rows // 2
    rows = half_band + 2 * reach
    width = window // 2 + 128
    smem = pl.BlockSpec(memory_space=pltpu.SMEM)
    vmem = pl.BlockSpec(memory_space=pltpu.VMEM)
    hbm = pl.BlockSpec(memory_space=pl.ANY)
    return pl.pallas_call(
        main_kernel,
        out_shape=jax.ShapeDtypeStruct((2, 2, 2, half_band, window), jnp.bfloat16),
        in_specs=[smem, vmem, hbm, hbm, hbm, hbm],
        out_specs=vmem,
        scratch_shapes=[
            pltpu.VMEM((2, band_rows, window), jnp.float32),
            pltpu.VMEM((half_band, window), jnp.float32),
            pltpu.VMEM((2, band_rows, window), jnp.float32),
            pltpu.VMEM((2, band_rows, window), jnp.bfloat16),
            pltpu.VMEM((2, 2, 2, band_rows + 2 * reach, window), jnp.bfloat16),
            pltpu.VMEM((2, band_rows + 2 * reach, window), jnp.bfloat16),
            pltpu.VMEM((slices, 2, rows, width), jnp.bfloat16),
            pltpu.VMEM((2, 2, rows, width), jnp.bfloat16),
            pltpu.VMEM((slices, 2, half_band, window), jnp.bfloat16),
            pltpu.VMEM((2, 2 * rows, 2 * rows), jnp.bfloat16),
            pltpu.VMEM((2, 768, 256), jnp.bfloat16),
            pltpu.SemaphoreType.DMA((27,)),
            pltpu.SemaphoreType.DMA((4,)),
            pltpu.SemaphoreType.DMA((2,)),
            pltpu.SemaphoreType.DMA((3,)),
            pltpu.SemaphoreType.DMA((2, 3)),
            pltpu.SemaphoreType.DMA((1,)),
            pltpu.SemaphoreType.DMA((2, 2)),
            pltpu.SemaphoreType.DMA((2, 4)),
        ],
        compiler_params=pltpu.CompilerParams(
            vmem_limit_bytes=60 * 1024 * 1024, collective_id=0, has_side_effects=True
        ),
    )(offsets, taps, own, far, incident, measured)


def place_rows(offsets, probe, lat, half_band, core_terms, out_ref):
    columns, window = out_ref.shape[3], core_terms[0].shape[2]
    out_ref[...] = jnp.zeros_like(out_ref)
    last = columns // 128 - 1
    lanes = lax.broadcasted_iota(jnp.int32, (ROW_BLOCK, 128), 1)
    for q in range(2):
        place = lax.rem(probe + q, 2)
        _, layer, col = probe_place(offsets, place, lat, lax.axis_size("lat"), 2 * half_band)
        block, lane = col // 128, lax.rem(col, 128)
        for part in range(2):
            turned = [jnp.zeros((ROW_BLOCK, 128), jnp.float32)]
            for b in range(window // 128):
                values = core_terms[q][part, :, pl.ds(128 * b, 128)]
                turned.append(pltpu.roll(values.astype(jnp.float32), lane, 1))
            pieces = [jnp.where(lanes < lane, low, high) for low, high in zip(turned, turned[1:])]
            wide = jnp.concatenate(pieces, axis=1)
            past = jnp.where(lanes < lane, turned[-1], 0.0)
            at = pl.ds(pl.multiple_of(128 * block, 128), window)
            end = pl.multiple_of(128 * jnp.minimum(block + window // 128, last), 128)
            if q == 1:
                wide = wide + out_ref[part, layer, :, at]
            out_ref[part, layer, :, at] = wide
            out_ref[part, layer, :, pl.ds(end, 128)] += past


def place_kernel(offsets, terms_hbm, out_hbm, terms, out, in_sem, out_sem):
    depth, lat = lax.axis_index("depth"), lax.axis_index("lat")
    probe, half = depth // 2, lax.rem(depth, 2)
    chunks, half_band = out.shape[0], terms_hbm.shape[3]
    per_half = chunks // 2

    def copy_in(q, r):
        core = lax.rem(r // per_half + half, 2)
        rows = pl.ds(ROW_BLOCK * (r % per_half), ROW_BLOCK)
        src = terms_hbm.at[q, core, :, rows]
        return pltpu.make_async_copy(src, terms.at[q, r], in_sem.at[q, r])

    def copies_out(r):
        rows = pl.ds(ROW_BLOCK * r, ROW_BLOCK)
        return [
            pltpu.make_async_copy(
                out.at[r, part, layer],
                out_hbm.at[part, 0, layer, rows],
                out_sem.at[r, part, layer],
            )
            for part in range(2)
            for layer in range(2)
        ]

    for r in range(chunks):
        for q in range(2):
            copy_in(q, r).start()
    for r in range(chunks):
        for q in range(2):
            copy_in(q, r).wait()
        place_rows(offsets, probe, lat, half_band, [terms.at[0, r], terms.at[1, r]], out.at[r])
        for copy in copies_out(r):
            copy.start()
    for r in range(chunks):
        for copy in copies_out(r):
            copy.wait()


def placed(offsets, terms, columns):
    half_band, window = terms.shape[3:]
    chunks = 2 * half_band // ROW_BLOCK
    return pl.pallas_call(
        place_kernel,
        out_shape=jax.ShapeDtypeStruct((2, 1, 2, 2 * half_band, columns), jnp.float32),
        in_specs=[
            pl.BlockSpec(memory_space=pltpu.SMEM),
            pl.BlockSpec(memory_space=pl.ANY),
        ],
        out_specs=pl.BlockSpec(memory_space=pl.ANY),
        scratch_shapes=[
            pltpu.VMEM((2, chunks, 2, ROW_BLOCK, window), jnp.bfloat16),
            pltpu.VMEM((chunks, 2, 2, ROW_BLOCK, columns), jnp.float32),
            pltpu.SemaphoreType.DMA((2, chunks)),
            pltpu.SemaphoreType.DMA((chunks, 2, 2)),
        ],
        compiler_params=pltpu.CompilerParams(vmem_limit_bytes=60 * 1024 * 1024),
    )(offsets, terms)


def local_fast(potential, incident, measured, offsets, kernel):
    reach = 4 * ((kernel.shape[1] - 1) // 2)
    own, far = transmissions(offsets, potential, incident.shape[3])
    terms = section_terms(offsets, kernel, own, far, incident, measured, reach)
    return placed(offsets, terms, potential.shape[4])


def solution(mesh):
    def run(*args):
        potential, incident, _, _, kernel = args
        body = local_fast if fits(mesh, potential.shape, incident.shape, kernel.shape) else local
        in_specs = (
            P(None, "depth", None, "lat", None),
            P(None, None, "lat", None),
            P(None, "lat", None),
            P(),
            P(),
        )
        out_specs = P(None, "depth", None, "lat", None)
        return jax.shard_map(
            body, mesh=mesh, in_specs=in_specs, out_specs=out_specs, check_vma=False
        )(*args)

    return run
```

```python
import functools

import jax
import jax.numpy as jnp
from jax import lax
from jax.experimental import pallas as pl
from jax.experimental.pallas import tpu as pltpu
from jax.sharding import PartitionSpec as P


def with_halo(cells, sides, width):
    for axis, dim in sides:
        count = lax.axis_size(axis)
        head = lax.slice_in_dim(cells, 0, width, axis=dim)
        tail = lax.slice_in_dim(cells, cells.shape[dim] - width, cells.shape[dim], axis=dim)
        cells = jnp.concatenate(
            [
                lax.ppermute(tail, axis, [(i, (i + 1) % count) for i in range(count)]),
                cells,
                lax.ppermute(head, axis, [((i + 1) % count, i) for i in range(count)]),
            ],
            axis=dim,
        )
    return cells


def from_behind(array, axis, by):
    count = lax.axis_size(axis)
    pairs = [(i, i + by) for i in range(count) if 0 <= i + by < count]
    return lax.ppermute(array, axis, pairs)


def rounded(field_in):
    return lax.optimization_barrier(field_in.astype(jnp.bfloat16)).astype(jnp.float32)


def band_matrix(taps_re, taps_im, row_count, col_count, half_width, transposed):
    row_index = lax.broadcasted_iota(jnp.int32, (row_count, col_count), 0)
    col_index = lax.broadcasted_iota(jnp.int32, (row_count, col_count), 1)
    offset = row_index - col_index if transposed else col_index - row_index
    chooser = (offset[:, :, None] == jnp.arange(2 * half_width + 1, dtype=jnp.int32)).astype(
        jnp.float32
    )
    real_part = jnp.sum(chooser * taps_re, axis=2).astype(jnp.bfloat16)
    imag_part = jnp.sum(chooser * taps_im, axis=2).astype(jnp.bfloat16)
    return (real_part, imag_part)


def along_rows(field_in, real_mat, imag_mat):
    direct = jnp.einsum("rq,xpqc->xprc", real_mat, field_in, preferred_element_type=jnp.float32)
    crossed = jnp.einsum("rq,xpqc->xprc", imag_mat, field_in, preferred_element_type=jnp.float32)
    return jnp.stack([direct[0] - crossed[1], crossed[0] + direct[1]])


def along_cols(field_in, real_slab, imag_slab, half_width):
    columns = field_in.shape[-1]
    blocks = columns // 128
    padded = jnp.pad(field_in, ((0, 0), (0, 0), (0, 0), (half_width, 128 - half_width)))
    main_part = padded[..., :columns].reshape(field_in.shape[:-1] + (blocks, 128))
    extra_part = padded[..., 128 : columns + 128].reshape(field_in.shape[:-1] + (blocks, 128))[
        ..., : 2 * half_width
    ]
    slab_rows = jnp.concatenate([main_part, extra_part], axis=-1)
    direct = jnp.einsum("xprbq,qo->xprbo", slab_rows, real_slab, preferred_element_type=jnp.float32)
    crossed = jnp.einsum(
        "xprbq,qo->xprbo", slab_rows, imag_slab, preferred_element_type=jnp.float32
    )
    joined = jnp.stack([direct[0] - crossed[1], crossed[0] + direct[1]])
    return joined.reshape(field_in.shape)


def local(potential, incident, measured, offsets, kernel):
    lat_count = lax.axis_size("lat")
    depth_count = lax.axis_size("depth")
    lat_index = lax.axis_index("lat")
    depth_index = lax.axis_index("depth")
    band_rows = potential.shape[3]
    window = incident.shape[3]
    probe_count = incident.shape[1]
    half_width = (kernel.shape[1] - 1) // 2
    taps_re = kernel[0].astype(jnp.float32)
    taps_im = kernel[1].astype(jnp.float32)
    back_re = taps_re[::-1]
    back_im = -taps_im[::-1]
    row_pixel = offsets[:, 0]
    col_pixel = offsets[:, 1]
    first_band = row_pixel // band_rows
    place_band = (lat_index - first_band) % lat_count
    layer_pot = potential[:, 0]
    reach_steps = 2
    margin = reach_steps * half_width
    full_rows = band_rows + 2 * margin
    most_out = full_rows - 2 * half_width
    row_forward = band_matrix(taps_re, taps_im, most_out, full_rows, half_width, False)
    row_adjoint = band_matrix(back_re, back_im, most_out, full_rows, half_width, False)
    column_forward = band_matrix(taps_re, taps_im, 128 + 2 * half_width, 128, half_width, True)
    column_adjoint = band_matrix(back_re, back_im, 128 + 2 * half_width, 128, half_width, True)
    local_rows = jnp.arange(full_rows, dtype=jnp.int32) - margin
    window_row = place_band[:, None] * band_rows + local_rows[None, :]
    valid_rows = (window_row >= 0) & (window_row < window)
    keep_mask = valid_rows[None, :, :, None]
    padded_pot = with_halo(layer_pot, (("lat", 2),), margin)
    local_rows = jnp.arange(band_rows + 2 * margin, dtype=jnp.int32) - margin
    side_rows = (local_rows >= band_rows).astype(jnp.int32) - (local_rows < 0).astype(jnp.int32)
    halves = jnp.clip(
        (first_band[:, None] + place_band[:, None] + side_rows[None, :]) // lat_count, 0, 1
    )

    def cut_window(col_start):
        return lax.dynamic_slice_in_dim(padded_pot, col_start, window, 3)

    windows = jax.vmap(cut_window)(col_pixel)
    chosen = jnp.where((halves == 0)[:, None, :, None], windows[:, :, 0], windows[:, :, 1])
    damping = jnp.exp(-chosen[:, 1])
    phase_part = chosen[:, 0]
    transmit = jnp.stack([damping * jnp.cos(phase_part), damping * jnp.sin(phase_part)])

    def forward_segment(wave_ext, extent):
        low_row = margin - extent
        rows_in = band_rows + 2 * extent
        rows_out = rows_in - 2 * half_width
        factor = transmit[:, :, low_row : low_row + rows_in]
        inside = keep_mask[:, :, low_row : low_row + rows_in]
        values = wave_ext.astype(jnp.float32)
        product = jnp.stack(
            [
                factor[0] * values[0] - factor[1] * values[1],
                factor[0] * values[1] + factor[1] * values[0],
            ]
        )
        product = jnp.where(inside, product, 0.0).astype(jnp.bfloat16)
        spread = along_rows(
            product, row_forward[0][:rows_out, :rows_in], row_forward[1][:rows_out, :rows_in]
        ).astype(jnp.bfloat16)
        return along_cols(spread, column_forward[0], column_forward[1], half_width).astype(
            jnp.bfloat16
        )

    def backward_segment(adjoint, extent, entry):
        low_row = margin - extent
        rows_in = band_rows + 2 * extent
        rows_out = rows_in - 2 * half_width
        inside = keep_mask[:, :, low_row : low_row + rows_in]
        masked = jnp.where(inside, adjoint, jnp.zeros_like(adjoint))
        spread = along_cols(masked, column_adjoint[0], column_adjoint[1], half_width).astype(
            jnp.bfloat16
        )
        local_grad = rounded(
            along_rows(
                spread, row_adjoint[0][:rows_out, :rows_in], row_adjoint[1][:rows_out, :rows_in]
            )
        )
        factor = transmit[:, :, low_row + half_width : low_row + half_width + rows_out]
        earlier = jnp.stack(
            [
                factor[0] * local_grad[0] + factor[1] * local_grad[1],
                factor[0] * local_grad[1] - factor[1] * local_grad[0],
            ]
        ).astype(jnp.bfloat16)
        centre = extent - half_width
        own_rows = local_grad[:, :, centre : centre + band_rows]
        own_factor = factor[:, :, centre : centre + band_rows]
        entry_wave = entry.astype(jnp.float32)
        cross_re = entry_wave[0] * own_rows[0] + entry_wave[1] * own_rows[1]
        cross_im = entry_wave[0] * own_rows[1] - entry_wave[1] * own_rows[0]
        turned_re = own_factor[0] * cross_re + own_factor[1] * cross_im
        turned_im = own_factor[0] * cross_im - own_factor[1] * cross_re
        return (earlier, jnp.stack([turned_im, -turned_re]))

    start_wave = incident.astype(jnp.bfloat16)
    zeros_wave = jnp.zeros_like(start_wave)
    blocks = depth_count // reach_steps

    def forward_block(block_index, carry):
        moving, stored, leaving = carry
        entering = jnp.where(depth_index == 0, start_wave, moving)
        wave_ext = with_halo(entering, (("lat", 2),), margin)
        for sub_step in range(reach_steps):
            extent = margin - sub_step * half_width
            result = forward_segment(wave_ext, extent)
            active = depth_index == block_index * reach_steps + sub_step
            stored = jnp.where(active, wave_ext[:, :, extent : extent + band_rows], stored)
            if sub_step == reach_steps - 1:
                leaving = jnp.where(active, result, leaving)
            wave_ext = from_behind(result, "depth", 1)
        return (wave_ext, stored, leaving)

    moving, stored, leaving = lax.fori_loop(
        0, blocks, forward_block, (zeros_wave, zeros_wave, zeros_wave)
    )
    exit_vals = leaving.astype(jnp.float32)
    residual = exit_vals[0] * exit_vals[0] + exit_vals[1] * exit_vals[1] - measured
    seed_wave = (2.0 * residual[None] * exit_vals).astype(jnp.bfloat16)
    zeros_term = jnp.zeros(start_wave.shape, jnp.float32)

    def backward_block(block_index, carry):
        moving_back, collected = carry
        entering = jnp.where(depth_index == depth_count - 1, seed_wave, moving_back)
        adjoint = with_halo(entering, (("lat", 2),), margin)
        for sub_step in range(reach_steps):
            extent = margin - sub_step * half_width
            earlier, grad_term = backward_segment(adjoint, extent, stored)
            active = depth_index == depth_count - 1 - (block_index * reach_steps + sub_step)
            collected = jnp.where(active, grad_term, collected)
            adjoint = from_behind(earlier, "depth", -1)
        return (adjoint, collected)

    moving_back, gathered = lax.fori_loop(0, blocks, backward_block, (zeros_wave, zeros_term))
    own_half = (first_band + place_band) // lat_count
    gradient = jnp.zeros_like(layer_pot)

    def accumulate(probe_index, running):
        portion = lax.dynamic_index_in_dim(gathered, probe_index, 1, keepdims=False)
        zero_index = jnp.zeros((), jnp.int32)
        corner = (zero_index, own_half[probe_index], zero_index, col_pixel[probe_index])
        current = lax.dynamic_slice(running, corner, (2, 1, band_rows, window))
        return lax.dynamic_update_slice(running, current + portion[:, None], corner)

    gradient = lax.fori_loop(0, probe_count, accumulate, gradient)
    return gradient[:, None]


ROW_BLOCK = 32


def fits(mesh, potential_shape, incident_shape, kernel_shape):
    depth_count, lat_count = mesh.shape["depth"], mesh.shape["lat"]
    slices, window, columns = potential_shape[1], incident_shape[3], potential_shape[4]
    half_width = (kernel_shape[1] - 1) // 2
    if incident_shape[1] != 2 or depth_count != 4 or slices != 4:
        return False
    half_band = potential_shape[3] // lat_count // 2
    reach = slices * half_width
    return (
        half_width <= 8
        and 2 * reach <= half_band
        and reach % 16 == 0
        and half_band % ROW_BLOCK == 0
        and window % 256 == 0
        and 8 * half_width <= 128
        and columns == 2 * window
    )


def series(square, divisors):
    total = 1.0 / divisors[-1]
    for divisor in divisors[-2::-1]:
        total = total * square + 1.0 / divisor
    return total


def probe_place(offsets, probe, lat, lat_count, band_rows):
    first_band = offsets[probe, 0] // band_rows
    place_band = lax.rem(lat - first_band + lat_count, lat_count)
    return place_band, (first_band + place_band) // lat_count, offsets[probe, 1]


def transmission(phase, absorb):
    damping = jnp.exp(-absorb)
    turn = 0.5 * phase
    square = turn * turn
    sine = turn * series(square, (1, -6, 120, -5040, 362880, -39916800, 6227020800))
    cosine = series(square, (1, -2, 24, -720, 40320, -3628800, 479001600))
    bent = 2.0 * damping * sine
    return damping - bent * sine, bent * cosine


def write_window(pot, block, lane, dst, convert):
    window = dst.shape[2]
    last = pot.shape[2] // 128 - 1
    turn_by = lax.rem(128 - lane, 128)
    here = lax.broadcasted_iota(jnp.int32, (ROW_BLOCK, 128), 1) < 128 - lane

    def turned(b):
        at = pl.multiple_of(128 * jnp.minimum(block + b, last), 128)
        return [pltpu.roll(pot[k, :, pl.ds(at, 128)], turn_by, 1) for k in range(2)]

    blocks = [turned(b) for b in range(window // 128 + 1)]
    for b in range(0, window // 128, 2):
        phase, absorb = [
            jnp.concatenate(
                [jnp.where(here, blocks[i][k], blocks[i + 1][k]) for i in (b, b + 1)], axis=1
            )
            for k in range(2)
        ]
        values = transmission(phase, absorb) if convert else (phase, absorb)
        for k in range(2):
            dst[k, :, pl.ds(128 * b, 256)] = values[k].astype(dst.dtype)


def transmission_kernel(offsets, pot_hbm, own_hbm, far_hbm, pot, own, far, in_sem, out_sem):
    depth, lat = lax.axis_index("depth"), lax.axis_index("lat")
    chunks = pot.shape[1]
    band_rows = ROW_BLOCK * chunks
    columns, fetched = pot_hbm.shape[4], pot.shape[4]
    places = []
    for q in range(2):
        place = lax.rem(depth // 2 + q, 2)
        _, layer, col = probe_place(offsets, place, lat, lax.axis_size("lat"), band_rows)
        places.append((layer, jnp.minimum(col // 128, (columns - fetched) // 128), col))

    def copy_in(q, r):
        layer, begin, _ = places[q]
        cols = pl.ds(pl.multiple_of(128 * begin, 128), fetched)
        src = pot_hbm.at[:, 0, layer, pl.ds(ROW_BLOCK * r, ROW_BLOCK), cols]
        return pltpu.make_async_copy(src, pot.at[q, r], in_sem.at[q, r])

    def copy_out(q, r):
        src, dst = ((own, own_hbm), (far, far_hbm))[q]
        dst = dst.at[:, pl.ds(ROW_BLOCK * r, ROW_BLOCK)]
        return pltpu.make_async_copy(src.at[r], dst, out_sem.at[q, r])

    order = [(q, r) for q in range(2) for r in range(chunks)]
    for q, r in order:
        copy_in(q, r).start()
    for q, r in order:
        _, begin, col = places[q]
        copy_in(q, r).wait()
        dst = (own, far)[q].at[r]
        write_window(pot.at[q, r], col // 128 - begin, lax.rem(col, 128), dst, q == 1)
        copy_out(q, r).start()
    for q, r in order:
        copy_out(q, r).wait()


def transmissions(offsets, potential, window):
    band_rows = potential.shape[3]
    chunks = band_rows // ROW_BLOCK
    return pl.pallas_call(
        transmission_kernel,
        out_shape=[
            jax.ShapeDtypeStruct((2, band_rows, window), jnp.float32),
            jax.ShapeDtypeStruct((2, band_rows, window), jnp.bfloat16),
        ],
        in_specs=[
            pl.BlockSpec(memory_space=pltpu.SMEM),
            pl.BlockSpec(memory_space=pl.ANY),
        ],
        out_specs=[pl.BlockSpec(memory_space=pl.ANY)] * 2,
        scratch_shapes=[
            pltpu.VMEM((2, chunks, 2, ROW_BLOCK, window + 128), jnp.float32),
            pltpu.VMEM((chunks, 2, ROW_BLOCK, window), jnp.float32),
            pltpu.VMEM((chunks, 2, ROW_BLOCK, window), jnp.bfloat16),
            pltpu.SemaphoreType.DMA((2, chunks)),
            pltpu.SemaphoreType.DMA((2, chunks)),
        ],
        compiler_params=pltpu.CompilerParams(vmem_limit_bytes=60 * 1024 * 1024),
    )(offsets, potential)


def band(taps, rows, cols, start, half_width):
    offset = (
        lax.broadcasted_iota(jnp.int32, (rows, cols), 0)
        - lax.broadcasted_iota(jnp.int32, (rows, cols), 1)
        - start
        + half_width
    )
    total = jnp.zeros((rows, cols), jnp.float32)
    for tap_index, tap in enumerate(taps):
        total = jnp.where(offset == tap_index, tap, total)
    return total


def main_kernel(
    offsets, taps_ref, own_hbm, far_hbm, incident_hbm, measured_hbm, out_ref,
    incident, measured, own_raw, far_t, t_all, start, waves, adj, terms, row_mat, col_mat,
    send_sem, load_sem, far_sem, beside_sem, edge_sem, start_sem, adj_sem, term_sem,
):
    slices, _, rows, width = waves.shape
    window = incident.shape[2]
    share = window // 2
    tap_count = taps_ref.shape[1]
    half_width = (tap_count - 1) // 2
    band_rows = far_t.shape[1]
    half_band = band_rows // 2
    reach = (rows - half_band) // 2
    blocks = width // 128
    depth, lat = lax.axis_index("depth"), lax.axis_index("lat")
    lat_count = lax.axis_size("lat")
    probe, half = depth // 2, lax.rem(depth, 2)
    other_half = 1 - half
    beside = 2 * probe + other_half
    across = 2 * (1 - probe) + half
    before, after = lax.rem(lat + lat_count - 1, lat_count), lax.rem(lat + 1, lat_count)
    near = lax.rem(lat + 2 * half + lat_count - 1, lat_count)

    def remote(src, dst, send, recv, to):
        return pltpu.make_async_remote_copy(
            src_ref=src,
            dst_ref=dst,
            send_sem=send_sem.at[send],
            recv_sem=recv,
            device_id=to,
            device_id_type=pl.DeviceIdType.MESH,
        )

    own_rows = pl.ds(pl.multiple_of(half_band * half, 16), half_band)
    loads = [
        pltpu.make_async_copy(src, dst, load_sem.at[i])
        for i, (src, dst) in enumerate(
            [
                (far_hbm, far_t),
                (own_hbm, own_raw),
                (incident_hbm.at[:, probe], incident),
                (measured_hbm.at[probe, own_rows], measured),
            ]
        )
    ]
    for load in loads:
        load.start()

    barrier = pltpu.get_barrier_semaphore()
    senders = [
        (beside, lat),
        (across, lat),
        (2 * (1 - probe) + other_half, lat),
        (2 * probe, near),
        (2 * probe + 1, near),
    ]
    for to in senders:
        pl.semaphore_signal(
            barrier, inc=1, device_id=to, device_id_type=pl.DeviceIdType.MESH
        )
    pl.semaphore_wait(barrier, len(senders))

    inner = pl.ds(reach, band_rows)
    place_row = band_rows * lat
    at_row = offsets[probe, 0]
    at_top = (at_row == place_row) | (at_row == place_row + window)
    at_bottom = (at_row == place_row + band_rows) | (at_row == place_row + band_rows - window)
    top_ok = jnp.logical_not(at_top) | (half == 1)
    bottom_ok = jnp.logical_not(at_bottom) | (half == 0)

    fresh = [pl.ds(0, width), pl.ds(width, window - width)]
    first = [0, window - width]
    far = [
        remote(
            far_t.at[:, :, cols], t_all.at[0, 1, :, inner, cols],
            13 + n, far_sem.at[n], (across, lat),
        )
        for n, cols in enumerate(fresh)
    ]
    loads[0].wait()
    far[0].start()
    far[1].start()
    loads[2].wait()
    start[:, inner] = incident[...].astype(jnp.bfloat16)
    loads[1].wait()

    @pl.loop(0, band_rows // 16)
    def _(r):
        rows_in = pl.ds(pl.multiple_of(16 * r, 16), 16)
        rows_out = pl.ds(pl.multiple_of(reach + 16 * r, 16), 16)
        for b in range(0, window, 256):
            at = pl.ds(b, 256)
            values = transmission(own_raw[0, rows_in, at], own_raw[1, rows_in, at])
            t_all[0, 0, 0, rows_out, at] = values[0].astype(jnp.bfloat16)
            t_all[0, 0, 1, rows_out, at] = values[1].astype(jnp.bfloat16)

    shared = pl.ds(pl.multiple_of(reach + (half_band - reach) * other_half, 16), half_band + reach)
    edge_rows = pl.ds(pl.multiple_of((band_rows + reach) * half, 16), reach)
    tail, head = pl.ds(band_rows, reach), pl.ds(reach, reach)
    low, high = pl.ds(0, reach), pl.ds(band_rows + reach, reach)

    groups = [(0, pl.ds(0, window)), (1, fresh[0]), (1, fresh[1])]

    def slot_copies(group):
        side, cols = groups[group]
        return [
            remote(
                t_all.at[0, side, :, shared, cols], t_all.at[1, side, :, shared, cols],
                3 * group, beside_sem.at[group], (beside, lat),
            ),
            remote(
                t_all.at[0, side, :, tail, cols], t_all.at[half, side, :, low, cols],
                3 * group + 1, edge_sem.at[half, group], (2 * probe, after),
            ),
            remote(
                t_all.at[0, side, :, head, cols], t_all.at[other_half, side, :, high, cols],
                3 * group + 2, edge_sem.at[other_half, group], (2 * probe + 1, before),
            ),
        ]

    def finish_slot(group):
        side, cols = groups[group]
        slot_copies(group)[0].wait_recv()
        for core in range(2):
            remote(
                t_all.at[0, side, :, tail, cols], t_all.at[core, side, :, edge_rows, cols],
                3 * group + 1, edge_sem.at[core, group], (beside, lat),
            ).wait_recv()
            edge = t_all[core, side, :, edge_rows, cols]
            t_all[core, side, :, edge_rows, cols] = jnp.where(
                top_ok & bottom_ok, edge, jnp.zeros_like(edge)
            )

    start_rows = pl.ds(pl.multiple_of(reach + (band_rows - reach) * other_half, 16), reach)
    toward = lax.rem(lat + 1 - 2 * half + lat_count, lat_count)
    start_copy = remote(
        start.at[:, start_rows], start.at[:, edge_rows], 9, start_sem.at[0], (depth, toward)
    )
    near_copies = slot_copies(0)
    for copy in [start_copy] + near_copies:
        copy.start()

    taps = taps_ref[...].astype(jnp.float32)
    re = [taps[0:1, i : i + 1] for i in range(tap_count)]
    im = [taps[1:2, i : i + 1] for i in range(tap_count)]
    ways = ((re, im), (re[::-1], [-tap for tap in im[::-1]]))
    for way, (tap_re, tap_im) in enumerate(ways):
        real = band(tap_re[::-1], rows, rows, 0, half_width)
        imag = band(tap_im[::-1], rows, rows, 0, half_width)
        row_mat[way] = jnp.concatenate(
            [
                jnp.concatenate([real, -imag], axis=1),
                jnp.concatenate([imag, real], axis=1),
            ],
            axis=0,
        ).astype(jnp.bfloat16)
        real = band(tap_re, 384, 128, 128, half_width)
        imag = band(tap_im, 384, 128, 128, half_width)
        col_mat[way, :384, :128] = real.astype(jnp.bfloat16)
        col_mat[way, :384, 128:] = imag.astype(jnp.bfloat16)
        col_mat[way, 384:, :128] = (-imag).astype(jnp.bfloat16)
        col_mat[way, 384:, 128:] = real.astype(jnp.bfloat16)

    def rows_conv(field, way):
        return jnp.dot(row_mat[way], field, preferred_element_type=jnp.float32).astype(
            jnp.bfloat16
        )

    def cols_conv(field, way):
        edge = jnp.zeros((rows, 128), jnp.bfloat16)
        padded = [
            jnp.concatenate([edge, field[k * rows : (k + 1) * rows], edge], axis=1)
            for k in range(2)
        ]
        slabs = jnp.concatenate(
            [
                jnp.concatenate([part[:, 128 * b : 128 * b + 384] for part in padded], axis=1)
                for b in range(blocks)
            ],
            axis=0,
        )
        out = jnp.dot(slabs, col_mat[way], preferred_element_type=jnp.float32)
        out = out.astype(jnp.bfloat16)
        return [
            jnp.concatenate(
                [out[b * rows : (b + 1) * rows, 128 * k : 128 * k + 128] for b in range(blocks)],
                axis=1,
            )
            for k in range(2)
        ]

    extent = pl.ds(pl.multiple_of(half_band * half, 16), rows)

    def place_of(s):
        return lax.rem(s % 2 + half, 2), lax.rem(s // 2 + probe, 2)

    def factor(s, cols):
        core, side = place_of(s)
        both = t_all[core, side, :, extent, cols].astype(jnp.float32)
        return both[0], both[1]

    def term_copy(n, s):
        core, side = place_of(s)
        at = 2 * side + core
        cols = pl.ds(share * n, share)
        return remote(
            terms.at[s, :, :, cols], out_ref.at[side, core, :, :, cols],
            15 + 4 * n + at, term_sem.at[n, at], (s, lat),
        )

    def adjoint_copies(n):
        return [
            remote(
                adj.at[n, :, pl.ds(reach, reach)], adj.at[n, :, pl.ds(rows - reach, reach)],
                23 + n, adj_sem.at[n, 1], (beside, up_lat),
            ),
            remote(
                adj.at[n, :, pl.ds(rows - 2 * reach, reach)], adj.at[n, :, pl.ds(0, reach)],
                25 + n, adj_sem.at[n, 0], (beside, down_lat),
            ),
        ]

    up_lat = lax.rem(lat + half + lat_count - 1, lat_count)
    down_lat = lax.rem(lat + half, lat_count)
    own = slice(reach, rows - reach)
    far[0].wait_recv()
    for copy in slot_copies(1):
        copy.start()
    start_copy.wait_recv()
    finish_slot(0)

    for n in range(2):
        cols = pl.ds(first[n], width)
        if n == 0:
            pl.when(probe == 1)(lambda: finish_slot(1))
        else:
            finish_slot(2)
        waves[0] = start[:, extent, cols]
        wave = None
        for s in range(slices):
            if s == slices // 2 and n == 0:
                pl.when(probe == 0)(lambda: finish_slot(1))
            t_re, t_im = factor(s, cols)
            w_re, w_im = waves[s, 0].astype(jnp.float32), waves[s, 1].astype(jnp.float32)
            product = jnp.concatenate(
                [t_re * w_re - t_im * w_im, t_re * w_im + t_im * w_re], axis=0
            )
            wave = cols_conv(rows_conv(product.astype(jnp.bfloat16), 0), 0)
            if s + 1 < slices:
                waves[s + 1, 0], waves[s + 1, 1] = wave

        w_re, w_im = [part[own].astype(jnp.float32) for part in wave]
        if n == 0:
            loads[3].wait()
        residual = 2.0 * (w_re * w_re + w_im * w_im - measured[:, cols])
        adj[n, 0, own] = (residual * w_re).astype(jnp.bfloat16)
        adj[n, 1, own] = (residual * w_im).astype(jnp.bfloat16)
        for copy in adjoint_copies(n):
            copy.start()
        if n == 0:
            far[1].wait_recv()
            for copy in slot_copies(2):
                copy.start()
        for copy in adjoint_copies(n):
            copy.wait_recv()
        adjoint = []
        for k in range(2):
            top, bottom = adj[n, k, :reach], adj[n, k, rows - reach :]
            adjoint.append(
                jnp.concatenate(
                    [
                        jnp.where(top_ok, top, jnp.zeros_like(top)),
                        adj[n, k, own],
                        jnp.where(bottom_ok, bottom, jnp.zeros_like(bottom)),
                    ],
                    axis=0,
                )
            )

        mine = slice(share * n - first[n], share * n - first[n] + share)
        kept = slice(share * n, share * n + share)
        for s in reversed(range(slices)):
            spread = cols_conv(jnp.concatenate(adjoint, axis=0), 1)
            grad = rows_conv(jnp.concatenate(spread, axis=0), 1).astype(jnp.float32)
            g_re, g_im = grad[:rows], grad[rows:]
            t_re, t_im = factor(s, cols)
            back_re = t_re * g_re + t_im * g_im
            back_im = t_re * g_im - t_im * g_re
            b_re, b_im = back_re[own, mine], back_im[own, mine]
            e_re = waves[s, 0, own, mine].astype(jnp.float32)
            e_im = waves[s, 1, own, mine].astype(jnp.float32)
            terms[s, 0, :, kept] = (e_re * b_im - e_im * b_re).astype(jnp.bfloat16)
            terms[s, 1, :, kept] = (-e_re * b_re - e_im * b_im).astype(jnp.bfloat16)
            pl.when(depth != s)(lambda: term_copy(n, s).start())

            @pl.when(depth == s)
            def _():
                out_ref[0, 0, :, :, kept] = terms[s, :, :, kept]

            adjoint = [back_re.astype(jnp.bfloat16), back_im.astype(jnp.bfloat16)]

    for copy in far + [start_copy] + near_copies + slot_copies(1) + slot_copies(2):
        copy.wait_send()
    for n in range(2):
        for copy in adjoint_copies(n):
            copy.wait_send()
        for s in range(slices):
            pl.when(depth != s)(lambda: term_copy(n, s).wait_send())
        cols = pl.ds(share * n, share)
        for at in range(1, 4):
            remote(
                terms.at[0, :, :, cols], out_ref.at[at // 2, at % 2, :, :, cols],
                15 + 4 * n + at, term_sem.at[n, at], (beside, lat),
            ).wait_recv()


def section_terms(offsets, taps, own, far, incident, measured, reach):
    slices, band_rows, window = 4, far.shape[1], far.shape[2]
    half_band = band_rows // 2
    rows = half_band + 2 * reach
    width = window // 2 + 128
    smem = pl.BlockSpec(memory_space=pltpu.SMEM)
    vmem = pl.BlockSpec(memory_space=pltpu.VMEM)
    hbm = pl.BlockSpec(memory_space=pl.ANY)
    return pl.pallas_call(
        main_kernel,
        out_shape=jax.ShapeDtypeStruct((2, 2, 2, half_band, window), jnp.bfloat16),
        in_specs=[smem, vmem, hbm, hbm, hbm, hbm],
        out_specs=vmem,
        scratch_shapes=[
            pltpu.VMEM((2, band_rows, window), jnp.float32),
            pltpu.VMEM((half_band, window), jnp.float32),
            pltpu.VMEM((2, band_rows, window), jnp.float32),
            pltpu.VMEM((2, band_rows, window), jnp.bfloat16),
            pltpu.VMEM((2, 2, 2, band_rows + 2 * reach, window), jnp.bfloat16),
            pltpu.VMEM((2, band_rows + 2 * reach, window), jnp.bfloat16),
            pltpu.VMEM((slices, 2, rows, width), jnp.bfloat16),
            pltpu.VMEM((2, 2, rows, width), jnp.bfloat16),
            pltpu.VMEM((slices, 2, half_band, window), jnp.bfloat16),
            pltpu.VMEM((2, 2 * rows, 2 * rows), jnp.bfloat16),
            pltpu.VMEM((2, 768, 256), jnp.bfloat16),
            pltpu.SemaphoreType.DMA((27,)),
            pltpu.SemaphoreType.DMA((4,)),
            pltpu.SemaphoreType.DMA((2,)),
            pltpu.SemaphoreType.DMA((3,)),
            pltpu.SemaphoreType.DMA((2, 3)),
            pltpu.SemaphoreType.DMA((1,)),
            pltpu.SemaphoreType.DMA((2, 2)),
            pltpu.SemaphoreType.DMA((2, 4)),
        ],
        compiler_params=pltpu.CompilerParams(
            vmem_limit_bytes=60 * 1024 * 1024, collective_id=0, has_side_effects=True
        ),
    )(offsets, taps, own, far, incident, measured)


def place_rows(offsets, probe, lat, half_band, core_terms, out_ref):
    columns, window = out_ref.shape[3], core_terms[0].shape[2]
    out_ref[...] = jnp.zeros_like(out_ref)
    last = columns // 128 - 1
    lanes = lax.broadcasted_iota(jnp.int32, (ROW_BLOCK, 128), 1)
    for q in range(2):
        place = lax.rem(probe + q, 2)
        _, layer, col = probe_place(offsets, place, lat, lax.axis_size("lat"), 2 * half_band)
        block, lane = col // 128, lax.rem(col, 128)
        for part in range(2):
            turned = [jnp.zeros((ROW_BLOCK, 128), jnp.float32)]
            for b in range(window // 128):
                values = core_terms[q][part, :, pl.ds(128 * b, 128)]
                turned.append(pltpu.roll(values.astype(jnp.float32), lane, 1))
            pieces = [jnp.where(lanes < lane, low, high) for low, high in zip(turned, turned[1:])]
            wide = jnp.concatenate(pieces, axis=1)
            past = jnp.where(lanes < lane, turned[-1], 0.0)
            at = pl.ds(pl.multiple_of(128 * block, 128), window)
            end = pl.multiple_of(128 * jnp.minimum(block + window // 128, last), 128)
            if q == 1:
                wide = wide + out_ref[part, layer, :, at]
            out_ref[part, layer, :, at] = wide
            out_ref[part, layer, :, pl.ds(end, 128)] += past


def place_kernel(offsets, terms_hbm, out_hbm, terms, out, in_sem, out_sem):
    depth, lat = lax.axis_index("depth"), lax.axis_index("lat")
    probe, half = depth // 2, lax.rem(depth, 2)
    chunks, half_band = out.shape[0], terms_hbm.shape[3]
    per_half = chunks // 2

    def copy_in(q, r):
        core = lax.rem(r // per_half + half, 2)
        rows = pl.ds(ROW_BLOCK * (r % per_half), ROW_BLOCK)
        src = terms_hbm.at[q, core, :, rows]
        return pltpu.make_async_copy(src, terms.at[q, r], in_sem.at[q, r])

    def copies_out(r):
        rows = pl.ds(ROW_BLOCK * r, ROW_BLOCK)
        return [
            pltpu.make_async_copy(
                out.at[r, part, layer],
                out_hbm.at[part, 0, layer, rows],
                out_sem.at[r, part, layer],
            )
            for part in range(2)
            for layer in range(2)
        ]

    for r in range(chunks):
        for q in range(2):
            copy_in(q, r).start()
    for r in range(chunks):
        for q in range(2):
            copy_in(q, r).wait()
        place_rows(offsets, probe, lat, half_band, [terms.at[0, r], terms.at[1, r]], out.at[r])
        for copy in copies_out(r):
            copy.start()
    for r in range(chunks):
        for copy in copies_out(r):
            copy.wait()


def placed(offsets, terms, columns):
    half_band, window = terms.shape[3:]
    chunks = 2 * half_band // ROW_BLOCK
    return pl.pallas_call(
        place_kernel,
        out_shape=jax.ShapeDtypeStruct((2, 1, 2, 2 * half_band, columns), jnp.float32),
        in_specs=[
            pl.BlockSpec(memory_space=pltpu.SMEM),
            pl.BlockSpec(memory_space=pl.ANY),
        ],
        out_specs=pl.BlockSpec(memory_space=pl.ANY),
        scratch_shapes=[
            pltpu.VMEM((2, chunks, 2, ROW_BLOCK, window), jnp.bfloat16),
            pltpu.VMEM((chunks, 2, 2, ROW_BLOCK, columns), jnp.float32),
            pltpu.SemaphoreType.DMA((2, chunks)),
            pltpu.SemaphoreType.DMA((chunks, 2, 2)),
        ],
        compiler_params=pltpu.CompilerParams(vmem_limit_bytes=60 * 1024 * 1024),
    )(offsets, terms)


def local_fast(potential, incident, measured, offsets, kernel):
    reach = 4 * ((kernel.shape[1] - 1) // 2)
    own, far = transmissions(offsets, potential, incident.shape[3])
    terms = section_terms(offsets, kernel, own, far, incident, measured, reach)
    return placed(offsets, terms, potential.shape[4])


def solution(mesh):
    def run(*args):
        potential, incident, _, _, kernel = args
        body = local_fast if fits(mesh, potential.shape, incident.shape, kernel.shape) else local
        in_specs = (
            P(None, "depth", None, "lat", None),
            P(None, None, "lat", None),
            P(None, "lat", None),
            P(),
            P(),
        )
        out_specs = P(None, "depth", None, "lat", None)
        return jax.shard_map(
            body, mesh=mesh, in_specs=in_specs, out_specs=out_specs, check_vma=False
        )(*args)

    return run
```
